32 devices in a mesh: dp: 8 (over z, x), mp: 4 (over y, core).
Axes of the slice: x: 2, y: 2, z: 4, core: 2. Of those that a mesh axis runs over, the one named last changes fastest.
Arguments:
- tokens: bfloat16 [16384, 768], P('dp'), may hold values from -6 to 6
- segment_ids: int32 [16384], P('dp'), may hold values from 0 to 1, as said below
- slot_valid: int32 [2048], P(('dp', 'mp')), may hold values from 0 to 1
- ln1_gain: bfloat16 [768], P('dp'), may hold values from 0.5 to 1.5
- ln1_bias: bfloat16 [768], P('dp'), may hold values from -1 to 1
- w_qkv: bfloat16 [3, 768, 768], P(None, 'dp', 'mp'), may hold values from -0.21875 to 0.21875
- w_out: bfloat16 [768, 768], P('mp', 'dp'), may hold values from -0.375 to 0.375
- ln2_gain: bfloat16 [768], P('dp'), may hold values from 0.5 to 1.5
- ln2_bias: bfloat16 [768], P('dp'), may hold values from -1 to 1
- w_up: bfloat16 [768, 3072], P('dp', 'mp'), may hold values from -0.21875 to 0.21875
- w_down: bfloat16 [3072, 768], P('mp', 'dp'), may hold values from -0.15625 to 0.15625
- class_tokens: bfloat16 [2048, 768], P(('dp', 'mp')), may hold values from -6 to 6
- image_gain: float32 [768], replicated, may hold values from 0.5 to 1.5
- image_bias: float32 [768], replicated, may hold values from -1.5 to 1.5
- image_proj: bfloat16 [768, 768], replicated, may hold values from -0.21875 to 0.21875
Outputs:
- loss: float32 [], replicated
- block_out: bfloat16 [16384, 768], P('dp')
- token_grad: float32 [16384, 768], P('dp')
- ln1_gain_grad: float32 [768], P('dp')
- ln1_bias_grad: float32 [768], P('dp')
- qkv_grad: float32 [3, 768, 768], P(None, 'dp', 'mp')
- out_grad: float32 [768, 768], P('mp', 'dp')
- ln2_gain_grad: float32 [768], P('dp')
- ln2_bias_grad: float32 [768], P('dp')
- up_grad: float32 [768, 3072], P('dp', 'mp')
- down_grad: float32 [3072, 768], P('mp', 'dp')
The draws below stay inside these ranges and needn't reach their ends.
Inputs may be any that keep to these rules, and one draw needn't show every extreme that they name: `segment_ids`: in each aligned run of 16 positions the ids are 0 and then 1, each present at least once.
All inputs are finite; a program needn't handle non-finite values.
Results may differ from the reference program's by a relative error of at most 0.012.
The reference program's roundings to bfloat16 on the way count: a program that leaves them out, or rounds other values in their place, can miss the bound.
Values may be sent and summed in bfloat16 or wider, within the bound.
A program may use at most 192 MiB of HBM per device.

```python
import jax
import jax.numpy as jnp
from jax import lax

D = 768
HEADS = 12
HEAD_DIM = 64
FF = 3072
VW = 768
SEQ_LEN = 16
TOKENS = 16384
SLOTS = 2048


def draw_segment_ids(key, part):
    count = TOKENS // SEQ_LEN
    splits = jax.random.randint(key, (count, 1), 1, SEQ_LEN, dtype=jnp.int32)
    places = jnp.arange(SEQ_LEN, dtype=jnp.int32)[None, :]
    return (places >= splits).astype(jnp.int32).reshape(TOKENS)


def draw_slot_valid(key, part):
    key = jax.random.fold_in(key, 7)
    places = jnp.arange(SLOTS, dtype=jnp.int32)
    limits = 300 + 700 * places // max(SLOTS - 1, 1)
    picks = jax.random.randint(key, (SLOTS,), 0, 1000, dtype=jnp.int32)
    return (picks < limits).astype(jnp.int32)


def block_levels(own_key, dims, cuts, low, largest):
    level, own = 1.0, jax.random.fold_in(own_key, 6)
    for dim, parts in cuts:
        draws = jnp.exp(jax.random.uniform(jax.random.fold_in(own, dim), (parts,), jnp.float32, low / len(cuts), largest / len(cuts)))
        level = level * jnp.repeat(draws, dims[dim] // parts).reshape([-1 if axis == dim else 1 for axis in range(len(dims))])
    return level


def bell_draw(stream_key, dims, scale, bound, cuts=(), kind=jnp.bfloat16):
    entries = jax.random.normal(stream_key, dims, jnp.float32) * scale
    if len(cuts) > 0:
        entries = block_levels(stream_key, dims, cuts, -0.22, 0.18) * entries
    return jnp.clip(entries, min=-bound, max=bound).astype(kind)


def setup_inputs(seed: int = 0) -> dict:
    arg_keys = jax.random.split(jax.random.key(seed), 16)
    return {
        "tokens": bell_draw(arg_keys[0], (TOKENS, D), 1.0, 6.0, ((0, 8),)),
        "segment_ids": draw_segment_ids(jax.random.fold_in(arg_keys[15], 71), 0),
        "slot_valid": draw_slot_valid(jax.random.fold_in(arg_keys[15], 71), 0),
        "ln1_gain": jnp.clip(1.0 + 0.1 * jax.random.normal(arg_keys[3], (D,), jnp.float32), 0.5, 1.5).astype(jnp.bfloat16),
        "ln1_bias": bell_draw(arg_keys[4], (D,), 0.2, 1.0, ((0, 8),)),
        "w_qkv": bell_draw(arg_keys[5], (3, D, D), D ** -0.5, 0.21875, ((1, 8), (2, 4))),
        "w_out": bell_draw(arg_keys[6], (D, D), (D // 3) ** -0.5, 0.375, ((0, 4), (1, 8))),
        "ln2_gain": jnp.clip(1.0 + 0.1 * jax.random.normal(arg_keys[7], (D,), jnp.float32), 0.5, 1.5).astype(jnp.bfloat16),
        "ln2_bias": bell_draw(arg_keys[8], (D,), 0.2, 1.0, ((0, 8),)),
        "w_up": bell_draw(arg_keys[9], (D, FF), D ** -0.5, 0.21875, ((0, 8), (1, 4))),
        "w_down": bell_draw(arg_keys[10], (FF, D), (FF // 2) ** -0.5, 0.15625, ((0, 4), (1, 8))),
        "class_tokens": bell_draw(arg_keys[11], (SLOTS, VW), 1.0, 6.0, ((0, 32),)),
        "image_gain": jnp.clip(1.0 + 0.1 * jax.random.normal(arg_keys[12], (VW,), jnp.float32), 0.5, 1.5),
        "image_bias": bell_draw(arg_keys[13], (VW,), 0.3, 1.5, (), jnp.float32),
        "image_proj": bell_draw(arg_keys[14], (VW, D), VW ** -0.5, 0.21875),
    }


@jax.custom_vjp
def low(v):
    return lax.optimization_barrier(v.astype(jnp.bfloat16)).astype(jnp.float32)

@jax.custom_vjp
def low_back(v):
    return v

def low_keep(v):
    return (low(v), None)

def low_pass(kept, grad):
    return (grad,)

def back_keep(v):
    return (v, None)

def back_low(kept, grad):
    return (low(grad),)
low.defvjp(low_keep, low_pass)
low_back.defvjp(back_keep, back_low)
highest = lax.Precision.HIGHEST
norm_epsilon = 1e-05
unit_epsilon = 1e-06
logit_scale = 50.0
masked_score = -1e+30

def layer_norm(values, gain_vec, bias_vec):
    centred = values - lax.optimization_barrier(jnp.mean(values, axis=-1, keepdims=True))
    spread = lax.optimization_barrier(jnp.mean(centred * centred, axis=-1, keepdims=True))
    return centred * lax.rsqrt(spread + norm_epsilon) * gain_vec + bias_vec

def unit_rows(values):
    return values * lax.rsqrt(lax.optimization_barrier(jnp.sum(values * values, axis=-1, keepdims=True)) + unit_epsilon)

def exact_gelu(values):
    return jax.nn.gelu(values, approximate=False)

def end_positions(segment_block):
    count = segment_block.shape[0] // SEQ_LEN
    grid_ids = segment_block.reshape(count, SEQ_LEN)
    first_len = lax.optimization_barrier(jnp.sum((grid_ids == 0).astype(jnp.int32), axis=1))
    starts = jnp.arange(count, dtype=jnp.int32) * SEQ_LEN
    return jnp.stack([starts + first_len - 1, starts + SEQ_LEN - 1], axis=1).reshape(2 * count)

def block_forward(params, row_values, segment_block):
    gain_one, bias_one, qkv_mat, out_mat, gain_two, bias_two, up_mat, down_mat = params
    width = row_values.shape[0]
    count = width // SEQ_LEN
    normed = low(layer_norm(row_values, gain_one, bias_one))
    projected = low(low_back(jnp.einsum('rd,cde->cre', normed, qkv_mat, precision=highest)))
    split = projected.reshape(3, count, SEQ_LEN, HEADS, HEAD_DIM)
    scores = jnp.einsum('sqhc,skhc->shqk', split[0], split[1], precision=highest) * HEAD_DIM ** (-0.5)
    scores = low_back(scores)
    grid_ids = segment_block.reshape(count, SEQ_LEN)
    places = jnp.arange(SEQ_LEN)
    allowed = (grid_ids[:, :, None] == grid_ids[:, None, :]) & (places[:, None] >= places[None, :])[None]
    scores = jnp.where(allowed[:, None], scores, masked_score)
    weights = low(jax.nn.softmax(scores, axis=-1))
    mixed = jnp.einsum('shqk,skhc->sqhc', weights, split[2], precision=highest).reshape(width, D)
    mixed = low(low_back(mixed))
    attended = low_back(jnp.dot(mixed, out_mat, precision=highest))
    hidden = row_values + attended
    normed_two = low(layer_norm(hidden, gain_two, bias_two))
    upper = low_back(jnp.dot(normed_two, up_mat, precision=highest))
    active = low(exact_gelu(upper))
    branch = low_back(jnp.dot(active, down_mat, precision=highest))
    output = hidden + branch
    return (output, output[end_positions(segment_block)])

def reference(tokens, segment_ids, slot_valid, ln1_gain, ln1_bias, w_qkv, w_out, ln2_gain, ln2_bias, w_up, w_down, class_tokens, image_gain, image_bias, image_proj):
    class_values = class_tokens.astype(jnp.float32)
    proj_values = image_proj.astype(jnp.float32)
    live = slot_valid > 0
    step = min(TOKENS, 4096)
    count = TOKENS // step
    segment_blocks = segment_ids.reshape(count, step)

    def objective(row_values, params):
        image_normed = low(layer_norm(class_values, image_gain, image_bias))
        image_unit = low(unit_rows(jnp.dot(image_normed, proj_values, precision=highest)))

        def one_block(pair_in):
            return block_forward(params, pair_in[0], pair_in[1])
        outputs, pooled = lax.map(jax.checkpoint(one_block), (row_values.reshape(count, step, D), segment_blocks))
        pooled = pooled.reshape(SLOTS, D)
        text_unit = low(unit_rows(pooled))
        cosine = low_back(jnp.dot(text_unit, image_unit.T, precision=highest))
        logits = logit_scale * cosine
        text_lse = jax.nn.logsumexp(jnp.where(live[None, :], logits, masked_score), axis=1)
        image_lse = jax.nn.logsumexp(jnp.where(live[:, None], logits, masked_score), axis=0)
        matched = jnp.diagonal(logits)
        total = 0.5 * jnp.sum(jnp.where(live, text_lse - matched, 0.0) + jnp.where(live, image_lse - matched, 0.0))
        return (total, outputs.reshape(TOKENS, D))
    params = tuple((weight_arr.astype(jnp.float32) for weight_arr in (ln1_gain, ln1_bias, w_qkv, w_out, ln2_gain, ln2_bias, w_up, w_down)))
    (total, outputs), pullback = jax.vjp(objective, tokens.astype(jnp.float32), params)
    token_grad, param_grads = pullback((jnp.ones_like(total), jnp.zeros_like(outputs)))
    return (total / SLOTS, outputs.astype(jnp.bfloat16), token_grad, param_grads[0], param_grads[1], param_grads[2], param_grads[3], param_grads[4], param_grads[5], param_grads[6], param_grads[7])
```

```python
import jax
import jax.numpy as jnp
from jax import lax
from jax.sharding import PartitionSpec as P

HEAD_DIM = 64
SEQ_LEN = 16
norm_epsilon = 1e-05
unit_epsilon = 1e-06
logit_scale = 50.0
tile_rows = 128
f32, bf16 = jnp.float32, jnp.bfloat16


def standardise(values):
    centred = values - jnp.mean(values, axis=-1, keepdims=True)
    rstd = lax.rsqrt(jnp.mean(centred * centred, axis=-1, keepdims=True) + norm_epsilon)
    return centred * rstd, rstd


def norm_pull(grad, hat, rstd, gain):
    scaled = grad * gain
    first = jnp.mean(scaled, axis=-1, keepdims=True)
    second = jnp.mean(scaled * hat, axis=-1, keepdims=True)
    return rstd * (scaled - first - hat * second)


def inverse_norm(values):
    return lax.rsqrt(jnp.sum(values * values, axis=-1, keepdims=True) + unit_epsilon)


def nn(left, right):
    return lax.dot_general(left, right, (((1,), (0,)), ((), ())), preferred_element_type=f32)


def nt(left, right):
    return lax.dot_general(left, right, (((1,), (1,)), ((), ())), preferred_element_type=f32)


def tn(left, right):
    return lax.dot_general(left, right, (((0,), (0,)), ((), ())), preferred_element_type=f32)


def phi(values):
    return 0.5 * lax.erfc(-values * (0.5**0.5))


def make(dp_size, mp_size):
    def on_device(
        tokens,
        segment_ids,
        slot_valid,
        ln1_gain,
        ln1_bias,
        w_qkv,
        w_out,
        ln2_gain,
        ln2_bias,
        w_up,
        w_down,
        class_tokens,
        image_gain,
        image_bias,
        image_proj,
    ):
        both = ("dp", "mp")
        dp_rank, mp_rank = lax.axis_index("dp"), lax.axis_index("mp")
        depth = w_up.shape[0]
        width = depth * dp_size
        head_cols = w_out.shape[0]
        heads = head_cols // HEAD_DIM
        rows = tokens.shape[0] // mp_size
        seqs = rows // SEQ_LEN
        slots = slot_valid.shape[0]
        slot_total = slots * dp_size * mp_size

        packed = jnp.stack(
            [jnp.concatenate([w_qkv[0], w_qkv[1], w_qkv[2], w_out.T], axis=1), w_up, w_down.T]
        )
        norms = jnp.stack([ln1_gain, ln1_bias, ln2_gain, ln2_bias])
        image_hat, _ = standardise(class_tokens.astype(f32))
        image_normed = (image_hat * image_gain + image_bias).astype(bf16)
        image_raw = nn(image_normed, image_proj)
        image_unit = (image_raw * inverse_norm(image_raw)).astype(bf16)

        weights = lax.all_gather(packed, both, axis=0).reshape(dp_size, mp_size, 3, depth, -1)
        weights = weights.transpose(2, 1, 0, 3, 4).reshape(3, mp_size, width, -1)
        vectors = lax.all_gather(norms, "dp", axis=1, tiled=True).astype(f32)
        all_image = lax.all_gather(image_unit, both, axis=0, tiled=True)
        all_valid = lax.all_gather(slot_valid.astype(bf16), both, axis=0, tiled=True) > 0

        own = lax.dynamic_slice_in_dim(tokens, mp_rank * rows, rows, 0).astype(f32)
        ids = lax.dynamic_slice_in_dim(segment_ids, mp_rank * rows, rows, 0)
        grid_ids = ids.reshape(seqs, SEQ_LEN)
        first_len = jnp.sum((grid_ids == 0).astype(jnp.int32), axis=1)
        starts = jnp.arange(seqs, dtype=jnp.int32) * SEQ_LEN
        ends = jnp.stack([starts + first_len - 1, starts + SEQ_LEN - 1], axis=1).reshape(2 * seqs)
        place = (ends[:, None] == jnp.arange(rows)[None, :]).astype(bf16)

        hat_one, rstd_one = standardise(own)
        normed = (hat_one * vectors[0] + vectors[1]).astype(bf16)
        attn = weights[0]
        qkv = jnp.einsum("rd,mde->mre", normed, attn[:, :, : 3 * head_cols], preferred_element_type=f32)
        qkv = qkv.astype(bf16).reshape(mp_size, rows, 3, heads, HEAD_DIM)
        blocks = rows // tile_rows
        split = qkv.reshape(mp_size, blocks, tile_rows, 3, heads, HEAD_DIM)
        query, key, value = split[:, :, :, 0], split[:, :, :, 1], split[:, :, :, 2]
        tile_ids = ids.reshape(blocks, tile_rows)
        spots = jnp.arange(tile_rows)
        allowed = (
            (tile_ids[:, :, None] == tile_ids[:, None, :])
            & (spots[:, None] // SEQ_LEN == spots[None, :] // SEQ_LEN)[None]
            & (spots[:, None] >= spots[None, :])[None]
        )[None, :, None]
        scale = HEAD_DIM**-0.5
        scores = jnp.einsum("mbqhc,mbkhc->mbhqk", query, key, preferred_element_type=f32) * scale
        scores = jnp.where(allowed, scores, -1e30)
        probs = jax.nn.softmax(scores, axis=-1)
        mixed = jnp.einsum("mbhqk,mbkhc->mbqhc", probs.astype(bf16), value, preferred_element_type=f32)
        mixed = mixed.astype(bf16).reshape(mp_size, rows, head_cols)
        out_t = attn[:, :, 3 * head_cols :]
        attended = jnp.einsum("mre,mde->rd", mixed, out_t, preferred_element_type=f32)
        hidden = own + attended

        def feed(rows_in):
            hat, rstd = standardise(rows_in)
            normed_two = (hat * vectors[2] + vectors[3]).astype(bf16)
            upper = jnp.einsum("rd,mdf->mrf", normed_two, weights[1], preferred_element_type=f32)
            active = (upper * phi(upper)).astype(bf16)
            branch = jnp.einsum("mrf,mdf->rd", active, weights[2], preferred_element_type=f32)
            return hat, rstd, normed_two, upper, active, rows_in + branch

        block_out = feed(hidden)[-1].astype(bf16)
        hidden_ends = hidden[ends]
        hat_two, rstd_two, normed_two, upper, active, pooled = feed(hidden_ends)

        scale_back = inverse_norm(pooled)
        text = (pooled * scale_back).astype(bf16)
        logits = logit_scale * nt(text, all_image)
        live = slot_valid > 0
        weight = jnp.exp(logits)
        row_sum = jnp.sum(jnp.where(all_valid[None, :], weight, 0.0), axis=1)
        col_part = jnp.sum(jnp.where(live[:, None], weight, 0.0), axis=0)
        row_index = (dp_rank * mp_size + mp_rank) * slots + jnp.arange(slots)
        target = jnp.arange(slot_total)[None, :] == row_index[:, None]
        matched = jnp.sum(jnp.where(target, logits, 0.0), axis=1)
        row_part = jnp.sum(jnp.where(live, jnp.log(row_sum) - 2.0 * matched, 0.0))
        sums = lax.psum(jnp.concatenate([col_part, row_part[None]]), both)
        col_sum = sums[:slot_total]
        loss = 0.5 * (sums[slot_total] + jnp.sum(jnp.where(all_valid, jnp.log(col_sum), 0.0))) / slot_total
        pair = live[:, None] & all_valid[None, :]
        spread = 0.5 * weight * (1.0 / row_sum[:, None] + 1.0 / col_sum[None, :])
        grad_logits = jnp.where(pair, spread, 0.0) - (target & live[:, None]).astype(f32)
        cosine_grad = (logit_scale * grad_logits).astype(bf16)
        unit_grad = nn(cosine_grad, all_image)
        along = jnp.sum(unit_grad * pooled, axis=-1, keepdims=True)
        pooled_grad = scale_back * unit_grad - pooled * (scale_back * scale_back * scale_back * along)

        branch_grad = pooled_grad.astype(bf16)
        down_local = jnp.einsum("rd,mrf->mdf", branch_grad, active, preferred_element_type=f32)
        active_grad = jnp.einsum("rd,mdf->mrf", branch_grad, weights[2], preferred_element_type=f32)
        slope = phi(upper) + upper * jnp.exp(-0.5 * upper * upper) * (1.0 / (2.0 * jnp.pi) ** 0.5)
        upper_grad = (active_grad * slope).astype(bf16)
        up_local = jnp.einsum("rd,mrf->mdf", normed_two, upper_grad, preferred_element_type=f32)
        normed_two_grad = jnp.einsum("mrf,mdf->rd", upper_grad, weights[1], preferred_element_type=f32)
        gain_two = jnp.sum(normed_two_grad * hat_two, axis=0)
        bias_two = jnp.sum(normed_two_grad, axis=0)
        hidden_grad = pooled_grad + norm_pull(normed_two_grad, hat_two, rstd_two, vectors[2])

        attended_grad = hidden_grad.astype(bf16)
        mixed_ends = mixed[:, ends]
        out_local = jnp.einsum("rd,mre->mde", attended_grad, mixed_ends, preferred_element_type=f32)
        mixed_grad = jnp.einsum("rd,mde->mre", attended_grad, out_t, preferred_element_type=f32).astype(bf16)
        mixed_grad = mixed_grad.reshape(mp_size, 2 * seqs, heads, HEAD_DIM)
        query_ends, keys, values = qkv[:, ends, 0], qkv[:, :, 1], qkv[:, :, 2]
        spot = jnp.arange(rows)
        allowed_ends = (
            (ids[ends][:, None] == ids[None, :])
            & (ends[:, None] // SEQ_LEN == spot[None, :] // SEQ_LEN)
            & (ends[:, None] >= spot[None, :])
        )[None, None]
        again = jnp.einsum("mqhc,mkhc->mhqk", query_ends, keys, preferred_element_type=f32) * scale
        probs_ends = jax.nn.softmax(jnp.where(allowed_ends, again, -1e30), axis=-1)
        probs_grad = jnp.einsum("mqhc,mkhc->mhqk", mixed_grad, values, preferred_element_type=f32)
        value_grad = jnp.einsum("mhqk,mqhc->mkhc", probs_ends.astype(bf16), mixed_grad, preferred_element_type=f32)
        centre = jnp.sum(probs_grad * probs_ends, axis=-1, keepdims=True)
        score_grad = (probs_ends * (probs_grad - centre)).astype(bf16)
        query_grad = jnp.einsum("mhqk,mkhc->mqhc", score_grad, keys, preferred_element_type=f32) * scale
        key_grad = jnp.einsum("mhqk,mqhc->mkhc", score_grad, query_ends, preferred_element_type=f32) * scale
        query_grad = query_grad.astype(bf16).reshape(mp_size, 2 * seqs, head_cols)
        query_grad = jnp.einsum("er,mec->mrc", place, query_grad, preferred_element_type=f32).astype(bf16)
        proj_grad = jnp.concatenate(
            [
                query_grad,
                key_grad.astype(bf16).reshape(mp_size, rows, head_cols),
                value_grad.astype(bf16).reshape(mp_size, rows, head_cols),
            ],
            axis=-1,
        )
        qkv_local = jnp.einsum("rd,mre->mde", normed, proj_grad, preferred_element_type=f32)
        normed_grad = jnp.einsum("mre,mde->rd", proj_grad, attn[:, :, : 3 * head_cols], preferred_element_type=f32)
        gain_one = jnp.sum(normed_grad * hat_one, axis=0)
        bias_one = jnp.sum(normed_grad, axis=0)
        token_grad = norm_pull(normed_grad, hat_one, rstd_one, vectors[0])
        token_grad = token_grad.at[ends].add(hidden_grad)

        local = jnp.stack([jnp.concatenate([qkv_local, out_local], axis=-1), up_local, down_local])
        local = local.reshape(3, mp_size, dp_size, depth, -1).transpose(2, 1, 0, 3, 4)
        local = local.reshape(dp_size * mp_size, 3, depth, -1)
        summed = lax.psum_scatter(local, both, scatter_dimension=0, tiled=False)
        vector_local = lax.psum(jnp.stack([gain_one, bias_one, gain_two, bias_two]), both)
        vector_own = lax.dynamic_slice_in_dim(vector_local, dp_rank * depth, depth, 1)

        block_out = lax.all_gather(block_out, "mp", axis=0, tiled=True)
        token_grad = lax.all_gather(token_grad, "mp", axis=0, tiled=True)
        qkv_grad = summed[0, :, : 3 * head_cols].reshape(depth, 3, head_cols).transpose(1, 0, 2)
        return (
            loss,
            block_out,
            token_grad,
            vector_own[0],
            vector_own[1],
            qkv_grad,
            summed[0, :, 3 * head_cols :].T,
            vector_own[2],
            vector_own[3],
            summed[1],
            summed[2].T,
        )

    return on_device


def solution(mesh):
    placed = (
        P("dp", None),
        P("dp"),
        P(("dp", "mp")),
        P("dp"),
        P("dp"),
        P(None, "dp", "mp"),
        P("mp", "dp"),
        P("dp"),
        P("dp"),
        P("dp", "mp"),
        P("mp", "dp"),
        P(("dp", "mp"), None),
        P(),
        P(),
        P(),
    )
    return jax.shard_map(
        make(mesh.shape["dp"], mesh.shape["mp"]),
        mesh=mesh,
        in_specs=placed,
        out_specs=(
            P(),
            P("dp", None),
            P("dp", None),
            P("dp"),
            P("dp"),
            P(None, "dp", "mp"),
            P("mp", "dp"),
            P("dp"),
            P("dp"),
            P("dp", "mp"),
            P("mp", "dp"),
        ),
        check_vma=False,
    )
```

```python
import jax
import jax.numpy as jnp
from jax import lax
from jax.sharding import PartitionSpec as P
import functools
from jax.experimental import pallas as pl
from jax.experimental.pallas import tpu as pltpu
MESH = pl.DeviceIdType.MESH

HEAD_DIM = 64
SEQ_LEN = 16
norm_epsilon = 1e-05
unit_epsilon = 1e-06
logit_scale = 50.0
tile_rows = 128
f32, bf16 = jnp.float32, jnp.bfloat16


def gather_kernel(kinds, order, *refs):
    n=len(kinds)
    srcs=refs[:n]; outs=refs[n:2*n]; sems=refs[2*n:]
    dp=lax.axis_index("dp"); mp=lax.axis_index("mp")
    z=lax.div(dp,2); x=lax.rem(dp,2); y=lax.div(mp,2); c=lax.rem(mp,2)
    xd, ym, cm = 2*z+(1-x), 2*(1-y)+c, 2*y+(1-c)
    zp=[lax.rem(z+j,4) for j in range(4)]
    zs=[lax.rem(z+4-j,4) for j in range(4)]
    X=(xd,mp); Y=(dp,ym); C=(dp,cm); Z=[(2*zp[j]+x,mp) for j in range(4)]
    bar=pltpu.get_barrier_semaphore()
    peers=[X,Y,C]+Z[1:]
    for p in peers: pl.semaphore_signal(bar,inc=1,device_id=p,device_id_type=MESH)
    pl.semaphore_wait(bar,len(peers))
    stages={}
    for k,(rows,cut) in enumerate(kinds):
        src,out=srcs[k],outs[k]
        zr,x0,y1,y0,x1,cr,sd=sems[7*k:7*k+7]
        spans=[(0,cut),(cut,rows-cut)] if cut else [(0,rows)]
        full=(0,rows)
        def piece(d,m,span,out=out,rows=rows):
            return out.at[m, pl.ds(pl.multiple_of(d*rows+span[0],16), span[1])]
        def send(src_ref,dst_ref,rsem,dev,sd=sd):
            pltpu.make_async_remote_copy(src_ref=src_ref,dst_ref=dst_ref,send_sem=sd.at[0],recv_sem=rsem,device_id=dev,device_id_type=MESH).start()
        def arrived(ref,rsem,sd=sd):
            pltpu.make_async_remote_copy(src_ref=ref,dst_ref=ref,send_sem=sd.at[0],recv_sem=rsem,device_id=X,device_id_type=MESH).wait_recv()
        h0=spans[0]; h1=spans[1] if cut else None
        def s0(src=src,zr=zr,x0=x0,y1=y1,y0=y0,x1=x1,cr=cr,sd=sd,send=send,piece=piece,h0=h0,h1=h1,full=full):
            for j in range(1,4): send(src,piece(dp,mp,full),zr.at[j],Z[j])
            send(src.at[pl.ds(*h0)],piece(dp,mp,h0),x0.at[0],X)
            if h1: send(src.at[pl.ds(*h1)],piece(dp,mp,h1),y1.at[0],Y)
            send(src.at[pl.ds(*h0)],piece(dp,mp,h0),y0.at[0],Y)
            if h1: send(src.at[pl.ds(*h1)],piece(dp,mp,h1),x1.at[0],X)
            send(src,piece(dp,mp,full),cr.at[0],C)
            pltpu.make_async_copy(src,piece(dp,mp,full),sd.at[0]).start()
        def s1(send=send,arrived=arrived,piece=piece,zr=zr,x0=x0,y1=y1,y0=y0,x1=x1,cr=cr,h0=h0,h1=h1,full=full):
            for j in range(1,4):
                d=2*zs[j]+x
                b=piece(d,mp,full); arrived(b,zr.at[j])
                send(piece(d,mp,h0),piece(d,mp,h0),x0.at[j],X)
                if h1: send(piece(d,mp,h1),piece(d,mp,h1),y1.at[j],Y)
                send(piece(d,mp,h0),piece(d,mp,h0),y0.at[j],Y)
                if h1: send(piece(d,mp,h1),piece(d,mp,h1),x1.at[j],X)
                send(b,b,cr.at[0],C)
        def s2(send=send,arrived=arrived,piece=piece,zr=zr,x0=x0,y1=y1,y0=y0,x1=x1,cr=cr,h0=h0,h1=h1):
            for j in range(4):
                b=piece(2*zs[j]+(1-x),mp,h0); arrived(b,x0.at[j])
                send(b,b,y0.at[4+j],Y); send(b,b,cr.at[0],C)
                if h1:
                    b=piece(2*zs[j]+x,ym,h1); arrived(b,y1.at[j])
                    send(b,b,x1.at[4+j],X); send(b,b,cr.at[0],C)
        def s3(send=send,arrived=arrived,piece=piece,zr=zr,x0=x0,y1=y1,y0=y0,x1=x1,cr=cr,h0=h0,h1=h1):
            for i in range(2):
                for j in range(4):
                    b=piece(2*zs[j]+(x if i==0 else 1-x),ym,h0); arrived(b,y0.at[4*i+j])
                    send(b,b,cr.at[0],C)
                    if h1:
                        b=piece(2*zs[j]+(1-x),(mp if i==0 else ym),h1); arrived(b,x1.at[4*i+j])
                        send(b,b,cr.at[0],C)
        def s4(out=out,cr=cr,sd=sd):
            half=out.at[pl.ds(0,2)]
            pltpu.make_async_copy(half,half,cr.at[0]).wait()
            pltpu.make_async_copy(out,out,sd.at[0]).wait()
        stages[k]=[s0,s1,s2,s3,s4]
    for k,s in order: stages[k][s]()

def gather(arrs, cuts, order, vmem=False):
    kinds=[(a.shape[0],c) for a,c in zip(arrs,cuts)]
    sems=[]
    for _ in kinds:
        sems+= [pltpu.SemaphoreType.DMA((4,)),pltpu.SemaphoreType.DMA((4,)),pltpu.SemaphoreType.DMA((4,)),pltpu.SemaphoreType.DMA((8,)),pltpu.SemaphoreType.DMA((8,)),pltpu.SemaphoreType.DMA((1,)),pltpu.SemaphoreType.DMA((1,))]
    ms=pltpu.VMEM if vmem else pltpu.HBM
    return pl.pallas_call(functools.partial(gather_kernel,kinds,order),
        out_shape=[jax.ShapeDtypeStruct((4,8*a.shape[0],a.shape[1]),a.dtype) for a in arrs],
        in_specs=[pl.BlockSpec(memory_space=ms)]*len(arrs), out_specs=[pl.BlockSpec(memory_space=ms)]*len(arrs),
        scratch_shapes=sems,
        compiler_params=pltpu.CompilerParams(collective_id=1,has_side_effects=True,vmem_limit_bytes=60*2**20),name="gatherk")(*arrs)


ORDER = sorted([(k, s) for k in range(5) for s in range(5)], key=lambda t: (t[1] * 2 + t[0], t[0]))
H=48
def reduce_kernel(nk, *refs):
    grads=refs[:nk]; vec=refs[nk]; outs=refs[nk+1:2*nk+1]; vout=refs[2*nk+1]
    (acc,cr,r1p,r1q,r2p,r2q,r3,vbuf,vrec, s_cr,s_1p,s_1q,s_2p,s_2q,s_3,s_send,s_v,s_vs)=refs[2*nk+2:]
    dp=lax.axis_index("dp"); mp=lax.axis_index("mp")
    z=lax.div(dp,2); x=lax.rem(dp,2); y=lax.div(mp,2); c=lax.rem(mp,2)
    X=(2*z+(1-x),mp); Y=(dp,2*(1-y)+c); C=(dp,2*y+(1-c))
    zt=[lax.rem(z+j,4) for j in range(4)]
    Z=[(2*zt[j]+x,mp) for j in range(4)]
    peers=[X,Y,C]+Z[1:]
    bar=pltpu.get_barrier_semaphore()
    for p in peers: pl.semaphore_signal(bar,inc=1,device_id=p,device_id_type=MESH)
    pl.semaphore_wait(bar,len(peers))
    def rows(yy,zz,xx,h,n=H):
        return pl.ds(pl.multiple_of(yy*768+(2*zz+xx)*96+h*H,16),n)
    def send(src,dst,rsem,dev,ssem):
        pltpu.make_async_remote_copy(src_ref=src,dst_ref=dst,send_sem=ssem,recv_sem=rsem,device_id=dev,device_id_type=MESH).start()
    def arrived(ref,rsem):
        pltpu.make_async_remote_copy(src_ref=ref,dst_ref=ref,send_sem=s_send.at[0],recv_sem=rsem,device_id=X,device_id_type=MESH).wait_recv()
    def add(k,src,dst_rows,got):
        acc[k,dst_rows,:]=(src.astype(f32)+got.astype(f32)).astype(bf16)
    far=[(1,1),(1,0),(0,1),(0,0)]
    def yy(d): return y if d==0 else 1-y
    def xx(d): return x if d==0 else 1-x
    def core_start(k):
        g=grads[k]
        for (dy,dx) in far:
            for j in range(4):
                src=g.at[pl.ds(pl.multiple_of((2*yy(dy)+(1-c))*768+(2*zt[j]+xx(dx))*96,16),96)]
                i=(dy*2+dx)*4+j
                send(src,cr.at[k,i],s_cr.at[k,i],C,s_send.at[k])
    def core_add(k):
        g=grads[k]
        for (dy,dx) in far:
            for j in range(4):
                i=(dy*2+dx)*4+j
                arrived(cr.at[k,i],s_cr.at[k,i])
                own=g[pl.ds(pl.multiple_of((2*yy(dy)+c)*768+(2*zt[j]+xx(dx))*96,16),96),:]
                add(k,own,rows(yy(dy),zt[j],xx(dx),0,96),cr[k,i])
                if dy==1: send(acc.at[k,rows(1-y,zt[j],xx(dx),0)],r1p.at[k,dx*4+j],s_1p.at[k,dx*4+j],Y,s_send.at[k])
                if dx==1: send(acc.at[k,rows(yy(dy),zt[j],1-x,1)],r1q.at[k,dy*4+j],s_1q.at[k,dy*4+j],X,s_send.at[k])
    def first_add(k):
        for d in (1,0):
            for j in range(4):
                i=d*4+j
                arrived(r1p.at[k,i],s_1p.at[k,i])
                rr=rows(y,zt[j],xx(d),0)
                add(k,acc[k,rr,:],rr,r1p[k,i])
                if d==1: send(acc.at[k,rr],r2p.at[k,j],s_2p.at[k,j],X,s_send.at[k])
                arrived(r1q.at[k,i],s_1q.at[k,i])
                rr=rows(yy(d),zt[j],x,1)
                add(k,acc[k,rr,:],rr,r1q[k,i])
                if d==1: send(acc.at[k,rr],r2q.at[k,j],s_2q.at[k,j],Y,s_send.at[k])
    def second_add(k):
        for j in (2,1,3,0):
            arrived(r2p.at[k,j],s_2p.at[k,j])
            rr=rows(y,zt[j],x,0)
            if j: add(k,acc[k,rr,:],rr,r2p[k,j])
            arrived(r2q.at[k,j],s_2q.at[k,j])
            r2=rows(y,zt[j],x,1)
            if j:
                add(k,acc[k,r2,:],r2,r2q[k,j])
                send(acc.at[k,rows(y,zt[j],x,0,96)],r3.at[k,j-1],s_3.at[k,j-1],Z[j],s_send.at[k])
            else:
                outs[k][0:H,:]=acc[k,rr,:].astype(f32)+r2p[k,0].astype(f32)
                outs[k][H:2*H,:]=acc[k,r2,:].astype(f32)+r2q[k,0].astype(f32)
    def third_add(k):
        for j in range(1,4): arrived(r3.at[k,j-1],s_3.at[k,j-1])
        outs[k][...]=outs[k][...]+r3[k,0].astype(f32)+r3[k,1].astype(f32)+r3[k,2].astype(f32)
        w=grads[k].at[pl.ds(0,31*96)]
        pltpu.make_async_copy(w,w,s_send.at[k]).wait()
    def v_swap(i,dev,cur):
        vbuf[i]=cur
        cp=pltpu.make_async_remote_copy(src_ref=vbuf.at[i],dst_ref=vrec.at[i],send_sem=s_vs.at[i],recv_sem=s_v.at[i],device_id=dev,device_id_type=MESH)
        cp.start(); return cp
    core_start(0)
    v0=v_swap(0,C,vec[...])
    for k in range(1,nk): core_start(k)
    core_add(0)
    v0.wait(); v1=v_swap(1,Y,vbuf[0]+vrec[0])
    if nk>1: core_add(1)
    first_add(0)
    v1.wait(); v2=v_swap(2,X,vbuf[1]+vrec[1])
    if nk>2: core_add(2)
    if nk>1: first_add(1)
    second_add(0)
    v2.wait()
    vbuf[3]=vbuf[2]+vrec[2]
    cps=[]
    for j in range(1,4):
        cp=pltpu.make_async_remote_copy(src_ref=vbuf.at[3],dst_ref=vrec.at[3+z],send_sem=s_vs.at[2+j],recv_sem=s_v.at[2+j],device_id=Z[j],device_id_type=MESH)
        cp.start(); cps.append(cp)
    vrec[3+z]=vbuf[3]
    if nk>2: first_add(2)
    if nk>1: second_add(1)
    third_add(0)
    if nk>2: second_add(2)
    if nk>1: third_add(1)
    if nk>2: third_add(2)
    for cp in cps: cp.wait()
    vout[...]=(vrec[3]+vrec[4])+(vrec[5]+vrec[6])
def reduce(grads,vec):
    nk=len(grads)
    V=pltpu.VMEM; D=pltpu.SemaphoreType.DMA
    return pl.pallas_call(functools.partial(reduce_kernel,nk),
      out_shape=[jax.ShapeDtypeStruct((96,768),f32)]*nk+[jax.ShapeDtypeStruct((8,768),f32)],
      in_specs=[pl.BlockSpec(memory_space=V)]*(nk+1), out_specs=[pl.BlockSpec(memory_space=V)]*(nk+1),
      scratch_shapes=[V((nk,1536,768),bf16),V((nk,16,96,768),bf16),V((nk,8,H,768),bf16),V((nk,8,H,768),bf16),V((nk,4,H,768),bf16),V((nk,4,H,768),bf16),V((nk,3,96,768),bf16),V((4,8,768),f32),V((7,8,768),f32),
        D((nk,16)),D((nk,8)),D((nk,8)),D((nk,4)),D((nk,4)),D((nk,3)),D((nk,)),D((6,)),D((6,))],
      compiler_params=pltpu.CompilerParams(collective_id=2,has_side_effects=True,vmem_limit_bytes=60*2**20),name="reducek")(*grads,vec)

def sum_kernel(val,out,buf,rec,s_r,s_s):
    dp=lax.axis_index("dp"); mp=lax.axis_index("mp")
    z=lax.div(dp,2); x=lax.rem(dp,2); y=lax.div(mp,2); c=lax.rem(mp,2)
    C=(dp,2*y+(1-c))
    zt=[lax.rem(z+j,4) for j in range(4)]
    Z=[(2*zt[j]+x,mp) for j in range(4)]
    xy=2*y+x
    Q=[]
    for j in range(1,4):
        o=lax.rem(xy+j,4); Q.append((2*z+lax.rem(o,2),2*lax.div(o,2)+c))
    peers=[C]+Q+Z[1:]
    bar=pltpu.get_barrier_semaphore()
    for p in peers: pl.semaphore_signal(bar,inc=1,device_id=p,device_id_type=MESH)
    pl.semaphore_wait(bar,len(peers))
    def go(src,dst,i,dev):
        cp=pltpu.make_async_remote_copy(src_ref=src,dst_ref=dst,send_sem=s_s.at[i],recv_sem=s_r.at[i],device_id=dev,device_id_type=MESH); cp.start(); return cp
    go(val,rec.at[0],0,C).wait()
    buf[0]=val[...]+rec[0]
    cps=[go(buf.at[0],rec.at[1+xy],j,Q[j-1]) for j in range(1,4)]
    rec[1+xy]=buf[0]
    for cp in cps: cp.wait()
    buf[1]=(rec[1]+rec[2])+(rec[3]+rec[4])
    cps=[go(buf.at[1],rec.at[5+z],3+j,Z[j]) for j in range(1,4)]
    rec[5+z]=buf[1]
    for cp in cps: cp.wait()
    out[...]=(rec[5]+rec[6])+(rec[7]+rec[8])
def allsum(v):
    V=pltpu.VMEM; D=pltpu.SemaphoreType.DMA
    return pl.pallas_call(sum_kernel,out_shape=jax.ShapeDtypeStruct(v.shape,f32),in_specs=[pl.BlockSpec(memory_space=V)],out_specs=pl.BlockSpec(memory_space=V),
      scratch_shapes=[V((2,)+v.shape,f32),V((9,)+v.shape,f32),D((7,)),D((7,))],
      compiler_params=pltpu.CompilerParams(collective_id=3,has_side_effects=True),name="sumk")(v)


def standardise(values):
    centred = values - jnp.mean(values, axis=-1, keepdims=True)
    rstd = lax.rsqrt(jnp.mean(centred * centred, axis=-1, keepdims=True) + norm_epsilon)
    return centred * rstd, rstd


def norm_pull(grad, hat, rstd, gain):
    scaled = grad * gain
    first = jnp.mean(scaled, axis=-1, keepdims=True)
    second = jnp.mean(scaled * hat, axis=-1, keepdims=True)
    return rstd * (scaled - first - hat * second)


def inverse_norm(values):
    return lax.rsqrt(jnp.sum(values * values, axis=-1, keepdims=True) + unit_epsilon)


def nn(left, right):
    return lax.dot_general(left, right, (((1,), (0,)), ((), ())), preferred_element_type=f32)


def nt(left, right):
    return lax.dot_general(left, right, (((1,), (1,)), ((), ())), preferred_element_type=f32)


def tn(left, right):
    return lax.dot_general(left, right, (((0,), (0,)), ((), ())), preferred_element_type=f32)


def phi(values):
    return 0.5 * lax.erfc(-values * (0.5**0.5))


def make(dp_size, mp_size):
    kernels = dp_size == 8 and mp_size == 4

    def on_device(
        tokens,
        segment_ids,
        slot_valid,
        ln1_gain,
        ln1_bias,
        w_qkv,
        w_out,
        ln2_gain,
        ln2_bias,
        w_up,
        w_down,
        class_tokens,
        image_gain,
        image_bias,
        image_proj,
    ):
        both = ("dp", "mp")
        dp_rank, mp_rank = lax.axis_index("dp"), lax.axis_index("mp")
        depth = w_up.shape[0]
        width = depth * dp_size
        head_cols = w_out.shape[0]
        heads = head_cols // HEAD_DIM
        rows = tokens.shape[0] // mp_size
        seqs = rows // SEQ_LEN
        slots = slot_valid.shape[0]
        slot_total = slots * dp_size * mp_size

        packed = jnp.stack(
            [jnp.concatenate([w_qkv[0], w_qkv[1], w_qkv[2], w_out.T], axis=1), w_up, w_down.T]
        )
        norms = jnp.stack([ln1_gain, ln1_bias, ln2_gain, ln2_bias])
        image_hat, _ = standardise(class_tokens.astype(f32))
        image_normed = (image_hat * image_gain + image_bias).astype(bf16)
        image_raw = nn(image_normed, image_proj)
        image_unit = (image_raw * inverse_norm(image_raw)).astype(bf16)

        if kernels:
            small = jnp.zeros((16, 128), bf16).at[:4, :depth].set(norms).at[4, :slots].set(slot_valid.astype(bf16))
            got = gather([small, packed[0], packed[1], packed[2], image_unit], [0, 48, 48, 48, 32], ORDER)
            weights = got[1:4]
            smalls = got[0].reshape(mp_size, dp_size, 16, 128).transpose(1, 0, 2, 3)
            vectors = smalls[:, 0, :4, :depth].transpose(1, 0, 2).reshape(4, width).astype(f32)
            all_valid = smalls[:, :, 4, :slots].reshape(slot_total) > 0
            all_image = got[4].reshape(mp_size, dp_size, slots, width).transpose(1, 0, 2, 3).reshape(slot_total, width)
        else:
            weights = lax.all_gather(packed, both, axis=0).reshape(dp_size, mp_size, 3, depth, -1)
            weights = weights.transpose(2, 1, 0, 3, 4).reshape(3, mp_size, width, -1)
            vectors = lax.all_gather(norms, "dp", axis=1, tiled=True).astype(f32)
            all_image = lax.all_gather(image_unit, both, axis=0, tiled=True)
            all_valid = lax.all_gather(slot_valid.astype(bf16), both, axis=0, tiled=True) > 0

        own = lax.dynamic_slice_in_dim(tokens, mp_rank * rows, rows, 0).astype(f32)
        ids = lax.dynamic_slice_in_dim(segment_ids, mp_rank * rows, rows, 0)
        grid_ids = ids.reshape(seqs, SEQ_LEN)
        first_len = jnp.sum((grid_ids == 0).astype(jnp.int32), axis=1)
        starts = jnp.arange(seqs, dtype=jnp.int32) * SEQ_LEN
        ends = jnp.stack([starts + first_len - 1, starts + SEQ_LEN - 1], axis=1).reshape(2 * seqs)
        place = (ends[:, None] == jnp.arange(rows)[None, :]).astype(bf16)

        hat_one, rstd_one = standardise(own)
        normed = (hat_one * vectors[0] + vectors[1]).astype(bf16)
        attn = weights[0]
        qkv = jnp.einsum("rd,mde->mre", normed, attn[:, :, : 3 * head_cols], preferred_element_type=f32)
        qkv = qkv.astype(bf16).reshape(mp_size, rows, 3, heads, HEAD_DIM)
        blocks = rows // tile_rows
        split = qkv.reshape(mp_size, blocks, tile_rows, 3, heads, HEAD_DIM)
        query, key, value = split[:, :, :, 0], split[:, :, :, 1], split[:, :, :, 2]
        tile_ids = ids.reshape(blocks, tile_rows)
        spots = jnp.arange(tile_rows)
        allowed = (
            (tile_ids[:, :, None] == tile_ids[:, None, :])
            & (spots[:, None] // SEQ_LEN == spots[None, :] // SEQ_LEN)[None]
            & (spots[:, None] >= spots[None, :])[None]
        )[None, :, None]
        scale = HEAD_DIM**-0.5
        scores = jnp.einsum("mbqhc,mbkhc->mbhqk", query, key, preferred_element_type=f32) * scale
        scores = jnp.where(allowed, scores, -1e30)
        probs = jax.nn.softmax(scores, axis=-1)
        mixed = jnp.einsum("mbhqk,mbkhc->mbqhc", probs.astype(bf16), value, preferred_element_type=f32)
        mixed = mixed.astype(bf16).reshape(mp_size, rows, head_cols)
        out_t = attn[:, :, 3 * head_cols :]
        attended = jnp.einsum("mre,mde->rd", mixed, out_t, preferred_element_type=f32)
        hidden = own + attended

        def feed(rows_in):
            hat, rstd = standardise(rows_in)
            normed_two = (hat * vectors[2] + vectors[3]).astype(bf16)
            upper = jnp.einsum("rd,mdf->mrf", normed_two, weights[1], preferred_element_type=f32)
            active = (upper * phi(upper)).astype(bf16)
            branch = jnp.einsum("mrf,mdf->rd", active, weights[2], preferred_element_type=f32)
            return hat, rstd, normed_two, upper, active, rows_in + branch

        block_out = feed(hidden)[-1].astype(bf16)
        hidden_ends = hidden[ends]
        hat_two, rstd_two, normed_two, upper, active, pooled = feed(hidden_ends)

        scale_back = inverse_norm(pooled)
        text = (pooled * scale_back).astype(bf16)
        logits = logit_scale * nt(text, all_image)
        live = slot_valid > 0
        weight = jnp.exp(logits)
        row_sum = jnp.sum(jnp.where(all_valid[None, :], weight, 0.0), axis=1)
        col_part = jnp.sum(jnp.where(live[:, None], weight, 0.0), axis=0)
        row_index = (dp_rank * mp_size + mp_rank) * slots + jnp.arange(slots)
        target = jnp.arange(slot_total)[None, :] == row_index[:, None]
        matched = jnp.sum(jnp.where(target, logits, 0.0), axis=1)
        row_part = jnp.sum(jnp.where(live, jnp.log(row_sum) - 2.0 * matched, 0.0))
        if kernels:
            parts = jnp.concatenate([col_part, jnp.broadcast_to(row_part[None], (1024,))])
            sums = allsum(parts.reshape(-1, 128)).reshape(-1)
        else:
            sums = lax.psum(jnp.concatenate([col_part, row_part[None]]), both)
        col_sum = sums[:slot_total]
        loss = 0.5 * (sums[slot_total] + jnp.sum(jnp.where(all_valid, jnp.log(col_sum), 0.0))) / slot_total
        pair = live[:, None] & all_valid[None, :]
        spread = 0.5 * weight * (1.0 / row_sum[:, None] + 1.0 / col_sum[None, :])
        grad_logits = jnp.where(pair, spread, 0.0) - (target & live[:, None]).astype(f32)
        cosine_grad = (logit_scale * grad_logits).astype(bf16)
        unit_grad = nn(cosine_grad, all_image)
        along = jnp.sum(unit_grad * pooled, axis=-1, keepdims=True)
        pooled_grad = scale_back * unit_grad - pooled * (scale_back * scale_back * scale_back * along)

        branch_grad = pooled_grad.astype(bf16)
        down_local = jnp.einsum("rd,mrf->mdf", branch_grad, active, preferred_element_type=f32)
        active_grad = jnp.einsum("rd,mdf->mrf", branch_grad, weights[2], preferred_element_type=f32)
        slope = phi(upper) + upper * jnp.exp(-0.5 * upper * upper) * (1.0 / (2.0 * jnp.pi) ** 0.5)
        upper_grad = (active_grad * slope).astype(bf16)
        up_local = jnp.einsum("rd,mrf->mdf", normed_two, upper_grad, preferred_element_type=f32)
        normed_two_grad = jnp.einsum("mrf,mdf->rd", upper_grad, weights[1], preferred_element_type=f32)
        gain_two = jnp.sum(normed_two_grad * hat_two, axis=0)
        bias_two = jnp.sum(normed_two_grad, axis=0)
        hidden_grad = pooled_grad + norm_pull(normed_two_grad, hat_two, rstd_two, vectors[2])

        attended_grad = hidden_grad.astype(bf16)
        mixed_ends = mixed[:, ends]
        out_local = jnp.einsum("rd,mre->mde", attended_grad, mixed_ends, preferred_element_type=f32)
        mixed_grad = jnp.einsum("rd,mde->mre", attended_grad, out_t, preferred_element_type=f32).astype(bf16)
        mixed_grad = mixed_grad.reshape(mp_size, 2 * seqs, heads, HEAD_DIM)
        query_ends, keys, values = qkv[:, ends, 0], qkv[:, :, 1], qkv[:, :, 2]
        spot = jnp.arange(rows)
        allowed_ends = (
            (ids[ends][:, None] == ids[None, :])
            & (ends[:, None] // SEQ_LEN == spot[None, :] // SEQ_LEN)
            & (ends[:, None] >= spot[None, :])
        )[None, None]
        again = jnp.einsum("mqhc,mkhc->mhqk", query_ends, keys, preferred_element_type=f32) * scale
        probs_ends = jax.nn.softmax(jnp.where(allowed_ends, again, -1e30), axis=-1)
        probs_grad = jnp.einsum("mqhc,mkhc->mhqk", mixed_grad, values, preferred_element_type=f32)
        value_grad = jnp.einsum("mhqk,mqhc->mkhc", probs_ends.astype(bf16), mixed_grad, preferred_element_type=f32)
        centre = jnp.sum(probs_grad * probs_ends, axis=-1, keepdims=True)
        score_grad = (probs_ends * (probs_grad - centre)).astype(bf16)
        query_grad = jnp.einsum("mhqk,mkhc->mqhc", score_grad, keys, preferred_element_type=f32) * scale
        key_grad = jnp.einsum("mhqk,mqhc->mkhc", score_grad, query_ends, preferred_element_type=f32) * scale
        query_grad = query_grad.astype(bf16).reshape(mp_size, 2 * seqs, head_cols)
        query_grad = jnp.einsum("er,mec->mrc", place, query_grad, preferred_element_type=f32).astype(bf16)
        proj_grad = jnp.concatenate(
            [
                query_grad,
                key_grad.astype(bf16).reshape(mp_size, rows, head_cols),
                value_grad.astype(bf16).reshape(mp_size, rows, head_cols),
            ],
            axis=-1,
        )
        qkv_local = jnp.einsum("rd,mre->mde", normed, proj_grad, preferred_element_type=f32)
        normed_grad = jnp.einsum("mre,mde->rd", proj_grad, attn[:, :, : 3 * head_cols], preferred_element_type=f32)
        gain_one = jnp.sum(normed_grad * hat_one, axis=0)
        bias_one = jnp.sum(normed_grad, axis=0)
        token_grad = norm_pull(normed_grad, hat_one, rstd_one, vectors[0])
        token_grad = token_grad.at[ends].add(hidden_grad)

        if kernels:
            attn_local = jnp.concatenate([qkv_local, out_local], axis=-1)
            local = [v.astype(bf16).reshape(mp_size * width, -1) for v in (down_local, up_local, attn_local)]
            zero = jnp.zeros_like(gain_one)
            own_down, own_up, own_attn, vector_local = reduce(
                local, jnp.stack([gain_one, bias_one, gain_two, bias_two] + [zero] * 4)
            )
            summed = (own_attn, own_up, own_down)
            token_grad = token_grad.astype(bf16)
        else:
            local = jnp.stack([jnp.concatenate([qkv_local, out_local], axis=-1), up_local, down_local])
            local = local.reshape(3, mp_size, dp_size, depth, -1).transpose(2, 1, 0, 3, 4)
            local = local.reshape(dp_size * mp_size, 3, depth, -1)
            summed = lax.psum_scatter(local, both, scatter_dimension=0, tiled=False)
            vector_local = lax.psum(jnp.stack([gain_one, bias_one, gain_two, bias_two]), both)
        vector_own = lax.dynamic_slice_in_dim(vector_local, dp_rank * depth, depth, 1)

        block_out = lax.all_gather(block_out, "mp", axis=0, tiled=True)
        token_grad = lax.all_gather(token_grad, "mp", axis=0, tiled=True).astype(f32)
        qkv_grad = summed[0][:, : 3 * head_cols].reshape(depth, 3, head_cols).transpose(1, 0, 2)
        return (
            loss,
            block_out,
            token_grad,
            vector_own[0],
            vector_own[1],
            qkv_grad,
            summed[0][:, 3 * head_cols :].T,
            vector_own[2],
            vector_own[3],
            summed[1],
            summed[2].T,
        )

    return on_device


def solution(mesh):
    placed = (
        P("dp", None),
        P("dp"),
        P(("dp", "mp")),
        P("dp"),
        P("dp"),
        P(None, "dp", "mp"),
        P("mp", "dp"),
        P("dp"),
        P("dp"),
        P("dp", "mp"),
        P("mp", "dp"),
        P(("dp", "mp"), None),
        P(),
        P(),
        P(),
    )
    return jax.shard_map(
        make(mesh.shape["dp"], mesh.shape["mp"]),
        mesh=mesh,
        in_specs=placed,
        out_specs=(
            P(),
            P("dp", None),
            P("dp", None),
            P("dp"),
            P("dp"),
            P(None, "dp", "mp"),
            P("mp", "dp"),
            P("dp"),
            P("dp"),
            P("dp", "mp"),
            P("mp", "dp"),
        ),
        check_vma=False,
    )
```

```python
import jax
import jax.numpy as jnp
from jax import lax
from jax.sharding import PartitionSpec as P
import functools
from jax.experimental import pallas as pl
from jax.experimental.pallas import tpu as pltpu

HEAD_DIM = 64
SEQ_LEN = 16
norm_epsilon = 1e-05
unit_epsilon = 1e-06
logit_scale = 50.0
tile_rows = 128
f32, bf16 = jnp.float32, jnp.bfloat16


def standardise(values):
    centred = values - jnp.mean(values, axis=-1, keepdims=True)
    rstd = lax.rsqrt(jnp.mean(centred * centred, axis=-1, keepdims=True) + norm_epsilon)
    return centred * rstd, rstd


def norm_pull(grad, hat, rstd, gain):
    scaled = grad * gain
    first = jnp.mean(scaled, axis=-1, keepdims=True)
    second = jnp.mean(scaled * hat, axis=-1, keepdims=True)
    return rstd * (scaled - first - hat * second)


def inverse_norm(values):
    return lax.rsqrt(jnp.sum(values * values, axis=-1, keepdims=True) + unit_epsilon)


def nn(left, right):
    return lax.dot_general(left, right, (((1,), (0,)), ((), ())), preferred_element_type=f32)


def nt(left, right):
    return lax.dot_general(left, right, (((1,), (1,)), ((), ())), preferred_element_type=f32)


def tn(left, right):
    return lax.dot_general(left, right, (((0,), (0,)), ((), ())), preferred_element_type=f32)


def phi(values):
    return 0.5 * lax.erfc(-values * (0.5**0.5))


MESH = pl.DeviceIdType.MESH
VMEM, DMA = pltpu.VMEM, pltpu.SemaphoreType.DMA
CUT = 48
LATE = 48


def loop(count, body):
    lax.fori_loop(0, count, lambda i, carry: (body(i), carry)[1], 0)


def rows_of(index, size):
    return pl.ds(pl.multiple_of(index * size, size), size)


def split_three(values):
    first = values.astype(bf16)
    rest = values - first.astype(f32)
    second = rest.astype(bf16)
    return first, second, (rest - second.astype(f32)).astype(bf16)


def pick(place, values):
    return sum(nn(place, part) for part in split_three(values))


def spread_rows(place, values):
    return sum(tn(place, part) for part in split_three(values))


def half_erf(values):
    return 0.5 + 0.5 * lax.erf(values * (0.5**0.5))


def layer_kernel(slot_total, *refs):
    (packed, small, classes, image_gain, image_bias, image_proj, tokens, ids) = refs[:8]
    (loss_out, block_out, token_out, attn_out, up_out, down_out, vec_out) = refs[8:15]
    (w_attn, w_up, w_down, images, smalls, x_ref, a_ref, qkv, hidden, a_two, active, stage_out, image_own, vecs) = refs[15:29]
    (mask_ref, place_ref, member_ref, h_ends, ends_two, ends_grad, u_ends, g_all, s_all, weight_ref, valid_ref) = refs[29:40]
    (sum_own, sum_buf, sum_got, d_attn, d_qkv) = refs[40:45]
    (grad_down, grad_up, ffn_one, ffn_three, attn_send, attn_acc, attn_core, one_p, one_q, two_p, two_q, three_a) = refs[45:57]
    (vec_buf, vec_got, stage_grad, grad_got) = refs[57:61]
    gsems = refs[61:96]
    (s_local, s_bo, s_boc, s_send, s_a2, s_dm, s_sum, s_sums, s_f1, s_f3, s_core, s_1p, s_1q, s_2p, s_2q, s_3, s_v, s_vs, s_tg, s_exs) = refs[96:116]

    dp = lax.axis_index("dp")
    mp = lax.axis_index("mp")
    z = lax.div(dp, 2)
    x = lax.rem(dp, 2)
    y = lax.div(mp, 2)
    c = lax.rem(mp, 2)
    xd, ym, cm = 2 * z + (1 - x), 2 * (1 - y) + c, 2 * y + (1 - c)
    zt = [lax.rem(z + j, 4) for j in range(4)]
    zs = [lax.rem(z + 4 - j, 4) for j in range(4)]
    X, Y, C, YC = (xd, mp), (dp, ym), (dp, cm), (dp, 3 - mp)
    Z = [(2 * zt[j] + x, mp) for j in range(4)]
    xy = 2 * y + x
    Q = []
    for j in range(1, 4):
        other = lax.rem(xy + j, 4)
        Q.append((2 * z + lax.rem(other, 2), 2 * lax.div(other, 2) + c))
    G = [(dp, lax.rem(mp + j, 4)) for j in range(4)]

    far_xy = (2 * z + (1 - x), 2 * (1 - y) + c)
    peers = [X, Y, C, YC, far_xy] + Z[1:]
    barrier = pltpu.get_barrier_semaphore()
    for peer in peers:
        pl.semaphore_signal(barrier, inc=1, device_id=peer, device_id_type=MESH)
    pl.semaphore_wait(barrier, len(peers))

    def remote(src, dst, send_sem, recv_sem, device):
        copy = pltpu.make_async_remote_copy(
            src_ref=src, dst_ref=dst, send_sem=send_sem, recv_sem=recv_sem, device_id=device, device_id_type=MESH
        )
        copy.start()
        return copy

    def arrived(ref, recv_sem, send_sem):
        pltpu.make_async_remote_copy(
            src_ref=ref, dst_ref=ref, send_sem=send_sem, recv_sem=recv_sem, device_id=X, device_id_type=MESH
        ).wait_recv()

    def gather_steps(src, out, rows, cut, sems):
        zr, x0, y1, y0, x1, cr, sd = sems
        first = (0, cut) if cut else (0, rows)
        second = (cut, rows - cut) if cut else None
        full = (0, rows)

        def piece(d, m, span):
            return out.at[m, pl.ds(pl.multiple_of(d * rows + span[0], 16), span[1])]

        def send(src_ref, dst_ref, sem, device):
            remote(src_ref, dst_ref, sd.at[0], sem, device)

        def got(ref, sem):
            arrived(ref, sem, sd.at[0])

        def step0():
            for j in range(1, 4):
                send(src, piece(dp, mp, full), zr.at[j], Z[j])
            send(src.at[pl.ds(*first)], piece(dp, mp, first), x0.at[0], X)
            if second:
                send(src.at[pl.ds(*second)], piece(dp, mp, second), y1.at[0], Y)
            send(src.at[pl.ds(*first)], piece(dp, mp, first), y0.at[0], Y)
            if second:
                send(src.at[pl.ds(*second)], piece(dp, mp, second), x1.at[0], X)
            send(src, piece(dp, mp, full), cr.at[0], C)
            pltpu.make_async_copy(src, piece(dp, mp, full), sd.at[0]).start()
            yield

        def step1():
            for j in range(1, 4):
                d = 2 * zs[j] + x
                block = piece(d, mp, full)
                got(block, zr.at[j])
                one = piece(d, mp, first)
                send(one, one, x0.at[j], X)
                if second:
                    two = piece(d, mp, second)
                    send(two, two, y1.at[j], Y)
                send(one, one, y0.at[j], Y)
                if second:
                    send(two, two, x1.at[j], X)
                send(block, block, cr.at[0], C)
                yield

        def step2():
            for j in range(4):
                one = piece(2 * zs[j] + (1 - x), mp, first)
                got(one, x0.at[j])
                send(one, one, y0.at[4 + j], Y)
                send(one, one, cr.at[0], C)
                if second:
                    two = piece(2 * zs[j] + x, ym, second)
                    got(two, y1.at[j])
                    send(two, two, x1.at[4 + j], X)
                    send(two, two, cr.at[0], C)
                yield

        def step3():
            for i in range(2):
                for j in range(4):
                    one = piece(2 * zs[j] + (x if i == 0 else 1 - x), ym, first)
                    got(one, y0.at[4 * i + j])
                    send(one, one, cr.at[0], C)
                    if second:
                        two = piece(2 * zs[j] + (1 - x), (mp if i == 0 else ym), second)
                        got(two, x1.at[4 * i + j])
                        send(two, two, cr.at[0], C)
                    yield

        def step4():
            half = out.at[pl.ds(0, 2)]
            pltpu.make_async_copy(half, half, cr.at[0]).wait()
            pltpu.make_async_copy(out, out, sd.at[0]).wait()
            yield

        return [step0, step1, step2, step3, step4]

    depth = packed.shape[1]
    slots = classes.shape[0]
    kinds = {
        "S": gather_steps(small, smalls, 16, 0, gsems[0:7]),
        "A": gather_steps(packed.at[0], w_attn, depth, CUT, gsems[7:14]),
        "U": gather_steps(packed.at[1], w_up, depth, CUT, gsems[14:21]),
        "D": gather_steps(packed.at[2], w_down, depth, CUT, gsems[21:28]),
        "I": gather_steps(image_own, images, slots, slots // 2, gsems[28:35]),
    }

    def run(*steps):
        for name in steps:
            for _ in kinds[name[0]][int(name[1])]():
                pass

    def blend(steps, chunks):
        chunks = list(chunks)
        micro = [kinds[name[0]][int(name[1])] for name in steps]
        count = sum((1, 3, 4, 8, 1)[int(name[1])] for name in steps)
        done, at = 0, 0
        for step in micro:
            for _ in step():
                at += 1
                while done < len(chunks) and done * count < at * len(chunks):
                    chunks[done]()
                    done += 1
        for chunk in chunks[done:]:
            chunk()

    lane = lax.broadcasted_iota(jnp.int32, (128, 128), 1)
    sub = lax.broadcasted_iota(jnp.int32, (128, 128), 0)
    low = lax.broadcasted_iota(jnp.int32, (1, 128), 1) < 64
    token_rows = x_ref.shape[0]
    tiles = token_rows // 128
    end_count = h_ends.shape[0]

    def keep_low(values):
        return jnp.where(low, values, jnp.zeros_like(values))

    def keep_high(values):
        return jnp.where(low, jnp.zeros_like(values), values)

    def masks():
        slot_row = lax.broadcasted_iota(jnp.int32, (end_count, 128), 0)
        parts, spots = [], []
        best = jnp.full((end_count, 1), -1, jnp.int32)
        for b in range(tiles):
            caption = 2 * (8 * b + lax.shift_right_logical(lax.broadcasted_iota(jnp.int32, (1, 128), 1), 4)) + ids[mp, pl.ds(b, 1), :]
            column = jnp.sum(jnp.where(lane == sub, caption, 0), axis=1, keepdims=True)
            mask_ref[b] = jnp.where((column == caption) & (sub >= lane), 0.0, -1e30)
            member = slot_row == caption
            spot = lax.broadcasted_iota(jnp.int32, (end_count, 128), 1) + 128 * b
            best = jnp.maximum(best, jnp.max(jnp.where(member, spot, -1), axis=1, keepdims=True))
            member_ref[:, 128 * b : 128 * (b + 1)] = jnp.where(member, 0.0, -1e30)
            spots.append(spot)
        for b in range(tiles):
            place_ref[:, 128 * b : 128 * (b + 1)] = (spots[b] == best).astype(f32).astype(bf16)

    def image_tower():
        hat, _ = standardise(classes[...].astype(f32))
        raw = nn((hat * image_gain[...] + image_bias[...]).astype(bf16), image_proj[...])
        image_own[...] = (raw * inverse_norm(raw)).astype(bf16)

    def small_vectors():
        halves = []
        for w in range(2):
            halves.append(sum(smalls[0, 64 * w + 16 * d : 64 * w + 16 * (d + 1), :].astype(f32) for d in range(4)))
        for v in range(4):
            for w in range(2):
                for t in range(3):
                    at = 384 * w + 128 * t
                    vecs[v : v + 1, at : at + 128] = halves[w][3 * v + t : 3 * v + t + 1, :]
        for m in range(4):
            for pair in range(4):
                both = sum(smalls[m, 32 * pair + 16 * d : 32 * pair + 16 * (d + 1), :].astype(f32) for d in range(2))
                valid_ref[m : m + 1, 128 * pair : 128 * (pair + 1)] = both[12:13, :]

    def first_norm():
        def body(b):
            rows = rows_of(b, 128)
            values = x_ref[rows, :].astype(f32)
            hat, _ = standardise(values)
            a_ref[rows, :] = (hat * vecs[0:1, :] + vecs[1:2, :]).astype(bf16)
            hidden[rows, :] = values

        loop(tiles, body)

    def soft(scores):
        top = jnp.max(scores, axis=-1, keepdims=True)
        raised = jnp.exp(scores - top)
        return raised * (1.0 / jnp.sum(raised, axis=-1, keepdims=True))

    scale = HEAD_DIM**-0.5

    def attention(m):
        def body(b):
            rows = rows_of(b, 128)
            made = nn(a_ref[rows, :], w_attn[m]).astype(bf16)
            q01, k01, v01, qv, ko = (made[:, 128 * i : 128 * (i + 1)] for i in range(5))
            mask = mask_ref[b]
            p0 = soft(nt(keep_low(q01), k01) * scale + mask).astype(bf16)
            p1 = soft(nt(keep_high(q01), k01) * scale + mask).astype(bf16)
            p2 = soft(nt(keep_low(qv), ko) * scale + mask).astype(bf16)
            o01 = jnp.where(low, nn(p0, v01), nn(p1, v01)).astype(bf16)
            o2 = keep_high(nn(p2, qv)).astype(bf16)
            qkv[m, rows, 0:512] = made[:, 0:512]
            qkv[m, rows, 512:640] = keep_low(ko) + o2
            qkv[m, rows, 640:768] = o01
            hidden[rows, :] += nt(o2, w_attn[m, :, 512:640]) + nt(o01, w_attn[m, :, 640:768])

        loop(tiles, body)

    def second_norm():
        def body(b):
            rows = rows_of(b, 128)
            hat, _ = standardise(hidden[rows, :])
            a_two[rows, :] = (hat * vecs[2:3, :] + vecs[3:4, :]).astype(bf16)

        loop(tiles, body)
        place = place_ref[...]
        ends = pick(place, hidden[...])
        h_ends[...] = ends
        hat, _ = standardise(ends)
        ends_two[mp] = (hat * vecs[2:3, :] + vecs[3:4, :]).astype(bf16)

    def ends_up(m):
        u_ends[m] = nn(ends_two[mp], w_up[m])

    def full_up(m):
        def body(b):
            rows = rows_of(b, 128)
            upper = nn(a_two[rows, :], w_up[m])
            active[m, rows, :] = (upper * half_erf(upper)).astype(bf16)

        loop(tiles, body)

    def slope_of(upper):
        return half_erf(upper) + upper * jnp.exp(-0.5 * upper * upper) * (1.0 / (2.0 * jnp.pi) ** 0.5)

    def group_up():
        def body(i):
            upper = nn(ends_two[i], w_up[mp])
            rows = rows_of(i, end_count)
            g_all[rows, :] = (upper * half_erf(upper)).astype(bf16)
            s_all[rows, :] = slope_of(upper)

        loop(4, body)

    def full_down(b):
        rows = slice(128 * b, 128 * (b + 1))
        hidden_down = hidden[rows, :]

        def body(m, total):
            return total + nt(active[m, rows, :], w_down[m])

        stage_out[rows, :] = lax.fori_loop(0, 4, body, hidden_down).astype(bf16)

    own_tokens = pltpu.make_async_copy(tokens.at[rows_of(mp, token_rows)], x_ref, s_local.at[0])
    own_tokens.start()
    run("S0", "A0", "U0")
    image_tower()
    masks()
    run("S1", "A1", "D0", "I0", "S2", "A2", "U1", "S3", "S4")
    own_tokens.wait()
    small_vectors()
    first_norm()
    run("D1", "A3", "A4")
    blend(("U2", "I1", "D2", "U3", "I2"), [functools.partial(attention, m) for m in range(4)])
    second_norm()
    swaps = [remote(ends_two.at[mp], ends_two.at[mp], s_exs.at[j - 1], s_a2.at[j - 1], G[j]) for j in range(1, 4)]
    run("U4")
    blend(("D3", "I3"), [functools.partial(full_up, m) for m in range(4)])
    loop(4, ends_up)
    for swap in swaps:
        swap.wait()
    group_up()
    run("D4", "I4")

    pooled = h_ends[...]
    for m in range(4):
        upper = u_ends[m]
        pooled = pooled + nt((upper * half_erf(upper)).astype(bf16), w_down[m])
    scale_back = inverse_norm(pooled)
    text = (pooled * scale_back).astype(bf16)
    own_valid = small[12:13, :].astype(f32)
    own_valid = jnp.max(
        jnp.where(
            lax.rem(lax.broadcasted_iota(jnp.int32, (slots, 128), 1), slots)
            == lax.broadcasted_iota(jnp.int32, (slots, 128), 0),
            own_valid,
            0.0,
        ),
        axis=1,
        keepdims=True,
    )
    live = own_valid > 0.0
    place_col = lax.broadcasted_iota(jnp.int32, (slots, 512), 1)
    place_row = lax.broadcasted_iota(jnp.int32, (slots, 512), 0)

    def target_of(m):
        return (place_col == place_row + dp * slots) & (mp == m)

    row_sum = jnp.zeros((slots, 1), f32)
    matched = jnp.zeros((slots, 1), f32)
    for m in range(4):
        logits = logit_scale * nt(text, images[m])
        weight = jnp.exp(logits)
        matched = matched + jnp.sum(jnp.where(target_of(m), logits, 0.0), axis=1, keepdims=True)
        seen = jnp.where(valid_ref[m : m + 1, :] > 0.0, weight, 0.0)
        weight_ref[m] = seen
        row_sum = row_sum + jnp.sum(seen, axis=1, keepdims=True)
        columns = jnp.sum(jnp.where(live, weight, 0.0), axis=0, keepdims=True)
        for part in range(4):
            sum_own[4 * m + part : 4 * m + part + 1, :] = columns[:, 128 * part : 128 * (part + 1)]
    row_part = jnp.sum(jnp.where(live, jnp.log(row_sum) - 2.0 * matched, 0.0), axis=0, keepdims=True)
    sum_own[16:24, :] = jnp.broadcast_to(row_part, (8, 128))

    swap = remote(sum_own, sum_got.at[0], s_sums.at[0], s_sum.at[0], C)
    full_down(0)
    swap.wait()
    sum_buf[0] = sum_own[...] + sum_got[0]
    swaps = [remote(sum_buf.at[0], sum_got.at[1 + xy], s_sums.at[j], s_sum.at[j], Q[j - 1]) for j in range(1, 4)]
    sum_got[1 + xy] = sum_buf[0]
    full_down(1)
    for swap in swaps:
        swap.wait()
    sum_buf[1] = (sum_got[1] + sum_got[2]) + (sum_got[3] + sum_got[4])
    swaps = [remote(sum_buf.at[1], sum_got.at[5 + z], s_sums.at[3 + j], s_sum.at[3 + j], Z[j]) for j in range(1, 4)]
    sum_got[5 + z] = sum_buf[1]
    full_down(2)
    for swap in swaps:
        swap.wait()
    sums = (sum_got[5] + sum_got[6]) + (sum_got[7] + sum_got[8])

    total = sums[16:17, 0:1]
    unit_grad = jnp.zeros((slots, text.shape[1]), f32)
    for m in range(4):
        columns = jnp.concatenate([sums[4 * m + part : 4 * m + part + 1, :] for part in range(4)], axis=1)
        seen = valid_ref[m : m + 1, :] > 0.0
        total = total + jnp.sum(jnp.where(seen, jnp.log(columns), 0.0), axis=1, keepdims=True)
        spread = 0.5 * weight_ref[m] * (1.0 / row_sum + 1.0 / columns)
        grad = jnp.where(seen & live, spread, 0.0) - jnp.where(target_of(m) & live, 1.0, 0.0)
        unit_grad = unit_grad + nn((logit_scale * grad).astype(bf16), images[m])
    loss_out[...] = jnp.broadcast_to(total * (0.5 / slot_total), (8, 128))
    along = jnp.sum(unit_grad * pooled, axis=-1, keepdims=True)
    pooled_grad = scale_back * unit_grad - pooled * (scale_back * scale_back * scale_back * along)
    branch_grad = pooled_grad.astype(bf16)
    ends_grad[mp] = branch_grad
    swaps = [remote(ends_grad.at[mp], ends_grad.at[mp], s_exs.at[2 + j], s_dm.at[j - 1], G[j]) for j in range(1, 4)]

    full_down(3)
    own_rows = rows_of(mp, token_rows)
    far_rows = rows_of(ym, token_rows)
    out_swaps = [
        remote(stage_out, block_out.at[own_rows], s_bo.at[0], s_bo.at[1], Y),
        remote(stage_out, block_out.at[own_rows], s_bo.at[2], s_bo.at[3], C),
    ]
    keep_out = pltpu.make_async_copy(stage_out, block_out.at[own_rows], s_local.at[1])
    keep_out.start()

    two_grad = jnp.zeros_like(pooled)
    for m in range(4):
        upper_grad = (nn(branch_grad, w_down[m]) * slope_of(u_ends[m])).astype(bf16)
        two_grad = two_grad + nt(upper_grad, w_up[m])
    hat_two, rstd_two = standardise(h_ends[...])
    vec_buf[0] = jnp.zeros_like(vec_buf[0])
    vec_buf[0, 2:3, :] = jnp.sum(two_grad * hat_two, axis=0, keepdims=True)
    vec_buf[0, 3:4, :] = jnp.sum(two_grad, axis=0, keepdims=True)
    hidden_grad = pooled_grad + norm_pull(two_grad, hat_two, rstd_two, vecs[2:3, :])
    attended_grad = hidden_grad.astype(bf16)
    h_ends[...] = hidden_grad

    for swap in swaps:
        swap.wait()
    group_grad = ends_grad[...].reshape(4 * end_count, -1)
    upper_grad = (nn(group_grad, w_down[mp]) * s_all[...]).astype(bf16)
    s_all_grad = upper_grad
    grad_down[...] = tn(group_grad, g_all[...]).astype(bf16)

    def block(z_, x_):
        return pl.ds(pl.multiple_of((2 * z_ + x_) * depth, 16), depth)

    ffn = [grad_down, grad_up]

    def ffn_start(k):
        for j in (2, 1, 3, 0):
            remote(ffn[k].at[block(zt[j], 1 - x)], ffn_one.at[k, j], s_send.at[k], s_f1.at[k, j], X)

    def ffn_add(k, out):
        for j in (2, 1, 3, 0):
            arrived(ffn_one.at[k, j], s_f1.at[k, j], s_send.at[k])
            mine = block(zt[j], x)
            summed = ffn[k][mine, :].astype(f32) + ffn_one[k, j].astype(f32)
            if j:
                ffn[k][mine, :] = summed.astype(bf16)
                remote(ffn[k].at[mine], ffn_three.at[k, j - 1], s_send.at[k], s_f3.at[k, j - 1], Z[j])
            else:
                out[...] = summed

    def ffn_end(k, out):
        for j in range(1, 4):
            arrived(ffn_three.at[k, j - 1], s_f3.at[k, j - 1], s_send.at[k])
        out[...] = out[...] + ffn_three[k, 0].astype(f32) + ffn_three[k, 1].astype(f32) + ffn_three[k, 2].astype(f32)
        sent = ffn[k].at[pl.ds(0, 7 * depth)]
        pltpu.make_async_copy(sent, sent, s_send.at[k]).wait()

    ffn_start(0)
    grad_up[...] = tn(ends_two[...].reshape(4 * end_count, -1), s_all_grad).astype(bf16)
    ffn_start(1)

    d_attn[...] = jnp.zeros_like(d_attn)

    def attention_back(m):
        place = place_ref[...]
        member = member_ref[...]
        k01, v01, qv, ko = (qkv[m, :, 128 * i : 128 * (i + 1)] for i in range(1, 5))
        q_e = nn(place, qkv[m, :, 0:128]).astype(bf16)
        q2_e = keep_low(nn(place, qv)).astype(bf16)
        do01 = nn(attended_grad, w_attn[m, :, 640:768]).astype(bf16)
        do2 = keep_high(nn(attended_grad, w_attn[m, :, 512:640])).astype(bf16)

        def head(query, keys, values, outer):
            probs = soft(nt(query, keys) * scale + member)
            probs_grad = nt(outer, values)
            centre = jnp.sum(probs_grad * probs, axis=-1, keepdims=True)
            return probs.astype(bf16), (probs * (probs_grad - centre)).astype(bf16)

        p0, ds0 = head(keep_low(q_e), k01, v01, keep_low(do01))
        p1, ds1 = head(keep_high(q_e), k01, v01, keep_high(do01))
        p2, ds2 = head(q2_e, ko, qv, do2)
        dq01 = (jnp.where(low, nn(ds0, k01), nn(ds1, k01)) * scale).astype(bf16)
        dq2 = keep_low(nn(ds2, ko) * scale).astype(bf16)
        d_qkv[m, :, 0:128] = tn(place, dq01).astype(bf16)
        d_qkv[m, :, 128:256] = (jnp.where(low, tn(ds0, q_e), tn(ds1, q_e)) * scale).astype(bf16)
        d_qkv[m, :, 256:384] = jnp.where(low, tn(p0, do01), tn(p1, do01)).astype(bf16)
        d_qkv[m, :, 384:512] = jnp.where(low, tn(place, dq2), tn(p2, do2)).astype(bf16)
        d_qkv[m, :, 512:640] = keep_low(tn(ds2, q2_e) * scale).astype(bf16)

    def token_back(m):
        def body(b):
            rows = rows_of(b, 128)
            d_attn[rows, :] += nt(d_qkv[m, rows, 0:640], w_attn[m, :, 0:640])

        loop(tiles, body)

    for m in range(4):
        attention_back(m)
        token_back(m)
        if m == 1:
            ffn_add(0, down_out)
    ffn_add(1, up_out)

    vec_buf[0, 0:2, :] = jnp.zeros((2, vec_buf.shape[2]), f32)

    def token_end(b):
        rows = rows_of(b, 128)
        hat, rstd = standardise(x_ref[rows, :].astype(f32))
        grad = d_attn[rows, :]
        vec_buf[0, 0:1, :] += jnp.sum(grad * hat, axis=0, keepdims=True)
        vec_buf[0, 1:2, :] += jnp.sum(grad, axis=0, keepdims=True)
        d_attn[rows, :] = norm_pull(grad, hat, rstd, vecs[0:1, :])

    loop(tiles, token_end)
    stage_grad[...] = (d_attn[...] + spread_rows(place_ref[...], h_ends[...])).astype(bf16)
    grad_swaps = [
        remote(stage_grad, token_out.at[own_rows], s_tg.at[0], s_tg.at[1], Y),
        remote(stage_grad, token_out.at[own_rows], s_tg.at[2], s_tg.at[3], C),
    ]
    keep_grad = pltpu.make_async_copy(stage_grad, token_out.at[own_rows], s_local.at[2])
    keep_grad.start()

    def attn_grad(m):
        made = tn(a_ref[...], d_qkv[m, :, 0:640])
        o_e = nn(place_ref[...], qkv[m, :, 512:768]).astype(bf16)
        outer = tn(attended_grad, o_e)
        last = jnp.where(low, made[:, 512:640], outer[:, 0:128])
        return jnp.concatenate([made[:, 0:512], last, outer[:, 128:256]], axis=1)

    def pair_y(d):
        return y if d == 0 else 1 - y

    def pair_x(d):
        return x if d == 0 else 1 - x

    first, second = pl.ds(0, LATE), pl.ds(LATE, depth - LATE)

    def half_rows(d):
        return d * 8 * depth

    def part(d, z_, x_, span):
        start = half_rows(d) + (2 * z_ + x_) * depth + span.start
        return attn_acc.at[pl.ds(pl.multiple_of(start, 16), span.size)]

    whole = pl.ds(0, depth)
    core_swaps = []
    for d in (1, 0):
        attn_send[d] = attn_grad(2 * pair_y(d) + (1 - c)).astype(bf16)
        core_swaps.append(remote(attn_send.at[d], attn_core.at[d], s_exs.at[6 + d], s_core.at[d], C))
    vec_swaps = [remote(vec_buf.at[0], vec_got.at[0], s_vs.at[0], s_v.at[0], C)]
    for i, d in enumerate((1, 0)):
        made = attn_grad(2 * pair_y(d) + c)
        core_swaps[i].wait()
        attn_acc[half_rows(d) : half_rows(d + 1), :] = (made + attn_core[d].astype(f32)).astype(bf16)
        for j in range(4):
            remote(part(d, zt[j], 1 - x, second), one_q.at[4 * d + j], s_send.at[2], s_1q.at[4 * d + j], X)
        if d:
            for e in (1, 0):
                for j in range(4):
                    remote(part(1, zt[j], pair_x(e), first), one_p.at[4 * e + j], s_send.at[2], s_1p.at[4 * e + j], Y)
            ffn_end(0, down_out)
            vec_swaps[0].wait()
            vec_buf[1] = vec_buf[0] + vec_got[0]
            vec_swaps.append(remote(vec_buf.at[1], vec_got.at[1], s_vs.at[1], s_v.at[1], Y))

    def add(ref, got):
        ref[...] = (ref[...].astype(f32) + got.astype(f32)).astype(bf16)

    ffn_end(1, up_out)
    vec_swaps[1].wait()
    vec_buf[2] = vec_buf[1] + vec_got[1]
    vec_swaps.append(remote(vec_buf.at[2], vec_got.at[2], s_vs.at[2], s_v.at[2], X))
    for e in (1, 0):
        for j in range(4):
            i = 4 * e + j
            arrived(one_p.at[i], s_1p.at[i], s_send.at[2])
            spot = part(0, zt[j], pair_x(e), first)
            add(spot, one_p[i])
            if e:
                remote(spot, two_p.at[j], s_send.at[2], s_2p.at[j], X)
            arrived(one_q.at[i], s_1q.at[i], s_send.at[2])
            spot = part(e, zt[j], x, second)
            add(spot, one_q[i])
            if e:
                remote(spot, two_q.at[j], s_send.at[2], s_2q.at[j], Y)
    vec_swaps[2].wait()
    vec_buf[3] = vec_buf[2] + vec_got[2]
    for j in range(1, 4):
        vec_swaps.append(remote(vec_buf.at[3], vec_got.at[3 + z], s_vs.at[2 + j], s_v.at[2 + j], Z[j]))
    vec_got[3 + z] = vec_buf[3]
    for j in (2, 1, 3, 0):
        arrived(two_p.at[j], s_2p.at[j], s_send.at[2])
        add(part(0, zt[j], x, first), two_p[j])
        arrived(two_q.at[j], s_2q.at[j], s_send.at[2])
        add(part(0, zt[j], x, second), two_q[j])
        spot = part(0, zt[j], x, whole)
        if j:
            remote(spot, three_a.at[j - 1], s_send.at[2], s_3.at[j - 1], Z[j])
        else:
            attn_out[...] = spot[...].astype(f32)
    out_swaps[0].wait()
    on = remote(block_out.at[far_rows], block_out.at[far_rows], s_boc.at[0], s_boc.at[1], C)
    grad_swaps[0].wait()
    on_grad = remote(token_out.at[far_rows], token_out.at[far_rows], s_boc.at[2], s_boc.at[3], C)
    for j in range(1, 4):
        arrived(three_a.at[j - 1], s_3.at[j - 1], s_send.at[2])
    attn_out[...] = attn_out[...] + three_a[0].astype(f32) + three_a[1].astype(f32) + three_a[2].astype(f32)
    for swap in vec_swaps[3:]:
        swap.wait()
    vec_out[...] = (vec_got[3] + vec_got[4]) + (vec_got[5] + vec_got[6])
    sent = attn_acc.at[pl.ds(0, 15 * depth)]
    pltpu.make_async_copy(sent, sent, s_send.at[2]).wait()
    out_swaps[1].wait()
    grad_swaps[1].wait()
    on.wait()
    on_grad.wait()
    keep_out.wait()
    keep_grad.wait()


def layer(slot_total, packed, small, classes, image_gain, image_bias, image_proj, tokens, ids):
    width, depth, slots = packed.shape[2], packed.shape[1], classes.shape[0]
    rows = tokens.shape[0] // 4

    def gather_sems():
        return [DMA((4,)), DMA((4,)), DMA((4,)), DMA((8,)), DMA((8,)), DMA((1,)), DMA((1,))]

    here, there = pl.BlockSpec(memory_space=VMEM), pl.BlockSpec(memory_space=pltpu.HBM)
    square = VMEM((4, width, width), bf16)
    scratch = [
        square,
        square,
        square,
        VMEM((4, 8 * slots, width), bf16),
        VMEM((4, 128, 128), bf16),
        VMEM((rows, width), bf16),
        VMEM((rows, width), bf16),
        VMEM((4, rows, width), bf16),
        VMEM((rows, width), f32),
        VMEM((rows, width), bf16),
        VMEM((4, rows, width), bf16),
        VMEM((rows, width), bf16),
        VMEM((slots, width), bf16),
        VMEM((8, width), f32),
        VMEM((rows // 128, 128, 128), f32),
        VMEM((slots, rows), bf16),
        VMEM((slots, rows), f32),
        VMEM((slots, width), f32),
        VMEM((4, slots, width), bf16),
        VMEM((4, slots, width), bf16),
        VMEM((4, slots, width), f32),
        VMEM((4 * slots, width), bf16),
        VMEM((4 * slots, width), f32),
        VMEM((4, slots, 8 * slots), f32),
        VMEM((8, 8 * slots), f32),
        VMEM((24, 128), f32),
        VMEM((2, 24, 128), f32),
        VMEM((9, 24, 128), f32),
        VMEM((rows, width), f32),
        VMEM((4, rows, 640), bf16),
        VMEM((width, width), bf16),
        VMEM((width, width), bf16),
        VMEM((2, 4, depth, width), bf16),
        VMEM((2, 3, depth, width), bf16),
        VMEM((2, width, width), bf16),
        VMEM((2 * width, width), bf16),
        VMEM((2, width, width), bf16),
        VMEM((8, LATE, width), bf16),
        VMEM((8, depth - LATE, width), bf16),
        VMEM((4, LATE, width), bf16),
        VMEM((4, depth - LATE, width), bf16),
        VMEM((3, depth, width), bf16),
        VMEM((4, 8, width), f32),
        VMEM((7, 8, width), f32),
        VMEM((rows, width), bf16),
        VMEM((8, 128), f32),
    ]
    for _ in range(5):
        scratch += gather_sems()
    scratch += [
        DMA((3,)),
        DMA((4,)),
        DMA((4,)),
        DMA((3,)),
        DMA((3,)),
        DMA((3,)),
        DMA((7,)),
        DMA((7,)),
        DMA((2, 4)),
        DMA((2, 3)),
        DMA((2,)),
        DMA((8,)),
        DMA((8,)),
        DMA((4,)),
        DMA((4,)),
        DMA((3,)),
        DMA((6,)),
        DMA((6,)),
        DMA((4,)),
        DMA((8,)),
    ]
    return pl.pallas_call(
        functools.partial(layer_kernel, slot_total),
        out_shape=[
            jax.ShapeDtypeStruct((8, 128), f32),
            jax.ShapeDtypeStruct((4 * rows, width), bf16),
            jax.ShapeDtypeStruct((4 * rows, width), bf16),
            jax.ShapeDtypeStruct((depth, width), f32),
            jax.ShapeDtypeStruct((depth, width), f32),
            jax.ShapeDtypeStruct((depth, width), f32),
            jax.ShapeDtypeStruct((8, width), f32),
        ],
        in_specs=[here] * 6 + [there, here],
        out_specs=[here, there, there, here, here, here, here],
        scratch_shapes=scratch,
        compiler_params=pltpu.CompilerParams(
            collective_id=1, has_side_effects=True, vmem_limit_bytes=63 * 2**20
        ),
        cost_estimate=pl.CostEstimate(flops=30 * 10**9, bytes_accessed=40 * 10**6, transcendentals=10**7),
        name="layer",
    )(packed, small, classes, image_gain, image_bias, image_proj, tokens, ids)


def on_kernel(
    tokens,
    segment_ids,
    slot_valid,
    ln1_gain,
    ln1_bias,
    w_qkv,
    w_out,
    ln2_gain,
    ln2_bias,
    w_up,
    w_down,
    class_tokens,
    image_gain,
    image_bias,
    image_proj,
):
    dp_rank = lax.axis_index("dp")
    depth, slots = w_up.shape[0], slot_valid.shape[0]
    out_t = w_out.T
    query, key, value = w_qkv[0], w_qkv[1], w_qkv[2]
    attn = jnp.concatenate(
        [
            query[:, :128],
            key[:, :128],
            value[:, :128],
            query[:, 128:],
            value[:, 128:],
            key[:, 128:],
            out_t[:, 128:],
            out_t[:, :128],
        ],
        axis=1,
    )
    packed = jnp.stack([attn, w_up, w_down.T])
    norms = jnp.stack([ln1_gain, ln1_bias, ln2_gain, ln2_bias])
    norms = jnp.where(
        (jnp.arange(4) == lax.rem(dp_rank, 4))[None, :, None], norms[:, None, :], jnp.zeros((), bf16)
    ).reshape(12, 128)
    valid = jnp.where(
        (jnp.arange(2) == lax.rem(dp_rank, 2))[:, None], slot_valid.astype(bf16)[None, :], jnp.zeros((), bf16)
    ).reshape(1, 128)
    small = jnp.concatenate([norms, valid, jnp.zeros((3, 128), bf16)], axis=0)
    loss, block_out, token_grad, own_attn, own_up, own_down, vectors = layer(
        slots * 32,
        packed,
        small,
        class_tokens,
        image_gain[None],
        image_bias[None],
        image_proj,
        tokens,
        segment_ids.reshape(4, 4, 128),
    )
    pick_cols = lambda *spans: jnp.concatenate([own_attn[:, a:b] for a, b in spans], axis=1)
    qkv_grad = jnp.stack(
        [pick_cols((0, 128), (384, 448)), pick_cols((128, 256), (512, 576)), pick_cols((256, 384), (448, 512))]
    )
    out_grad = pick_cols((640, 768), (576, 640)).T
    vectors = lax.dynamic_slice_in_dim(vectors, dp_rank * depth, depth, 1)
    return (
        loss[0, 0],
        block_out,
        token_grad.astype(f32),
        vectors[0],
        vectors[1],
        qkv_grad,
        out_grad,
        vectors[2],
        vectors[3],
        own_up,
        own_down.T,
    )


def make(dp_size, mp_size):
    def on_device(
        tokens,
        segment_ids,
        slot_valid,
        ln1_gain,
        ln1_bias,
        w_qkv,
        w_out,
        ln2_gain,
        ln2_bias,
        w_up,
        w_down,
        class_tokens,
        image_gain,
        image_bias,
        image_proj,
    ):
        both = ("dp", "mp")
        dp_rank, mp_rank = lax.axis_index("dp"), lax.axis_index("mp")
        depth = w_up.shape[0]
        width = depth * dp_size
        head_cols = w_out.shape[0]
        heads = head_cols // HEAD_DIM
        rows = tokens.shape[0] // mp_size
        seqs = rows // SEQ_LEN
        slots = slot_valid.shape[0]
        slot_total = slots * dp_size * mp_size

        packed = jnp.stack(
            [jnp.concatenate([w_qkv[0], w_qkv[1], w_qkv[2], w_out.T], axis=1), w_up, w_down.T]
        )
        norms = jnp.stack([ln1_gain, ln1_bias, ln2_gain, ln2_bias])
        image_hat, _ = standardise(class_tokens.astype(f32))
        image_normed = (image_hat * image_gain + image_bias).astype(bf16)
        image_raw = nn(image_normed, image_proj)
        image_unit = (image_raw * inverse_norm(image_raw)).astype(bf16)

        weights = lax.all_gather(packed, both, axis=0).reshape(dp_size, mp_size, 3, depth, -1)
        weights = weights.transpose(2, 1, 0, 3, 4).reshape(3, mp_size, width, -1)
        vectors = lax.all_gather(norms, "dp", axis=1, tiled=True).astype(f32)
        all_image = lax.all_gather(image_unit, both, axis=0, tiled=True)
        all_valid = lax.all_gather(slot_valid.astype(bf16), both, axis=0, tiled=True) > 0

        own = lax.dynamic_slice_in_dim(tokens, mp_rank * rows, rows, 0).astype(f32)
        ids = lax.dynamic_slice_in_dim(segment_ids, mp_rank * rows, rows, 0)
        grid_ids = ids.reshape(seqs, SEQ_LEN)
        first_len = jnp.sum((grid_ids == 0).astype(jnp.int32), axis=1)
        starts = jnp.arange(seqs, dtype=jnp.int32) * SEQ_LEN
        ends = jnp.stack([starts + first_len - 1, starts + SEQ_LEN - 1], axis=1).reshape(2 * seqs)
        place = (ends[:, None] == jnp.arange(rows)[None, :]).astype(bf16)

        hat_one, rstd_one = standardise(own)
        normed = (hat_one * vectors[0] + vectors[1]).astype(bf16)
        attn = weights[0]
        qkv = jnp.einsum("rd,mde->mre", normed, attn[:, :, : 3 * head_cols], preferred_element_type=f32)
        qkv = qkv.astype(bf16).reshape(mp_size, rows, 3, heads, HEAD_DIM)
        blocks = rows // tile_rows
        split = qkv.reshape(mp_size, blocks, tile_rows, 3, heads, HEAD_DIM)
        query, key, value = split[:, :, :, 0], split[:, :, :, 1], split[:, :, :, 2]
        tile_ids = ids.reshape(blocks, tile_rows)
        spots = jnp.arange(tile_rows)
        allowed = (
            (tile_ids[:, :, None] == tile_ids[:, None, :])
            & (spots[:, None] // SEQ_LEN == spots[None, :] // SEQ_LEN)[None]
            & (spots[:, None] >= spots[None, :])[None]
        )[None, :, None]
        scale = HEAD_DIM**-0.5
        scores = jnp.einsum("mbqhc,mbkhc->mbhqk", query, key, preferred_element_type=f32) * scale
        scores = jnp.where(allowed, scores, -1e30)
        probs = jax.nn.softmax(scores, axis=-1)
        mixed = jnp.einsum("mbhqk,mbkhc->mbqhc", probs.astype(bf16), value, preferred_element_type=f32)
        mixed = mixed.astype(bf16).reshape(mp_size, rows, head_cols)
        out_t = attn[:, :, 3 * head_cols :]
        attended = jnp.einsum("mre,mde->rd", mixed, out_t, preferred_element_type=f32)
        hidden = own + attended

        def feed(rows_in):
            hat, rstd = standardise(rows_in)
            normed_two = (hat * vectors[2] + vectors[3]).astype(bf16)
            upper = jnp.einsum("rd,mdf->mrf", normed_two, weights[1], preferred_element_type=f32)
            active = (upper * phi(upper)).astype(bf16)
            branch = jnp.einsum("mrf,mdf->rd", active, weights[2], preferred_element_type=f32)
            return hat, rstd, normed_two, upper, active, rows_in + branch

        block_out = feed(hidden)[-1].astype(bf16)
        hidden_ends = hidden[ends]
        hat_two, rstd_two, normed_two, upper, active, pooled = feed(hidden_ends)

        scale_back = inverse_norm(pooled)
        text = (pooled * scale_back).astype(bf16)
        logits = logit_scale * nt(text, all_image)
        live = slot_valid > 0
        weight = jnp.exp(logits)
        row_sum = jnp.sum(jnp.where(all_valid[None, :], weight, 0.0), axis=1)
        col_part = jnp.sum(jnp.where(live[:, None], weight, 0.0), axis=0)
        row_index = (dp_rank * mp_size + mp_rank) * slots + jnp.arange(slots)
        target = jnp.arange(slot_total)[None, :] == row_index[:, None]
        matched = jnp.sum(jnp.where(target, logits, 0.0), axis=1)
        row_part = jnp.sum(jnp.where(live, jnp.log(row_sum) - 2.0 * matched, 0.0))
        sums = lax.psum(jnp.concatenate([col_part, row_part[None]]), both)
        col_sum = sums[:slot_total]
        loss = 0.5 * (sums[slot_total] + jnp.sum(jnp.where(all_valid, jnp.log(col_sum), 0.0))) / slot_total
        pair = live[:, None] & all_valid[None, :]
        spread = 0.5 * weight * (1.0 / row_sum[:, None] + 1.0 / col_sum[None, :])
        grad_logits = jnp.where(pair, spread, 0.0) - (target & live[:, None]).astype(f32)
        cosine_grad = (logit_scale * grad_logits).astype(bf16)
        unit_grad = nn(cosine_grad, all_image)
        along = jnp.sum(unit_grad * pooled, axis=-1, keepdims=True)
        pooled_grad = scale_back * unit_grad - pooled * (scale_back * scale_back * scale_back * along)

        branch_grad = pooled_grad.astype(bf16)
        down_local = jnp.einsum("rd,mrf->mdf", branch_grad, active, preferred_element_type=f32)
        active_grad = jnp.einsum("rd,mdf->mrf", branch_grad, weights[2], preferred_element_type=f32)
        slope = phi(upper) + upper * jnp.exp(-0.5 * upper * upper) * (1.0 / (2.0 * jnp.pi) ** 0.5)
        upper_grad = (active_grad * slope).astype(bf16)
        up_local = jnp.einsum("rd,mrf->mdf", normed_two, upper_grad, preferred_element_type=f32)
        normed_two_grad = jnp.einsum("mrf,mdf->rd", upper_grad, weights[1], preferred_element_type=f32)
        gain_two = jnp.sum(normed_two_grad * hat_two, axis=0)
        bias_two = jnp.sum(normed_two_grad, axis=0)
        hidden_grad = pooled_grad + norm_pull(normed_two_grad, hat_two, rstd_two, vectors[2])

        attended_grad = hidden_grad.astype(bf16)
        mixed_ends = mixed[:, ends]
        out_local = jnp.einsum("rd,mre->mde", attended_grad, mixed_ends, preferred_element_type=f32)
        mixed_grad = jnp.einsum("rd,mde->mre", attended_grad, out_t, preferred_element_type=f32).astype(bf16)
        mixed_grad = mixed_grad.reshape(mp_size, 2 * seqs, heads, HEAD_DIM)
        query_ends, keys, values = qkv[:, ends, 0], qkv[:, :, 1], qkv[:, :, 2]
        spot = jnp.arange(rows)
        allowed_ends = (
            (ids[ends][:, None] == ids[None, :])
            & (ends[:, None] // SEQ_LEN == spot[None, :] // SEQ_LEN)
            & (ends[:, None] >= spot[None, :])
        )[None, None]
        again = jnp.einsum("mqhc,mkhc->mhqk", query_ends, keys, preferred_element_type=f32) * scale
        probs_ends = jax.nn.softmax(jnp.where(allowed_ends, again, -1e30), axis=-1)
        probs_grad = jnp.einsum("mqhc,mkhc->mhqk", mixed_grad, values, preferred_element_type=f32)
        value_grad = jnp.einsum("mhqk,mqhc->mkhc", probs_ends.astype(bf16), mixed_grad, preferred_element_type=f32)
        centre = jnp.sum(probs_grad * probs_ends, axis=-1, keepdims=True)
        score_grad = (probs_ends * (probs_grad - centre)).astype(bf16)
        query_grad = jnp.einsum("mhqk,mkhc->mqhc", score_grad, keys, preferred_element_type=f32) * scale
        key_grad = jnp.einsum("mhqk,mqhc->mkhc", score_grad, query_ends, preferred_element_type=f32) * scale
        query_grad = query_grad.astype(bf16).reshape(mp_size, 2 * seqs, head_cols)
        query_grad = jnp.einsum("er,mec->mrc", place, query_grad, preferred_element_type=f32).astype(bf16)
        proj_grad = jnp.concatenate(
            [
                query_grad,
                key_grad.astype(bf16).reshape(mp_size, rows, head_cols),
                value_grad.astype(bf16).reshape(mp_size, rows, head_cols),
            ],
            axis=-1,
        )
        qkv_local = jnp.einsum("rd,mre->mde", normed, proj_grad, preferred_element_type=f32)
        normed_grad = jnp.einsum("mre,mde->rd", proj_grad, attn[:, :, : 3 * head_cols], preferred_element_type=f32)
        gain_one = jnp.sum(normed_grad * hat_one, axis=0)
        bias_one = jnp.sum(normed_grad, axis=0)
        token_grad = norm_pull(normed_grad, hat_one, rstd_one, vectors[0])
        token_grad = token_grad.at[ends].add(hidden_grad)

        local = jnp.stack([jnp.concatenate([qkv_local, out_local], axis=-1), up_local, down_local])
        local = local.reshape(3, mp_size, dp_size, depth, -1).transpose(2, 1, 0, 3, 4)
        local = local.reshape(dp_size * mp_size, 3, depth, -1)
        summed = lax.psum_scatter(local, both, scatter_dimension=0, tiled=False)
        vector_local = lax.psum(jnp.stack([gain_one, bias_one, gain_two, bias_two]), both)
        vector_own = lax.dynamic_slice_in_dim(vector_local, dp_rank * depth, depth, 1)

        block_out = lax.all_gather(block_out, "mp", axis=0, tiled=True)
        token_grad = lax.all_gather(token_grad, "mp", axis=0, tiled=True)
        qkv_grad = summed[0, :, : 3 * head_cols].reshape(depth, 3, head_cols).transpose(1, 0, 2)
        return (
            loss,
            block_out,
            token_grad,
            vector_own[0],
            vector_own[1],
            qkv_grad,
            summed[0, :, 3 * head_cols :].T,
            vector_own[2],
            vector_own[3],
            summed[1],
            summed[2].T,
        )

    return on_device


def solution(mesh):
    placed = (
        P("dp", None),
        P("dp"),
        P(("dp", "mp")),
        P("dp"),
        P("dp"),
        P(None, "dp", "mp"),
        P("mp", "dp"),
        P("dp"),
        P("dp"),
        P("dp", "mp"),
        P("mp", "dp"),
        P(("dp", "mp"), None),
        P(),
        P(),
        P(),
    )
    sizes = (mesh.shape["dp"], mesh.shape["mp"])
    return jax.shard_map(
        on_kernel if sizes == (8, 4) else make(*sizes),
        mesh=mesh,
        in_specs=placed,
        out_specs=(
            P(),
            P("dp", None),
            P("dp", None),
            P("dp"),
            P("dp"),
            P(None, "dp", "mp"),
            P("mp", "dp"),
            P("dp"),
            P("dp"),
            P("dp", "mp"),
            P("mp", "dp"),
        ),
        check_vma=False,
    )
```

```python
import jax
import jax.numpy as jnp
from jax import lax
from jax.sharding import PartitionSpec as P
import functools
from jax.experimental import pallas as pl
from jax.experimental.pallas import tpu as pltpu

HEAD_DIM = 64
SEQ_LEN = 16
norm_epsilon = 1e-05
unit_epsilon = 1e-06
logit_scale = 50.0
tile_rows = 128
f32, bf16 = jnp.float32, jnp.bfloat16


def standardise(values):
    centred = values - jnp.mean(values, axis=-1, keepdims=True)
    rstd = lax.rsqrt(jnp.mean(centred * centred, axis=-1, keepdims=True) + norm_epsilon)
    return centred * rstd, rstd


def norm_pull(grad, hat, rstd, gain):
    scaled = grad * gain
    first = jnp.mean(scaled, axis=-1, keepdims=True)
    second = jnp.mean(scaled * hat, axis=-1, keepdims=True)
    return rstd * (scaled - first - hat * second)


def inverse_norm(values):
    return lax.rsqrt(jnp.sum(values * values, axis=-1, keepdims=True) + unit_epsilon)


def nn(left, right):
    return lax.dot_general(left, right, (((1,), (0,)), ((), ())), preferred_element_type=f32)


def nt(left, right):
    return lax.dot_general(left, right, (((1,), (1,)), ((), ())), preferred_element_type=f32)


def tn(left, right):
    return lax.dot_general(left, right, (((0,), (0,)), ((), ())), preferred_element_type=f32)


def phi(values):
    return 0.5 * lax.erfc(-values * (0.5**0.5))


MESH = pl.DeviceIdType.MESH
VMEM, DMA = pltpu.VMEM, pltpu.SemaphoreType.DMA
CUT = 48


def loop(count, body):
    lax.fori_loop(0, count, lambda i, carry: (body(i), carry)[1], 0)


def rows_of(index, size):
    return pl.ds(pl.multiple_of(index * size, size), size)


def split_three(values):
    first = values.astype(bf16)
    rest = values - first.astype(f32)
    second = rest.astype(bf16)
    return first, second, (rest - second.astype(f32)).astype(bf16)


def pick(place, values):
    return sum(nn(place, part) for part in split_three(values))


def spread_rows(place, values):
    return sum(tn(place, part) for part in split_three(values))


def half_erf(values):
    return 0.5 + 0.5 * lax.erf(values * (0.5**0.5))


def layer_kernel(slot_total, *refs):
    (w_qkv, w_out, up_own, down_own, norms, valid_own, classes, image_gain, image_bias, image_proj, tokens, ids) = refs[:12]
    (loss_out, block_out, token_out, attn_out, up_out, down_out, vec_out) = refs[12:19]
    (w_attn, w_up, w_down, images, smalls, x_ref, a_ref, qkv, hidden, a_two, active, stage_out, image_own, vecs) = refs[19:33]
    (mask_ref, place_ref, member_ref, h_ends, ends_two, ends_grad, u_ends, g_all, s_all, weight_ref, valid_ref) = refs[33:44]
    (sum_own, sum_buf, sum_got, d_attn, d_far) = refs[44:49]
    (grad_down, grad_up, grad_attn, step_x, step_z, attn_send, attn_core, ends_back) = refs[49:57]
    (vec_buf, vec_got, stage_grad, attn_own, small_own, far_mix) = refs[57:63]
    gsems = refs[63:91]
    isems = refs[91:100]
    (s_local, s_bo, s_on, s_send, s_a2, s_dm, s_dh, s_sum, s_sums, s_x, s_z, s_core, s_v, s_vs, s_tg, s_exs) = refs[100:116]

    dp = lax.axis_index("dp")
    mp = lax.axis_index("mp")
    z = lax.div(dp, 2)
    x = lax.rem(dp, 2)
    y = lax.div(mp, 2)
    c = lax.rem(mp, 2)
    xd, ym, cm = 2 * z + (1 - x), 2 * (1 - y) + c, 2 * y + (1 - c)
    zt = [lax.rem(z + j, 4) for j in range(4)]
    zs = [lax.rem(z + 4 - j, 4) for j in range(4)]
    X, Y, C, YC = (xd, mp), (dp, ym), (dp, cm), (dp, 3 - mp)
    Z = [(2 * zt[j] + x, mp) for j in range(4)]
    here = 4 * x + mp
    PLANE = []
    for j in range(1, 8):
        other = lax.rem(here + j, 8)
        PLANE.append((2 * z + lax.div(other, 4), lax.rem(other, 4)))
    G = [(dp, lax.rem(mp + j, 4)) for j in range(4)]

    peers = PLANE + Z[1:]
    barrier = pltpu.get_barrier_semaphore()
    for peer in peers:
        pl.semaphore_signal(barrier, inc=1, device_id=peer, device_id_type=MESH)
    pl.semaphore_wait(barrier, len(peers))

    def remote(src, dst, send_sem, recv_sem, device):
        copy = pltpu.make_async_remote_copy(
            src_ref=src, dst_ref=dst, send_sem=send_sem, recv_sem=recv_sem, device_id=device, device_id_type=MESH
        )
        copy.start()
        return copy

    def arrived(ref, recv_sem, send_sem):
        pltpu.make_async_remote_copy(
            src_ref=ref, dst_ref=ref, send_sem=send_sem, recv_sem=recv_sem, device_id=X, device_id_type=MESH
        ).wait_recv()

    def gather_steps(src, out, rows, cut, sems):
        zr, x0, y1, y0, x1, cr, sd = sems
        first = (0, cut) if cut else (0, rows)
        second = (cut, rows - cut) if cut else None
        full = (0, rows)

        def piece(d, m, span):
            return out.at[m, pl.ds(pl.multiple_of(d * rows + span[0], 16), span[1])]

        def send(src_ref, dst_ref, sem, device):
            remote(src_ref, dst_ref, sd.at[0], sem, device)

        def got(ref, sem):
            arrived(ref, sem, sd.at[0])

        def step0():
            for j in range(1, 4):
                send(src, piece(dp, mp, full), zr.at[j], Z[j])
            send(src.at[pl.ds(*first)], piece(dp, mp, first), x0.at[0], X)
            if second:
                send(src.at[pl.ds(*second)], piece(dp, mp, second), y1.at[0], Y)
            send(src.at[pl.ds(*first)], piece(dp, mp, first), y0.at[0], Y)
            if second:
                send(src.at[pl.ds(*second)], piece(dp, mp, second), x1.at[0], X)
            send(src, piece(dp, mp, full), cr.at[0], C)
            pltpu.make_async_copy(src, piece(dp, mp, full), sd.at[0]).start()
            yield

        def step1():
            for j in range(1, 4):
                d = 2 * zs[j] + x
                block = piece(d, mp, full)
                got(block, zr.at[j])
                one = piece(d, mp, first)
                send(one, one, x0.at[j], X)
                if second:
                    two = piece(d, mp, second)
                    send(two, two, y1.at[j], Y)
                send(one, one, y0.at[j], Y)
                if second:
                    send(two, two, x1.at[j], X)
                send(block, block, cr.at[0], C)
                yield

        def step2():
            for j in range(4):
                one = piece(2 * zs[j] + (1 - x), mp, first)
                got(one, x0.at[j])
                send(one, one, y0.at[4 + j], Y)
                send(one, one, cr.at[0], C)
                if second:
                    two = piece(2 * zs[j] + x, ym, second)
                    got(two, y1.at[j])
                    send(two, two, x1.at[4 + j], X)
                    send(two, two, cr.at[0], C)
                yield

        def step3():
            for i in range(2):
                for j in range(4):
                    one = piece(2 * zs[j] + (x if i == 0 else 1 - x), ym, first)
                    got(one, y0.at[4 * i + j])
                    send(one, one, cr.at[0], C)
                    if second:
                        two = piece(2 * zs[j] + (1 - x), (mp if i == 0 else ym), second)
                        got(two, x1.at[4 * i + j])
                        send(two, two, cr.at[0], C)
                    yield

        def step4():
            half = out.at[pl.ds(0, 2)]
            pltpu.make_async_copy(half, half, cr.at[0]).wait()
            pltpu.make_async_copy(out, out, sd.at[0]).wait()
            yield

        return [step0, step1, step2, step3, step4]

    depth = up_own.shape[0]
    slots = classes.shape[0]

    def image_steps():
        near, cross, core, near_sent, core_sent, up_got, down_got, up_sent, down_sent = isems

        def at(d, m, start=0, size=slots):
            return images.at[m, pl.ds(pl.multiple_of(d * slots + start, 16), size)]

        def plane(z_, i):
            return images.at[2 * i + c, pl.ds(pl.multiple_of(2 * z_ * slots, 16), 2 * slots)]

        def to_core(ref):
            remote(ref, ref, core_sent.at[0], core.at[0], C)

        half = slots // 2

        def step0():
            remote(image_own, at(dp, mp), near_sent.at[0], near.at[0], X)
            remote(image_own, at(dp, mp), near_sent.at[0], near.at[1], Y)
            remote(image_own, at(dp, mp), core_sent.at[0], core.at[0], C)
            pltpu.make_async_copy(image_own, at(dp, mp), s_local.at[5]).start()
            yield

        def step1():
            arrived(at(xd, mp), near.at[0], near_sent.at[0])
            remote(at(xd, mp, 0, half), at(xd, mp, 0, half), near_sent.at[0], cross.at[0], Y)
            to_core(at(xd, mp))
            arrived(at(dp, ym), near.at[1], near_sent.at[0])
            remote(at(dp, ym, half, half), at(dp, ym, half, half), near_sent.at[0], cross.at[1], X)
            to_core(at(dp, ym))
            yield

        def up(i, t):
            ref = plane(z - t, i)
            return pltpu.make_async_remote_copy(
                src_ref=ref, dst_ref=ref, send_sem=up_sent.at[t, i], recv_sem=up_got.at[t, i],
                device_id=(2 * (z + 1) + x, mp), device_id_type=MESH,
            )

        def down(i, t):
            ref = plane(z + t, i)
            return pltpu.make_async_remote_copy(
                src_ref=ref, dst_ref=ref, send_sem=down_sent.at[t, i], recv_sem=down_got.at[t, i],
                device_id=(2 * (z - 1) + x, mp), device_id_type=MESH,
            )

        def step2():
            arrived(at(xd, ym, 0, half), cross.at[0], near_sent.at[0])
            arrived(at(xd, ym, half, half), cross.at[1], near_sent.at[0])
            to_core(at(xd, ym))
            pltpu.make_async_copy(image_own, at(dp, mp), s_local.at[5]).wait()
            for i in range(2):
                pl.when(z < 3)(lambda i=i: up(i, 0).start())
                pl.when(z > 0)(lambda i=i: down(i, 0).start())
            yield

        def step3():
            for t in range(1, 4):
                for i in range(2):

                    def from_below(i=i, t=t):
                        ref = plane(z - t, i)
                        arrived(ref, up_got.at[t - 1, i], near_sent.at[0])
                        if t < 3:
                            pl.when(z < 3)(lambda: up(i, t).start())
                        to_core(ref)

                    def from_above(i=i, t=t):
                        ref = plane(z + t, i)
                        arrived(ref, down_got.at[t - 1, i], near_sent.at[0])
                        if t < 3:
                            pl.when(z > 0)(lambda: down(i, t).start())
                        to_core(ref)

                    pl.when(z >= t)(from_below)
                    pl.when(z + t <= 3)(from_above)
                    yield

        def step4():
            halves = images.at[pl.ds(0, 2)]
            pltpu.make_async_copy(halves, halves, core.at[0]).wait()
            pltpu.make_async_copy(halves, halves, core_sent.at[0]).wait()
            three = images.at[0, pl.ds(0, 3 * slots)]
            pltpu.make_async_copy(three, three, near_sent.at[0]).wait()
            for t in range(3):
                for i in range(2):
                    pl.when((z >= t) & (z < 3))(lambda i=i, t=t: up(i, t).wait_send())
                    pl.when((z + t <= 3) & (z > 0))(lambda i=i, t=t: down(i, t).wait_send())
            yield

        return [step0, step1, step2, step3, step4]

    kinds = {
        "S": gather_steps(small_own, smalls, 16, 0, gsems[0:7]),
        "A": gather_steps(attn_own, w_attn, depth, CUT, gsems[7:14]),
        "U": gather_steps(up_own, w_up, depth, CUT, gsems[14:21]),
        "D": gather_steps(down_own, w_down, depth, CUT, gsems[21:28]),
        "I": image_steps(),
    }

    def run(*steps):
        for name in steps:
            for _ in kinds[name[0]][int(name[1])]():
                pass

    def blend(steps, chunks):
        chunks = list(chunks)
        micro = [kinds[name[0]][int(name[1])] for name in steps]
        count = sum((1, 3, 4, 8, 1)[int(name[1])] if name[0] != "I" else (1, 1, 1, 6, 1)[int(name[1])] for name in steps)
        done, at = 0, 0
        for step in micro:
            for _ in step():
                at += 1
                while done < len(chunks) and done * count < at * len(chunks):
                    chunks[done]()
                    done += 1
        for chunk in chunks[done:]:
            chunk()

    lane = lax.broadcasted_iota(jnp.int32, (128, 128), 1)
    sub = lax.broadcasted_iota(jnp.int32, (128, 128), 0)
    low = lax.broadcasted_iota(jnp.int32, (1, 128), 1) < 64
    token_rows = hidden.shape[0]
    tiles = token_rows // 128
    end_count = h_ends.shape[0]

    def keep_low(values):
        return jnp.where(low, values, jnp.zeros_like(values))

    def keep_high(values):
        return jnp.where(low, jnp.zeros_like(values), values)

    def pack_own():
        rows = lax.broadcasted_iota(jnp.int32, (depth, depth), 0)
        eye = (rows == lax.broadcasted_iota(jnp.int32, (depth, depth), 1)).astype(f32).astype(bf16)
        out_t = nt(eye, w_out[...]).astype(bf16)
        query, key, value = w_qkv[0], w_qkv[1], w_qkv[2]
        attn_own[:, 0:128] = query[:, 0:128]
        attn_own[:, 128:256] = key[:, 0:128]
        attn_own[:, 256:384] = value[:, 0:128]
        attn_own[:, 384:512] = jnp.concatenate([query[:, 128:192], value[:, 128:192]], axis=1)
        attn_own[:, 512:640] = jnp.concatenate([key[:, 128:192], out_t[:, 128:192]], axis=1)
        attn_own[:, 640:768] = out_t[:, 0:128]

    def pack_small():
        shift = lax.broadcasted_iota(jnp.int32, (depth, 384), 1) - lax.broadcasted_iota(jnp.int32, (depth, 384), 0)
        made = nn(norms[...], (shift == depth * lax.rem(dp, 4)).astype(f32).astype(bf16))
        shift = lax.broadcasted_iota(jnp.int32, (slots, 128), 1) - lax.broadcasted_iota(jnp.int32, (slots, 128), 0)
        flags = jnp.broadcast_to(valid_own[...].astype(f32), (8, slots)).astype(bf16)
        flags = nn(flags, (shift == slots * lax.rem(dp, 2)).astype(f32).astype(bf16))
        parts = [made[v : v + 1, 128 * t : 128 * (t + 1)] for v in range(4) for t in range(3)]
        small_own[...] = jnp.concatenate(parts + [flags[0:4, :]], axis=0).astype(bf16)

    def masks(g):
        slot_row = lax.broadcasted_iota(jnp.int32, (end_count, 128), 0)
        spots = []
        best = jnp.full((end_count, 1), -1, jnp.int32)
        for b in range(tiles):
            sequence = 8 * b + lax.shift_right_logical(lax.broadcasted_iota(jnp.int32, (1, 128), 1), 4)
            caption = 2 * sequence + ids[ym if g else mp, pl.ds(b, 1), :]
            column = jnp.sum(jnp.where(lane == sub, caption, 0), axis=1, keepdims=True)
            mask_ref[tiles * g + b] = jnp.where((column == caption) & (sub >= lane), 0.0, -1e30)
            member = slot_row == caption
            spot = lax.broadcasted_iota(jnp.int32, (end_count, 128), 1) + 128 * b
            best = jnp.maximum(best, jnp.max(jnp.where(member, spot, -1), axis=1, keepdims=True))
            member_ref[g, :, 128 * b : 128 * (b + 1)] = jnp.where(member, 0.0, -1e30)
            spots.append(spot)
        for b in range(tiles):
            place_ref[g, :, 128 * b : 128 * (b + 1)] = (spots[b] == best).astype(f32).astype(bf16)

    def image_tower():
        hat, _ = standardise(classes[...].astype(f32))
        raw = nn((hat * image_gain[...].reshape(1, -1) + image_bias[...].reshape(1, -1)).astype(bf16), image_proj[...])
        image_own[...] = (raw * inverse_norm(raw)).astype(bf16)

    def small_vectors():
        halves = []
        for w in range(2):
            halves.append(sum(smalls[0, 64 * w + 16 * d : 64 * w + 16 * (d + 1), :].astype(f32) for d in range(4)))
        for v in range(4):
            for w in range(2):
                for t in range(3):
                    at = 384 * w + 128 * t
                    vecs[v : v + 1, at : at + 128] = halves[w][3 * v + t : 3 * v + t + 1, :]
        for m in range(4):
            for pair in range(4):
                both = sum(smalls[m, 32 * pair + 16 * d : 32 * pair + 16 * (d + 1), :].astype(f32) for d in range(2))
                valid_ref[m : m + 1, 128 * pair : 128 * (pair + 1)] = both[12:13, :]

    def first_norm(g):
        def body(b):
            rows = rows_of(tiles * g + b, 128)
            values = x_ref[rows, :].astype(f32)
            hat, _ = standardise(values)
            a_ref[rows, :] = (hat * vecs[0:1, :] + vecs[1:2, :]).astype(bf16)
            if g == 0:
                hidden[rows, :] = values

        loop(tiles, body)

    def soft(scores):
        top = jnp.max(scores, axis=-1, keepdims=True)
        raised = jnp.exp(scores - top)
        return raised * (1.0 / jnp.sum(raised, axis=-1, keepdims=True))

    scale = HEAD_DIM**-0.5

    def project(m, g):
        def body(b):
            rows = rows_of(2 * g + b, 256)
            qkv[m, rows, :] = nn(a_ref[rows, :], w_attn[m]).astype(bf16)

        loop(2, body)

    def attention(m):
        project(m, 0)

        def body(pair):
            for b in (2 * pair, 2 * pair + 1):
                rows = rows_of(b, 128)
                q01, k01, v01, qv, ko = (qkv[m, rows, 128 * i : 128 * (i + 1)] for i in range(5))
                mask = mask_ref[b]
                p0 = soft(nt(keep_low(q01), k01) * scale + mask).astype(bf16)
                p1 = soft(nt(keep_high(q01), k01) * scale + mask).astype(bf16)
                p2 = soft(nt(keep_low(qv), ko) * scale + mask).astype(bf16)
                o01 = jnp.where(low, nn(p0, v01), nn(p1, v01)).astype(bf16)
                o2 = keep_high(nn(p2, qv)).astype(bf16)
                qkv[m, rows, 512:640] = keep_low(ko) + o2
                qkv[m, rows, 640:768] = o01

        loop(tiles // 2, body)

        def attended(b):
            rows = rows_of(b, 256)
            mixed = jnp.concatenate([keep_high(qkv[m, rows, 512:640]), qkv[m, rows, 640:768]], axis=1)
            hidden[rows, :] += nt(mixed, w_attn[m, :, 512:768])

        loop(2, attended)

    def second_norm():
        def body(b):
            rows = rows_of(b, 128)
            hat, _ = standardise(hidden[rows, :])
            a_two[rows, :] = (hat * vecs[2:3, :] + vecs[3:4, :]).astype(bf16)

        loop(tiles, body)
        place = place_ref[0]
        ends = pick(place, hidden[...])
        h_ends[...] = ends
        hat, _ = standardise(ends)
        ends_two[mp] = (hat * vecs[2:3, :] + vecs[3:4, :]).astype(bf16)

    def ends_up(m):
        u_ends[m] = nn(ends_two[mp], w_up[m])

    def full_up(m):
        def body(b):
            rows = rows_of(b, 256)
            upper = nn(a_two[rows, :], w_up[m])
            active[m, rows, :] = (upper * half_erf(upper)).astype(bf16)

        loop(tiles // 2, body)

    def slope_of(upper):
        return half_erf(upper) + upper * jnp.exp(-0.5 * upper * upper) * (1.0 / (2.0 * jnp.pi) ** 0.5)

    def group_up():
        def body(i):
            upper = nn(ends_two[i], w_up[mp])
            rows = rows_of(i, end_count)
            g_all[rows, :] = (upper * half_erf(upper)).astype(bf16)
            s_all[rows, :] = slope_of(upper)

        loop(4, body)

    def full_down(b):
        rows = slice(256 * b, 256 * (b + 1))

        def body(m, total):
            return total + nt(active[m, rows, :], w_down[m])

        stage_out[rows, :] = lax.fori_loop(0, 4, body, hidden[rows, :]).astype(bf16)

    token_copies = []
    for g in range(2):
        wanted = tokens.at[rows_of(ym if g else mp, token_rows)]
        token_copies.append(pltpu.make_async_copy(wanted, x_ref.at[pl.ds(g * token_rows, token_rows)], s_local.at[g]))
        token_copies[g].start()
    pack_small()
    run("S0")
    pack_own()
    run("A0")
    image_tower()
    run("I0", "U0")
    masks(0)
    masks(1)
    run("S1", "A1", "D0", "I1", "S2", "A2", "I2", "U1", "S3", "S4")
    small_vectors()
    for g in range(2):
        token_copies[g].wait()
        first_norm(g)
    run("D1", "A3", "A4")
    blend(("U2", "I3", "D2", "U3"), [functools.partial(attention, m) for m in range(4)])
    second_norm()
    swaps = [remote(ends_two.at[mp], ends_two.at[mp], s_exs.at[j - 1], s_a2.at[j - 1], G[j]) for j in range(1, 4)]
    run("U4")
    blend(
        ("D3",),
        [functools.partial(full_up, m) for m in range(4)] + [functools.partial(project, m, 1) for m in range(4)],
    )
    loop(4, ends_up)
    run("I4")
    for swap in swaps:
        swap.wait()
    group_up()
    run("D4")

    pooled = h_ends[...]
    for m in range(4):
        upper = u_ends[m]
        pooled = pooled + nt((upper * half_erf(upper)).astype(bf16), w_down[m])
    scale_back = inverse_norm(pooled)
    text = (pooled * scale_back).astype(bf16)
    own_valid = small_own[12:13, :].astype(f32)
    own_valid = jnp.max(
        jnp.where(
            lax.rem(lax.broadcasted_iota(jnp.int32, (slots, 128), 1), slots)
            == lax.broadcasted_iota(jnp.int32, (slots, 128), 0),
            own_valid,
            0.0,
        ),
        axis=1,
        keepdims=True,
    )
    live = own_valid > 0.0
    place_col = lax.broadcasted_iota(jnp.int32, (slots, 512), 1)
    place_row = lax.broadcasted_iota(jnp.int32, (slots, 512), 0)

    def target_of(m):
        return (place_col == place_row + dp * slots) & (mp == m)

    row_sum = jnp.zeros((slots, 1), f32)
    matched = jnp.zeros((slots, 1), f32)
    for m in range(4):
        logits = logit_scale * nt(text, images[m])
        weight = jnp.exp(logits)
        matched = matched + jnp.sum(jnp.where(target_of(m), logits, 0.0), axis=1, keepdims=True)
        seen = jnp.where(valid_ref[m : m + 1, :] > 0.0, weight, 0.0)
        weight_ref[m] = seen
        row_sum = row_sum + jnp.sum(seen, axis=1, keepdims=True)
        columns = jnp.sum(jnp.where(live, weight, 0.0), axis=0, keepdims=True)
        for part in range(4):
            sum_own[4 * m + part : 4 * m + part + 1, :] = columns[:, 128 * part : 128 * (part + 1)]
    row_part = jnp.sum(jnp.where(live, jnp.log(row_sum) - 2.0 * matched, 0.0), axis=0, keepdims=True)
    sum_own[16:24, :] = jnp.broadcast_to(row_part, (8, 128))

    swaps = [remote(sum_own, sum_got.at[here], s_sums.at[j - 1], s_sum.at[j - 1], PLANE[j - 1]) for j in range(1, 8)]
    sum_got[here] = sum_own[...]
    full_down(0)
    for swap in swaps:
        swap.wait()
    sum_buf[...] = ((sum_got[0] + sum_got[1]) + (sum_got[2] + sum_got[3])) + (
        (sum_got[4] + sum_got[5]) + (sum_got[6] + sum_got[7])
    )
    swaps = [remote(sum_buf, sum_got.at[8 + z], s_sums.at[6 + j], s_sum.at[6 + j], Z[j]) for j in range(1, 4)]
    sum_got[8 + z] = sum_buf[...]
    full_down(1)
    for swap in swaps:
        swap.wait()
    sums = (sum_got[8] + sum_got[9]) + (sum_got[10] + sum_got[11])

    total = sums[16:17, 0:1]
    unit_grad = jnp.zeros((slots, text.shape[1]), f32)
    for m in range(4):
        columns = jnp.concatenate([sums[4 * m + part : 4 * m + part + 1, :] for part in range(4)], axis=1)
        seen = valid_ref[m : m + 1, :] > 0.0
        total = total + jnp.sum(jnp.where(seen, jnp.log(columns), 0.0), axis=1, keepdims=True)
        spread = 0.5 * weight_ref[m] * (1.0 / row_sum + 1.0 / columns)
        grad = jnp.where(seen & live, spread, 0.0) - jnp.where(target_of(m) & live, 1.0, 0.0)
        unit_grad = unit_grad + nn((logit_scale * grad).astype(bf16), images[m])
    loss_out[...] = total * (0.5 / slot_total)
    along = jnp.sum(unit_grad * pooled, axis=-1, keepdims=True)
    pooled_grad = scale_back * unit_grad - pooled * (scale_back * scale_back * scale_back * along)
    branch_grad = pooled_grad.astype(bf16)
    ends_grad[mp] = branch_grad
    swaps = [remote(ends_grad.at[mp], ends_grad.at[mp], s_exs.at[2 + j], s_dm.at[j - 1], G[j]) for j in range(1, 4)]

    own_rows = rows_of(mp, token_rows)
    far_rows = rows_of(ym, token_rows)
    out_swaps = [
        remote(stage_out, block_out.at[own_rows], s_bo.at[0], s_bo.at[1], Y),
        remote(stage_out, block_out.at[own_rows], s_bo.at[2], s_bo.at[3], C),
    ]
    keep_out = pltpu.make_async_copy(stage_out, block_out.at[own_rows], s_local.at[2])
    keep_out.start()

    two_grad = jnp.zeros_like(pooled)
    for m in range(4):
        upper_grad = (nn(branch_grad, w_down[m]) * slope_of(u_ends[m])).astype(bf16)
        two_grad = two_grad + nt(upper_grad, w_up[m])
    hat_two, rstd_two = standardise(h_ends[...])
    vec_buf[0] = jnp.zeros_like(vec_buf[0])
    vec_buf[0, 2:3, :] = jnp.sum(two_grad * hat_two, axis=0, keepdims=True)
    vec_buf[0, 3:4, :] = jnp.sum(two_grad, axis=0, keepdims=True)
    hidden_grad = pooled_grad + norm_pull(two_grad, hat_two, rstd_two, vecs[2:3, :])
    ends_back[0] = hidden_grad.astype(bf16)
    back_swap = remote(ends_back.at[0], ends_back.at[1], s_exs.at[6], s_dh.at[0], Y)

    for swap in swaps:
        swap.wait()
    group_grad = ends_grad[...].reshape(4 * end_count, -1)
    upper_grad = (nn(group_grad, w_down[mp]) * s_all[...]).astype(bf16)
    grad_down[...] = tn(group_grad, g_all[...]).astype(bf16)

    def block(z_, x_):
        return pl.ds(pl.multiple_of((2 * z_ + x_) * depth, 16), depth)

    grads, outs = [grad_down, grad_up, grad_attn], [down_out, up_out, attn_out]

    def sum_start(k):
        for j in (2, 1, 3, 0):
            remote(grads[k].at[block(zt[j], 1 - x)], step_x.at[k, j], s_send.at[k], s_x.at[k, j], X)

    def sum_add(k, j):
        arrived(step_x.at[k, j], s_x.at[k, j], s_send.at[k])
        mine = block(zt[j], x)
        summed = grads[k][mine, :].astype(f32) + step_x[k, j].astype(f32)
        if j:
            grads[k][mine, :] = summed.astype(bf16)
            remote(grads[k].at[mine], step_z.at[k, j - 1], s_send.at[k], s_z.at[k, j - 1], Z[j])
        else:
            outs[k][...] = summed

    def sum_end(k):
        for j in range(1, 4):
            arrived(step_z.at[k, j - 1], s_z.at[k, j - 1], s_send.at[k])
        outs[k][...] = outs[k][...] + step_z[k, 0].astype(f32) + step_z[k, 1].astype(f32) + step_z[k, 2].astype(f32)
        sent = grads[k].at[pl.ds(0, 7 * depth)]
        pltpu.make_async_copy(sent, sent, s_send.at[k]).wait()

    sum_start(0)
    grad_up[...] = tn(ends_two[...].reshape(4 * end_count, -1), upper_grad).astype(bf16)
    sum_start(1)

    def attention_back(m, g, mix=False):
        place = place_ref[g]
        member = member_ref[g]
        ends_row = ends_back[g]
        span = slice(token_rows * g, token_rows * (g + 1))
        k01, v01, qv, ko = (qkv[m, span, 128 * i : 128 * (i + 1)] for i in range(1, 5))
        q_e = nn(place, qkv[m, span, 0:128]).astype(bf16)
        q2_e = keep_low(nn(place, qv)).astype(bf16)
        do01 = nn(ends_row, w_attn[m, :, 640:768]).astype(bf16)
        do2 = keep_high(nn(ends_row, w_attn[m, :, 512:640])).astype(bf16)

        def head(query, keys, values, outer):
            probs = soft(nt(query, keys) * scale + member)
            probs_grad = nt(outer, values)
            centre = jnp.sum(probs_grad * probs, axis=-1, keepdims=True)
            return probs.astype(bf16), (probs * (probs_grad - centre)).astype(bf16)

        p0, ds0 = head(keep_low(q_e), k01, v01, keep_low(do01))
        p1, ds1 = head(keep_high(q_e), k01, v01, keep_high(do01))
        p2, ds2 = head(q2_e, ko, qv, do2)
        dq01 = (jnp.where(low, nn(ds0, k01), nn(ds1, k01)) * scale).astype(bf16)
        dq2 = keep_low(nn(ds2, ko) * scale).astype(bf16)
        if g == 1 and mix:
            far_mix[:, 0:128] = nn(p2, qv).astype(bf16)
            far_mix[:, 128:256] = jnp.where(low, nn(p0, v01), nn(p1, v01)).astype(bf16)
        d_ref = d_far if g else active
        d_ref[m, :, 0:128] = tn(place, dq01).astype(bf16)
        d_ref[m, :, 128:256] = (jnp.where(low, tn(ds0, q_e), tn(ds1, q_e)) * scale).astype(bf16)
        d_ref[m, :, 256:384] = jnp.where(low, tn(p0, do01), tn(p1, do01)).astype(bf16)
        d_ref[m, :, 384:512] = jnp.where(low, tn(place, dq2), tn(p2, do2)).astype(bf16)
        d_ref[m, :, 512:640] = keep_low(tn(ds2, q2_e) * scale).astype(bf16)

    def token_back(g):
        d_ref = d_far if g else active

        def body(b):
            rows = rows_of(b, 256)
            total = jnp.zeros((256, d_attn.shape[1]), f32)
            for m in range(4):
                total = total + nt(d_ref[m, rows, 0:640], w_attn[m, :, 0:640])
            d_attn[rows_of(2 * g + b, 256), :] = total

        loop(2, body)

    def attn_grad(m):
        ends_mix = nn(place_ref[0], qkv[m, 0:token_rows, 512:768]).astype(bf16)
        outer = tn(ends_back[0], ends_mix) + tn(ends_back[1], far_mix[...])

        def made(start, stop):
            span = slice(start, stop)
            return tn(a_ref[0:token_rows, :], active[m, :, span]) + tn(a_ref[token_rows:, :], d_far[m, :, span])

        last = jnp.where(low, made(512, 640), outer[:, 0:128])
        return jnp.concatenate([made(0, 512), last, outer[:, 128:256]], axis=1)

    steps = iter([(k, j) for k in range(3) for j in range(4)])

    def sum_some(count):
        for _ in range(count):
            k, i = next(steps)
            sum_add(k, (2, 1, 3, 0)[i])

    back_swap.wait()
    m = 2 * y + (1 - c)
    attention_back(m, 0, True)
    attention_back(m, 1, True)
    sum_some(1)
    attn_send[...] = attn_grad(m).astype(bf16)
    core_swap = remote(attn_send, attn_core, s_exs.at[7], s_core.at[0], C)
    sum_some(1)
    m = 2 * y + c
    attention_back(m, 0, True)
    attention_back(m, 1, True)
    sum_some(1)
    made = attn_grad(m)
    core_swap.wait()
    grad_attn[...] = (made + attn_core[...].astype(f32)).astype(bf16)
    sum_start(2)
    sum_some(1)
    for i in range(2):
        for g in range(2):
            attention_back(2 * (1 - y) + i, g)
            sum_some(1)
    def token_end(g):
        def body(b):
            rows = rows_of(tiles * g + b, 128)
            hat, rstd = standardise(x_ref[rows, :].astype(f32))
            grad = d_attn[rows, :]
            if g == 0:
                vec_buf[0, 0:1, :] += jnp.sum(grad * hat, axis=0, keepdims=True)
                vec_buf[0, 1:2, :] += jnp.sum(grad, axis=0, keepdims=True)
            d_attn[rows, :] = norm_pull(grad, hat, rstd, vecs[0:1, :])

        loop(tiles, body)
        span = slice(token_rows * g, token_rows * (g + 1))
        stage_grad[span, :] = (d_attn[span, :] + tn(place_ref[g], ends_back[g])).astype(bf16)

    grad_swaps, keep_grads, vec_swaps = [], [], []
    for g in range(2):
        token_back(g)
        sum_some(1)
        if g == 0:
            out_swaps[0].wait()
            on = remote(block_out.at[far_rows], block_out.at[far_rows], s_on.at[0], s_on.at[1], C)
        token_end(g)
        if g == 0:
            for j in range(1, 8):
                vec_swaps.append(
                    remote(vec_buf.at[0], vec_got.at[here], s_vs.at[j - 1], s_v.at[j - 1], PLANE[j - 1])
                )
            vec_got[here] = vec_buf[0]
        ref = stage_grad.at[pl.ds(token_rows * g, token_rows)]
        spot = token_out.at[far_rows if g else own_rows]
        grad_swaps.append(remote(ref, spot, s_tg.at[2 * g], s_tg.at[2 * g + 1], C))
        keep_grads.append(pltpu.make_async_copy(ref, spot, s_local.at[3 + g]))
        keep_grads[g].start()
        sum_some(1)
    for swap in vec_swaps:
        swap.wait()
    vec_buf[1] = ((vec_got[0] + vec_got[1]) + (vec_got[2] + vec_got[3])) + (
        (vec_got[4] + vec_got[5]) + (vec_got[6] + vec_got[7])
    )
    vec_swaps = [
        remote(vec_buf.at[1], vec_got.at[8 + z], s_vs.at[6 + j], s_v.at[6 + j], Z[j]) for j in range(1, 4)
    ]
    vec_got[8 + z] = vec_buf[1]
    sum_end(0)
    sum_end(1)
    for swap in vec_swaps:
        swap.wait()
    vec_out[...] = (vec_got[8] + vec_got[9]) + (vec_got[10] + vec_got[11])
    sum_end(2)
    out_swaps[1].wait()
    on.wait()
    keep_out.wait()
    for swap in grad_swaps + keep_grads:
        swap.wait()


def layer(slot_total, w_qkv, w_out, up_own, down_own, norms, valid, classes, *rest):
    depth, width = up_own.shape
    slots = classes.shape[0]
    rows = rest[3].shape[0] // 4

    def gather_sems():
        return [DMA((4,)), DMA((4,)), DMA((4,)), DMA((8,)), DMA((8,)), DMA((1,)), DMA((1,))]

    here, there = pl.BlockSpec(memory_space=VMEM), pl.BlockSpec(memory_space=pltpu.HBM)
    square = VMEM((4, width, width), bf16)
    scratch = [
        square,
        square,
        square,
        VMEM((4, 8 * slots, width), bf16),
        VMEM((4, 128, 128), bf16),
        VMEM((2 * rows, width), bf16),
        VMEM((2 * rows, width), bf16),
        VMEM((4, 2 * rows, width), bf16),
        VMEM((rows, width), f32),
        VMEM((rows, width), bf16),
        VMEM((4, rows, width), bf16),
        VMEM((rows, width), bf16),
        VMEM((slots, width), bf16),
        VMEM((8, width), f32),
        VMEM((2 * rows // 128, 128, 128), f32),
        VMEM((2, slots, rows), bf16),
        VMEM((2, slots, rows), f32),
        VMEM((slots, width), f32),
        VMEM((4, slots, width), bf16),
        VMEM((4, slots, width), bf16),
        VMEM((4, slots, width), f32),
        VMEM((4 * slots, width), bf16),
        VMEM((4 * slots, width), f32),
        VMEM((4, slots, 8 * slots), f32),
        VMEM((8, 8 * slots), f32),
        VMEM((24, 128), f32),
        VMEM((24, 128), f32),
        VMEM((12, 24, 128), f32),
        VMEM((2 * rows, width), f32),
        VMEM((4, rows, 640), bf16),
        VMEM((width, width), bf16),
        VMEM((width, width), bf16),
        VMEM((width, width), bf16),
        VMEM((3, 4, depth, width), bf16),
        VMEM((3, 3, depth, width), bf16),
        VMEM((width, width), bf16),
        VMEM((width, width), bf16),
        VMEM((2, slots, width), bf16),
        VMEM((2, 8, width), f32),
        VMEM((12, 8, width), f32),
        VMEM((2 * rows, width), bf16),
        VMEM((depth, width), bf16),
        VMEM((16, 128), bf16),
        VMEM((slots, 256), bf16),
    ]
    for _ in range(4):
        scratch += gather_sems()
    scratch += [DMA((2,)), DMA((2,)), DMA((1,)), DMA((1,)), DMA((1,)), DMA((3, 2)), DMA((3, 2)), DMA((3, 2)), DMA((3, 2))]
    scratch += [DMA((6,)), DMA((4,)), DMA((2,)), DMA((3,)), DMA((3,)), DMA((3,)), DMA((1,)), DMA((10,)), DMA((10,))]
    scratch += [DMA((3, 4)), DMA((3, 3)), DMA((1,)), DMA((10,)), DMA((10,)), DMA((4,)), DMA((8,))]
    return pl.pallas_call(
        functools.partial(layer_kernel, slot_total),
        out_shape=[
            jax.ShapeDtypeStruct((1, 1), f32),
            jax.ShapeDtypeStruct((4 * rows, width), bf16),
            jax.ShapeDtypeStruct((4 * rows, width), bf16),
            jax.ShapeDtypeStruct((depth, width), f32),
            jax.ShapeDtypeStruct((depth, width), f32),
            jax.ShapeDtypeStruct((depth, width), f32),
            jax.ShapeDtypeStruct((8, width), f32),
        ],
        in_specs=[here] * 10 + [there, here],
        out_specs=[here, there, there, here, here, here, here],
        scratch_shapes=scratch,
        compiler_params=pltpu.CompilerParams(
            collective_id=1, has_side_effects=True, vmem_limit_bytes=63 * 2**20
        ),
        cost_estimate=pl.CostEstimate(flops=30 * 10**9, bytes_accessed=40 * 10**6, transcendentals=10**7),
        name="layer",
    )(w_qkv, w_out, up_own, down_own, norms, valid, classes, *rest)


def finish_kernel(block_in, token_in, attn_in, up_in, down_in, block_out, token_out, qkv_out, out_out, up_out, down_out, narrow, wide, held, sems):
    parts = narrow.shape[0]
    rows = narrow.shape[1]
    loads, saves, keeps = [], [], []
    for i in range(parts):
        load = pltpu.make_async_copy(block_in.at[pl.ds(i * rows, rows)], held.at[i], sems.at[1 + 2 * parts + i])
        load.start()
        save = pltpu.make_async_copy(held.at[i], block_out.at[pl.ds(i * rows, rows)], sems.at[1 + 3 * parts + i])
        keeps.append((load, save))
    for i in range(parts):
        loads.append(pltpu.make_async_copy(token_in.at[pl.ds(i * rows, rows)], narrow.at[i], sems.at[1 + i]))
        loads[i].start()
        saves.append(pltpu.make_async_copy(wide.at[i], token_out.at[pl.ds(i * rows, rows)], sems.at[1 + parts + i]))
    up_out[...] = up_in[...]
    down_out[...] = down_in[...]
    for i, (pair, single) in enumerate(((0, 384), (128, 512), (256, 448))):
        qkv_out[i] = jnp.concatenate([attn_in[:, pair : pair + 128], attn_in[:, single : single + 64]], axis=1)
    depth = attn_in.shape[0]
    row = lax.broadcasted_iota(jnp.int32, (depth, depth), 0)
    eye = (row == lax.broadcasted_iota(jnp.int32, (depth, depth), 1)).astype(f32).astype(bf16)
    mixed = jnp.concatenate([attn_in[:, 640:768], attn_in[:, 576:640]], axis=1)
    out_out[...] = sum(tn(part, eye) for part in split_three(mixed))
    for i in range(parts):
        loads[i].wait()
        wide[i] = narrow[i].astype(f32)
        saves[i].start()
    for load, save in keeps:
        load.wait()
        save.start()
    for save in saves:
        save.wait()
    for load, save in keeps:
        save.wait()


def finish(block_out, token_grad, own_attn, own_up, own_down):
    rows, width = token_grad.shape
    depth = own_up.shape[0]
    parts = 4
    here, there = pl.BlockSpec(memory_space=VMEM), pl.BlockSpec(memory_space=pltpu.HBM)
    return pl.pallas_call(
        finish_kernel,
        out_shape=[
            jax.ShapeDtypeStruct(block_out.shape, bf16),
            jax.ShapeDtypeStruct((rows, width), f32),
            jax.ShapeDtypeStruct((3, depth, 192), f32),
            jax.ShapeDtypeStruct((192, depth), f32),
            jax.ShapeDtypeStruct((depth, width), f32),
            jax.ShapeDtypeStruct((depth, width), f32),
        ],
        in_specs=[there, there, here, here, here],
        out_specs=[there, there, here, here, here, here],
        scratch_shapes=[
            VMEM((parts, rows // parts, width), bf16),
            VMEM((parts, rows // parts, width), f32),
            VMEM((parts, rows // parts, width), bf16),
            DMA((1 + 4 * parts,)),
        ],
        compiler_params=pltpu.CompilerParams(vmem_limit_bytes=63 * 2**20),
        name="finish",
    )(block_out, token_grad, own_attn, own_up, own_down)


def on_kernel(
    tokens,
    segment_ids,
    slot_valid,
    ln1_gain,
    ln1_bias,
    w_qkv,
    w_out,
    ln2_gain,
    ln2_bias,
    w_up,
    w_down,
    class_tokens,
    image_gain,
    image_bias,
    image_proj,
):
    dp_rank = lax.axis_index("dp")
    depth, slots = w_up.shape[0], slot_valid.shape[0]
    loss, block_out, token_grad, own_attn, own_up, own_down, vectors = layer(
        slots * 32,
        w_qkv,
        w_out,
        w_up,
        w_down.T,
        jnp.stack([ln1_gain, ln1_bias, ln2_gain, ln2_bias]),
        slot_valid.reshape(1, slots),
        class_tokens,
        image_gain,
        image_bias,
        image_proj,
        tokens,
        segment_ids.reshape(4, 4, 128),
    )
    block_out, token_grad, qkv_grad, out_grad, own_up, own_down = finish(
        block_out, token_grad, own_attn, own_up, own_down
    )
    vectors = lax.dynamic_slice_in_dim(vectors, dp_rank * depth, depth, 1)
    return (
        loss.reshape(()),
        block_out,
        token_grad,
        vectors[0],
        vectors[1],
        qkv_grad,
        out_grad,
        vectors[2],
        vectors[3],
        own_up,
        own_down.T,
    )


def make(dp_size, mp_size):
    def on_device(
        tokens,
        segment_ids,
        slot_valid,
        ln1_gain,
        ln1_bias,
        w_qkv,
        w_out,
        ln2_gain,
        ln2_bias,
        w_up,
        w_down,
        class_tokens,
        image_gain,
        image_bias,
        image_proj,
    ):
        both = ("dp", "mp")
        dp_rank, mp_rank = lax.axis_index("dp"), lax.axis_index("mp")
        depth = w_up.shape[0]
        width = depth * dp_size
        head_cols = w_out.shape[0]
        heads = head_cols // HEAD_DIM
        rows = tokens.shape[0] // mp_size
        seqs = rows // SEQ_LEN
        slots = slot_valid.shape[0]
        slot_total = slots * dp_size * mp_size

        packed = jnp.stack(
            [jnp.concatenate([w_qkv[0], w_qkv[1], w_qkv[2], w_out.T], axis=1), w_up, w_down.T]
        )
        norms = jnp.stack([ln1_gain, ln1_bias, ln2_gain, ln2_bias])
        image_hat, _ = standardise(class_tokens.astype(f32))
        image_normed = (image_hat * image_gain + image_bias).astype(bf16)
        image_raw = nn(image_normed, image_proj)
        image_unit = (image_raw * inverse_norm(image_raw)).astype(bf16)

        weights = lax.all_gather(packed, both, axis=0).reshape(dp_size, mp_size, 3, depth, -1)
        weights = weights.transpose(2, 1, 0, 3, 4).reshape(3, mp_size, width, -1)
        vectors = lax.all_gather(norms, "dp", axis=1, tiled=True).astype(f32)
        all_image = lax.all_gather(image_unit, both, axis=0, tiled=True)
        all_valid = lax.all_gather(slot_valid.astype(bf16), both, axis=0, tiled=True) > 0

        own = lax.dynamic_slice_in_dim(tokens, mp_rank * rows, rows, 0).astype(f32)
        ids = lax.dynamic_slice_in_dim(segment_ids, mp_rank * rows, rows, 0)
        grid_ids = ids.reshape(seqs, SEQ_LEN)
        first_len = jnp.sum((grid_ids == 0).astype(jnp.int32), axis=1)
        starts = jnp.arange(seqs, dtype=jnp.int32) * SEQ_LEN
        ends = jnp.stack([starts + first_len - 1, starts + SEQ_LEN - 1], axis=1).reshape(2 * seqs)
        place = (ends[:, None] == jnp.arange(rows)[None, :]).astype(bf16)

        hat_one, rstd_one = standardise(own)
        normed = (hat_one * vectors[0] + vectors[1]).astype(bf16)
        attn = weights[0]
        qkv = jnp.einsum("rd,mde->mre", normed, attn[:, :, : 3 * head_cols], preferred_element_type=f32)
        qkv = qkv.astype(bf16).reshape(mp_size, rows, 3, heads, HEAD_DIM)
        blocks = rows // tile_rows
        split = qkv.reshape(mp_size, blocks, tile_rows, 3, heads, HEAD_DIM)
        query, key, value = split[:, :, :, 0], split[:, :, :, 1], split[:, :, :, 2]
        tile_ids = ids.reshape(blocks, tile_rows)
        spots = jnp.arange(tile_rows)
        allowed = (
            (tile_ids[:, :, None] == tile_ids[:, None, :])
            & (spots[:, None] // SEQ_LEN == spots[None, :] // SEQ_LEN)[None]
            & (spots[:, None] >= spots[None, :])[None]
        )[None, :, None]
        scale = HEAD_DIM**-0.5
        scores = jnp.einsum("mbqhc,mbkhc->mbhqk", query, key, preferred_element_type=f32) * scale
        scores = jnp.where(allowed, scores, -1e30)
        probs = jax.nn.softmax(scores, axis=-1)
        mixed = jnp.einsum("mbhqk,mbkhc->mbqhc", probs.astype(bf16), value, preferred_element_type=f32)
        mixed = mixed.astype(bf16).reshape(mp_size, rows, head_cols)
        out_t = attn[:, :, 3 * head_cols :]
        attended = jnp.einsum("mre,mde->rd", mixed, out_t, preferred_element_type=f32)
        hidden = own + attended

        def feed(rows_in):
            hat, rstd = standardise(rows_in)
            normed_two = (hat * vectors[2] + vectors[3]).astype(bf16)
            upper = jnp.einsum("rd,mdf->mrf", normed_two, weights[1], preferred_element_type=f32)
            active = (upper * phi(upper)).astype(bf16)
            branch = jnp.einsum("mrf,mdf->rd", active, weights[2], preferred_element_type=f32)
            return hat, rstd, normed_two, upper, active, rows_in + branch

        block_out = feed(hidden)[-1].astype(bf16)
        hidden_ends = hidden[ends]
        hat_two, rstd_two, normed_two, upper, active, pooled = feed(hidden_ends)

        scale_back = inverse_norm(pooled)
        text = (pooled * scale_back).astype(bf16)
        logits = logit_scale * nt(text, all_image)
        live = slot_valid > 0
        weight = jnp.exp(logits)
        row_sum = jnp.sum(jnp.where(all_valid[None, :], weight, 0.0), axis=1)
        col_part = jnp.sum(jnp.where(live[:, None], weight, 0.0), axis=0)
        row_index = (dp_rank * mp_size + mp_rank) * slots + jnp.arange(slots)
        target = jnp.arange(slot_total)[None, :] == row_index[:, None]
        matched = jnp.sum(jnp.where(target, logits, 0.0), axis=1)
        row_part = jnp.sum(jnp.where(live, jnp.log(row_sum) - 2.0 * matched, 0.0))
        sums = lax.psum(jnp.concatenate([col_part, row_part[None]]), both)
        col_sum = sums[:slot_total]
        loss = 0.5 * (sums[slot_total] + jnp.sum(jnp.where(all_valid, jnp.log(col_sum), 0.0))) / slot_total
        pair = live[:, None] & all_valid[None, :]
        spread = 0.5 * weight * (1.0 / row_sum[:, None] + 1.0 / col_sum[None, :])
        grad_logits = jnp.where(pair, spread, 0.0) - (target & live[:, None]).astype(f32)
        cosine_grad = (logit_scale * grad_logits).astype(bf16)
        unit_grad = nn(cosine_grad, all_image)
        along = jnp.sum(unit_grad * pooled, axis=-1, keepdims=True)
        pooled_grad = scale_back * unit_grad - pooled * (scale_back * scale_back * scale_back * along)

        branch_grad = pooled_grad.astype(bf16)
        down_local = jnp.einsum("rd,mrf->mdf", branch_grad, active, preferred_element_type=f32)
        active_grad = jnp.einsum("rd,mdf->mrf", branch_grad, weights[2], preferred_element_type=f32)
        slope = phi(upper) + upper * jnp.exp(-0.5 * upper * upper) * (1.0 / (2.0 * jnp.pi) ** 0.5)
        upper_grad = (active_grad * slope).astype(bf16)
        up_local = jnp.einsum("rd,mrf->mdf", normed_two, upper_grad, preferred_element_type=f32)
        normed_two_grad = jnp.einsum("mrf,mdf->rd", upper_grad, weights[1], preferred_element_type=f32)
        gain_two = jnp.sum(normed_two_grad * hat_two, axis=0)
        bias_two = jnp.sum(normed_two_grad, axis=0)
        hidden_grad = pooled_grad + norm_pull(normed_two_grad, hat_two, rstd_two, vectors[2])

        attended_grad = hidden_grad.astype(bf16)
        mixed_ends = mixed[:, ends]
        out_local = jnp.einsum("rd,mre->mde", attended_grad, mixed_ends, preferred_element_type=f32)
        mixed_grad = jnp.einsum("rd,mde->mre", attended_grad, out_t, preferred_element_type=f32).astype(bf16)
        mixed_grad = mixed_grad.reshape(mp_size, 2 * seqs, heads, HEAD_DIM)
        query_ends, keys, values = qkv[:, ends, 0], qkv[:, :, 1], qkv[:, :, 2]
        spot = jnp.arange(rows)
        allowed_ends = (
            (ids[ends][:, None] == ids[None, :])
            & (ends[:, None] // SEQ_LEN == spot[None, :] // SEQ_LEN)
            & (ends[:, None] >= spot[None, :])
        )[None, None]
        again = jnp.einsum("mqhc,mkhc->mhqk", query_ends, keys, preferred_element_type=f32) * scale
        probs_ends = jax.nn.softmax(jnp.where(allowed_ends, again, -1e30), axis=-1)
        probs_grad = jnp.einsum("mqhc,mkhc->mhqk", mixed_grad, values, preferred_element_type=f32)
        value_grad = jnp.einsum("mhqk,mqhc->mkhc", probs_ends.astype(bf16), mixed_grad, preferred_element_type=f32)
        centre = jnp.sum(probs_grad * probs_ends, axis=-1, keepdims=True)
        score_grad = (probs_ends * (probs_grad - centre)).astype(bf16)
        query_grad = jnp.einsum("mhqk,mkhc->mqhc", score_grad, keys, preferred_element_type=f32) * scale
        key_grad = jnp.einsum("mhqk,mqhc->mkhc", score_grad, query_ends, preferred_element_type=f32) * scale
        query_grad = query_grad.astype(bf16).reshape(mp_size, 2 * seqs, head_cols)
        query_grad = jnp.einsum("er,mec->mrc", place, query_grad, preferred_element_type=f32).astype(bf16)
        proj_grad = jnp.concatenate(
            [
                query_grad,
                key_grad.astype(bf16).reshape(mp_size, rows, head_cols),
                value_grad.astype(bf16).reshape(mp_size, rows, head_cols),
            ],
            axis=-1,
        )
        qkv_local = jnp.einsum("rd,mre->mde", normed, proj_grad, preferred_element_type=f32)
        normed_grad = jnp.einsum("mre,mde->rd", proj_grad, attn[:, :, : 3 * head_cols], preferred_element_type=f32)
        gain_one = jnp.sum(normed_grad * hat_one, axis=0)
        bias_one = jnp.sum(normed_grad, axis=0)
        token_grad = norm_pull(normed_grad, hat_one, rstd_one, vectors[0])
        token_grad = token_grad.at[ends].add(hidden_grad)

        local = jnp.stack([jnp.concatenate([qkv_local, out_local], axis=-1), up_local, down_local])
        local = local.reshape(3, mp_size, dp_size, depth, -1).transpose(2, 1, 0, 3, 4)
        local = local.reshape(dp_size * mp_size, 3, depth, -1)
        summed = lax.psum_scatter(local, both, scatter_dimension=0, tiled=False)
        vector_local = lax.psum(jnp.stack([gain_one, bias_one, gain_two, bias_two]), both)
        vector_own = lax.dynamic_slice_in_dim(vector_local, dp_rank * depth, depth, 1)

        block_out = lax.all_gather(block_out, "mp", axis=0, tiled=True)
        token_grad = lax.all_gather(token_grad, "mp", axis=0, tiled=True)
        qkv_grad = summed[0, :, : 3 * head_cols].reshape(depth, 3, head_cols).transpose(1, 0, 2)
        return (
            loss,
            block_out,
            token_grad,
            vector_own[0],
            vector_own[1],
            qkv_grad,
            summed[0, :, 3 * head_cols :].T,
            vector_own[2],
            vector_own[3],
            summed[1],
            summed[2].T,
        )

    return on_device


def solution(mesh):
    placed = (
        P("dp", None),
        P("dp"),
        P(("dp", "mp")),
        P("dp"),
        P("dp"),
        P(None, "dp", "mp"),
        P("mp", "dp"),
        P("dp"),
        P("dp"),
        P("dp", "mp"),
        P("mp", "dp"),
        P(("dp", "mp"), None),
        P(),
        P(),
        P(),
    )
    sizes = (mesh.shape["dp"], mesh.shape["mp"])
    return jax.shard_map(
        on_kernel if sizes == (8, 4) else make(*sizes),
        mesh=mesh,
        in_specs=placed,
        out_specs=(
            P(),
            P("dp", None),
            P("dp", None),
            P("dp"),
            P("dp"),
            P(None, "dp", "mp"),
            P("mp", "dp"),
            P("dp"),
            P("dp"),
            P("dp", "mp"),
            P("mp", "dp"),
        ),
        check_vma=False,
    )
```

```python
import jax
import jax.numpy as jnp
from jax import lax
from jax.sharding import PartitionSpec as P
import functools
from jax.experimental import pallas as pl
from jax.experimental.pallas import tpu as pltpu

HEAD_DIM = 64
SEQ_LEN = 16
norm_epsilon = 1e-05
unit_epsilon = 1e-06
logit_scale = 50.0
tile_rows = 128
f32, bf16 = jnp.float32, jnp.bfloat16


def standardise(values):
    centred = values - jnp.mean(values, axis=-1, keepdims=True)
    rstd = lax.rsqrt(jnp.mean(centred * centred, axis=-1, keepdims=True) + norm_epsilon)
    return centred * rstd, rstd


def norm_pull(grad, hat, rstd, gain):
    scaled = grad * gain
    first = jnp.mean(scaled, axis=-1, keepdims=True)
    second = jnp.mean(scaled * hat, axis=-1, keepdims=True)
    return rstd * (scaled - first - hat * second)


def inverse_norm(values):
    return lax.rsqrt(jnp.sum(values * values, axis=-1, keepdims=True) + unit_epsilon)


def nn(left, right):
    return lax.dot_general(left, right, (((1,), (0,)), ((), ())), preferred_element_type=f32)


def nt(left, right):
    return lax.dot_general(left, right, (((1,), (1,)), ((), ())), preferred_element_type=f32)


def tn(left, right):
    return lax.dot_general(left, right, (((0,), (0,)), ((), ())), preferred_element_type=f32)


def phi(values):
    return 0.5 * lax.erfc(-values * (0.5**0.5))


MESH = pl.DeviceIdType.MESH
VMEM, DMA = pltpu.VMEM, pltpu.SemaphoreType.DMA
CUT = 48
WINDOW = 3


def loop(count, body):
    lax.fori_loop(0, count, lambda i, carry: (body(i), carry)[1], 0)


def rows_of(index, size):
    return pl.ds(pl.multiple_of(index * size, size), size)


def split_three(values):
    first = values.astype(bf16)
    rest = values - first.astype(f32)
    second = rest.astype(bf16)
    return first, second, (rest - second.astype(f32)).astype(bf16)


def pick(place, values):
    return sum(nn(place, part) for part in split_three(values))


def spread_rows(place, values):
    return sum(tn(place, part) for part in split_three(values))


def half_erf(values):
    return 0.5 + 0.5 * lax.erf(values * (0.5**0.5))


def layer_kernel(slot_total, *refs):
    (w_qkv, w_out, up_own, down_own, norms, valid_own, classes, image_gain, image_bias, image_proj, tokens, ids) = refs[:12]
    (loss_out, block_out, token_out, attn_out, up_out, down_out, vec_out) = refs[12:19]
    (w_attn, w_up, w_down, images, smalls, x_ref, a_ref, qkv, hidden, a_two, active, stage_out, image_own, vecs) = refs[19:33]
    (mask_ref, place_ref, member_ref, h_ends, ends_two, ends_grad, u_ends, g_all, s_all, weight_ref, valid_ref) = refs[33:44]
    (sum_own, sum_buf, sum_got, d_attn, d_far) = refs[44:49]
    (grad_down, grad_up, grad_attn, step_x, step_z, attn_send, attn_core, ends_back) = refs[49:57]
    (vec_buf, vec_pack, vec_got, stage_grad, attn_own, small_own, far_mix) = refs[57:64]
    gsems = refs[64:92]
    isems = refs[92:101]
    (s_local, s_bo, s_on, s_send, s_a2, s_dm, s_dh, s_sum, s_sums, s_x, s_z, s_core, s_v, s_vs, s_tg, s_exs) = refs[101:117]

    dp = lax.axis_index("dp")
    mp = lax.axis_index("mp")
    z = lax.div(dp, 2)
    x = lax.rem(dp, 2)
    y = lax.div(mp, 2)
    c = lax.rem(mp, 2)
    xd, ym, cm = 2 * z + (1 - x), 2 * (1 - y) + c, 2 * y + (1 - c)
    zt = [lax.rem(z + j, 4) for j in range(4)]
    zs = [lax.rem(z + 4 - j, 4) for j in range(4)]
    X, Y, C, YC = (xd, mp), (dp, ym), (dp, cm), (dp, 3 - mp)
    Z = [(2 * zt[j] + x, mp) for j in range(4)]
    here = 4 * x + mp
    PLANE = []
    for j in range(1, 8):
        other = lax.rem(here + j, 8)
        PLANE.append((2 * z + lax.div(other, 4), lax.rem(other, 4)))
    G = [(dp, lax.rem(mp + j, 4)) for j in range(4)]

    peers = PLANE + Z[1:]
    barrier = pltpu.get_barrier_semaphore()
    for peer in peers:
        pl.semaphore_signal(barrier, inc=1, device_id=peer, device_id_type=MESH)
    pl.semaphore_wait(barrier, len(peers))

    def remote(src, dst, send_sem, recv_sem, device):
        copy = pltpu.make_async_remote_copy(
            src_ref=src, dst_ref=dst, send_sem=send_sem, recv_sem=recv_sem, device_id=device, device_id_type=MESH
        )
        copy.start()
        return copy

    def arrived(ref, recv_sem, send_sem):
        pltpu.make_async_remote_copy(
            src_ref=ref, dst_ref=ref, send_sem=send_sem, recv_sem=recv_sem, device_id=X, device_id_type=MESH
        ).wait_recv()

    def gather_steps(src, out, rows, cut, sems):
        zr, x0, y1, y0, x1, cr, sd = sems
        first = (0, cut) if cut else (0, rows)
        second = (cut, rows - cut) if cut else None
        full = (0, rows)

        def piece(d, m, span):
            return out.at[m, pl.ds(pl.multiple_of(d * rows + span[0], 16), span[1])]

        def send(src_ref, dst_ref, sem, device):
            remote(src_ref, dst_ref, sd.at[0], sem, device)

        def got(ref, sem):
            arrived(ref, sem, sd.at[0])

        def step0():
            for j in range(1, 4):
                send(src, piece(dp, mp, full), zr.at[j], Z[j])
            send(src.at[pl.ds(*first)], piece(dp, mp, first), x0.at[0], X)
            if second:
                send(src.at[pl.ds(*second)], piece(dp, mp, second), y1.at[0], Y)
            send(src.at[pl.ds(*first)], piece(dp, mp, first), y0.at[0], Y)
            if second:
                send(src.at[pl.ds(*second)], piece(dp, mp, second), x1.at[0], X)
            send(src, piece(dp, mp, full), cr.at[0], C)
            pltpu.make_async_copy(src, piece(dp, mp, full), sd.at[0]).start()
            yield

        def step1():
            for j in range(1, 4):
                d = 2 * zs[j] + x
                block = piece(d, mp, full)
                got(block, zr.at[j])
                one = piece(d, mp, first)
                send(one, one, x0.at[j], X)
                if second:
                    two = piece(d, mp, second)
                    send(two, two, y1.at[j], Y)
                send(one, one, y0.at[j], Y)
                if second:
                    send(two, two, x1.at[j], X)
                send(block, block, cr.at[0], C)
                yield

        def step2():
            for j in range(4):
                one = piece(2 * zs[j] + (1 - x), mp, first)
                got(one, x0.at[j])
                send(one, one, y0.at[4 + j], Y)
                send(one, one, cr.at[0], C)
                if second:
                    two = piece(2 * zs[j] + x, ym, second)
                    got(two, y1.at[j])
                    send(two, two, x1.at[4 + j], X)
                    send(two, two, cr.at[0], C)
                yield

        def step3():
            for i in range(2):
                for j in range(4):
                    one = piece(2 * zs[j] + (x if i == 0 else 1 - x), ym, first)
                    got(one, y0.at[4 * i + j])
                    send(one, one, cr.at[0], C)
                    if second:
                        two = piece(2 * zs[j] + (1 - x), (mp if i == 0 else ym), second)
                        got(two, x1.at[4 * i + j])
                        send(two, two, cr.at[0], C)
                    yield

        def step4():
            half = out.at[pl.ds(0, 2)]
            pltpu.make_async_copy(half, half, cr.at[0]).wait()
            pltpu.make_async_copy(out, out, sd.at[0]).wait()
            yield

        return [step0, step1, step2, step3, step4]

    depth = up_own.shape[0]
    slots = classes.shape[0]

    def image_steps():
        near, cross, core, near_sent, core_sent, up_got, down_got, up_sent, down_sent = isems

        def at(d, m, start=0, size=slots):
            return images.at[m, pl.ds(pl.multiple_of(d * slots + start, 16), size)]

        def plane(z_, i):
            return images.at[2 * i + c, pl.ds(pl.multiple_of(2 * z_ * slots, 16), 2 * slots)]

        def to_core(ref):
            remote(ref, ref, core_sent.at[0], core.at[0], C)

        half = slots // 2

        def step0():
            remote(image_own, at(dp, mp), near_sent.at[0], near.at[0], X)
            remote(image_own, at(dp, mp), near_sent.at[0], near.at[1], Y)
            remote(image_own, at(dp, mp), core_sent.at[0], core.at[0], C)
            pltpu.make_async_copy(image_own, at(dp, mp), s_local.at[5]).start()
            yield

        def step1():
            arrived(at(xd, mp), near.at[0], near_sent.at[0])
            remote(at(xd, mp, 0, half), at(xd, mp, 0, half), near_sent.at[0], cross.at[0], Y)
            to_core(at(xd, mp))
            arrived(at(dp, ym), near.at[1], near_sent.at[0])
            remote(at(dp, ym, half, half), at(dp, ym, half, half), near_sent.at[0], cross.at[1], X)
            to_core(at(dp, ym))
            yield

        def up(i, t):
            ref = plane(z - t, i)
            return pltpu.make_async_remote_copy(
                src_ref=ref, dst_ref=ref, send_sem=up_sent.at[t, i], recv_sem=up_got.at[t, i],
                device_id=(2 * (z + 1) + x, mp), device_id_type=MESH,
            )

        def down(i, t):
            ref = plane(z + t, i)
            return pltpu.make_async_remote_copy(
                src_ref=ref, dst_ref=ref, send_sem=down_sent.at[t, i], recv_sem=down_got.at[t, i],
                device_id=(2 * (z - 1) + x, mp), device_id_type=MESH,
            )

        def step2():
            arrived(at(xd, ym, 0, half), cross.at[0], near_sent.at[0])
            arrived(at(xd, ym, half, half), cross.at[1], near_sent.at[0])
            to_core(at(xd, ym))
            pltpu.make_async_copy(image_own, at(dp, mp), s_local.at[5]).wait()
            for i in range(2):
                pl.when(z < 3)(lambda i=i: up(i, 0).start())
                pl.when(z > 0)(lambda i=i: down(i, 0).start())
            yield

        def step3():
            for t in range(1, 4):
                for i in range(2):

                    def from_below(i=i, t=t):
                        ref = plane(z - t, i)
                        arrived(ref, up_got.at[t - 1, i], near_sent.at[0])
                        if t < 3:
                            pl.when(z < 3)(lambda: up(i, t).start())
                        to_core(ref)

                    def from_above(i=i, t=t):
                        ref = plane(z + t, i)
                        arrived(ref, down_got.at[t - 1, i], near_sent.at[0])
                        if t < 3:
                            pl.when(z > 0)(lambda: down(i, t).start())
                        to_core(ref)

                    pl.when(z >= t)(from_below)
                    pl.when(z + t <= 3)(from_above)
                    yield

        def step4():
            halves = images.at[pl.ds(0, 2)]
            pltpu.make_async_copy(halves, halves, core.at[0]).wait()
            pltpu.make_async_copy(halves, halves, core_sent.at[0]).wait()
            three = images.at[0, pl.ds(0, 3 * slots)]
            pltpu.make_async_copy(three, three, near_sent.at[0]).wait()
            for t in range(3):
                for i in range(2):
                    pl.when((z >= t) & (z < 3))(lambda i=i, t=t: up(i, t).wait_send())
                    pl.when((z + t <= 3) & (z > 0))(lambda i=i, t=t: down(i, t).wait_send())
            yield

        return [step0, step1, step2, step3, step4]

    kinds = {
        "S": gather_steps(small_own, smalls, 16, 0, gsems[0:7]),
        "A": gather_steps(attn_own, w_attn, depth, CUT, gsems[7:14]),
        "U": gather_steps(up_own, w_up, depth, CUT, gsems[14:21]),
        "D": gather_steps(down_own, w_down, depth, CUT, gsems[21:28]),
        "I": image_steps(),
    }

    def run(*steps):
        for name in steps:
            for _ in kinds[name[0]][int(name[1])]():
                pass

    def blend(steps, chunks):
        chunks = list(chunks)
        micro = [kinds[name[0]][int(name[1])] for name in steps]
        count = sum((1, 3, 4, 8, 1)[int(name[1])] if name[0] != "I" else (1, 1, 1, 6, 1)[int(name[1])] for name in steps)
        done, at = 0, 0
        for step in micro:
            for _ in step():
                at += 1
                while done < len(chunks) and done * count < at * len(chunks):
                    chunks[done]()
                    done += 1
        for chunk in chunks[done:]:
            chunk()

    lane = lax.broadcasted_iota(jnp.int32, (128, 128), 1)
    sub = lax.broadcasted_iota(jnp.int32, (128, 128), 0)
    low = lax.broadcasted_iota(jnp.int32, (1, 128), 1) < 64
    token_rows = hidden.shape[0]
    tiles = token_rows // 128
    end_count = h_ends.shape[0]

    def keep_low(values):
        return jnp.where(low, values, jnp.zeros_like(values))

    def keep_high(values):
        return jnp.where(low, jnp.zeros_like(values), values)

    def pack_own():
        rows = lax.broadcasted_iota(jnp.int32, (depth, depth), 0)
        eye = (rows == lax.broadcasted_iota(jnp.int32, (depth, depth), 1)).astype(f32).astype(bf16)
        out_t = nt(eye, w_out[...]).astype(bf16)
        query, key, value = w_qkv[0], w_qkv[1], w_qkv[2]
        attn_own[:, 0:128] = query[:, 0:128]
        attn_own[:, 128:256] = key[:, 0:128]
        attn_own[:, 256:384] = value[:, 0:128]
        attn_own[:, 384:512] = jnp.concatenate([query[:, 128:192], value[:, 128:192]], axis=1)
        attn_own[:, 512:640] = jnp.concatenate([key[:, 128:192], out_t[:, 128:192]], axis=1)
        attn_own[:, 640:768] = out_t[:, 0:128]

    def pack_small():
        shift = lax.broadcasted_iota(jnp.int32, (depth, 384), 1) - lax.broadcasted_iota(jnp.int32, (depth, 384), 0)
        made = nn(norms[...], (shift == depth * lax.rem(dp, 4)).astype(f32).astype(bf16))
        shift = lax.broadcasted_iota(jnp.int32, (slots, 128), 1) - lax.broadcasted_iota(jnp.int32, (slots, 128), 0)
        flags = jnp.broadcast_to(valid_own[...].astype(f32), (8, slots)).astype(bf16)
        flags = nn(flags, (shift == slots * lax.rem(dp, 2)).astype(f32).astype(bf16))
        parts = [made[v : v + 1, 128 * t : 128 * (t + 1)] for v in range(4) for t in range(3)]
        small_own[...] = jnp.concatenate(parts + [flags[0:4, :]], axis=0).astype(bf16)

    def masks(g):
        slot_row = lax.broadcasted_iota(jnp.int32, (end_count, 128), 0)
        spots = []
        best = jnp.full((end_count, 1), -1, jnp.int32)
        for b in range(tiles):
            sequence = 8 * b + lax.shift_right_logical(lax.broadcasted_iota(jnp.int32, (1, 128), 1), 4)
            caption = 2 * sequence + ids[ym if g else mp, pl.ds(b, 1), :]
            column = jnp.sum(jnp.where(lane == sub, caption, 0), axis=1, keepdims=True)
            mask_ref[tiles * g + b] = jnp.where((column == caption) & (sub >= lane), 0.0, -1e30)
            member = slot_row == caption
            spot = lax.broadcasted_iota(jnp.int32, (end_count, 128), 1) + 128 * b
            best = jnp.maximum(best, jnp.max(jnp.where(member, spot, -1), axis=1, keepdims=True))
            member_ref[g, :, 128 * b : 128 * (b + 1)] = jnp.where(member, 0.0, -1e30)
            spots.append(spot)
        for b in range(tiles):
            place_ref[g, :, 128 * b : 128 * (b + 1)] = (spots[b] == best).astype(f32).astype(bf16)

    def image_tower():
        hat, _ = standardise(classes[...].astype(f32))
        raw = nn((hat * image_gain[...].reshape(1, -1) + image_bias[...].reshape(1, -1)).astype(bf16), image_proj[...])
        image_own[...] = (raw * inverse_norm(raw)).astype(bf16)

    def small_vectors():
        halves = []
        for w in range(2):
            halves.append(sum(smalls[0, 64 * w + 16 * d : 64 * w + 16 * (d + 1), :].astype(f32) for d in range(4)))
        for v in range(4):
            for w in range(2):
                for t in range(3):
                    at = 384 * w + 128 * t
                    vecs[v : v + 1, at : at + 128] = halves[w][3 * v + t : 3 * v + t + 1, :]
        for m in range(4):
            for pair in range(4):
                both = sum(smalls[m, 32 * pair + 16 * d : 32 * pair + 16 * (d + 1), :].astype(f32) for d in range(2))
                valid_ref[m : m + 1, 128 * pair : 128 * (pair + 1)] = both[12:13, :]

    def first_norm(g):
        def body(b):
            rows = rows_of(tiles * g + b, 128)
            values = x_ref[rows, :].astype(f32)
            hat, _ = standardise(values)
            a_ref[rows, :] = (hat * vecs[0:1, :] + vecs[1:2, :]).astype(bf16)
            if g == 0:
                hidden[rows, :] = values

        loop(tiles, body)

    def soft(scores):
        top = jnp.max(scores, axis=-1, keepdims=True)
        raised = jnp.exp(scores - top)
        return raised * (1.0 / jnp.sum(raised, axis=-1, keepdims=True))

    scale = HEAD_DIM**-0.5

    def project(m, g):
        def body(b):
            rows = rows_of(2 * g + b, 256)
            qkv[m, rows, :] = nn(a_ref[rows, :], w_attn[m]).astype(bf16)

        loop(2, body)

    def attention(m):
        project(m, 0)

        def body(pair):
            for b in (2 * pair, 2 * pair + 1):
                rows = rows_of(b, 128)
                q01, k01, v01, qv, ko = (qkv[m, rows, 128 * i : 128 * (i + 1)] for i in range(5))
                mask = mask_ref[b]
                p0 = soft(nt(keep_low(q01), k01) * scale + mask).astype(bf16)
                p1 = soft(nt(keep_high(q01), k01) * scale + mask).astype(bf16)
                p2 = soft(nt(keep_low(qv), ko) * scale + mask).astype(bf16)
                o01 = jnp.where(low, nn(p0, v01), nn(p1, v01)).astype(bf16)
                o2 = keep_high(nn(p2, qv)).astype(bf16)
                qkv[m, rows, 512:640] = keep_low(ko) + o2
                qkv[m, rows, 640:768] = o01

        loop(tiles // 2, body)

        def attended(b):
            rows = rows_of(b, 256)
            mixed = jnp.concatenate([keep_high(qkv[m, rows, 512:640]), qkv[m, rows, 640:768]], axis=1)
            hidden[rows, :] += nt(mixed, w_attn[m, :, 512:768])

        loop(2, attended)

    def second_norm():
        def body(b):
            rows = rows_of(b, 128)
            hat, _ = standardise(hidden[rows, :])
            a_two[rows, :] = (hat * vecs[2:3, :] + vecs[3:4, :]).astype(bf16)

        loop(tiles, body)
        place = place_ref[0]
        ends = pick(place, hidden[...])
        h_ends[...] = ends
        hat, _ = standardise(ends)
        ends_two[mp] = (hat * vecs[2:3, :] + vecs[3:4, :]).astype(bf16)

    def ends_up(m):
        u_ends[m] = nn(ends_two[mp], w_up[m])

    def full_up(m):
        def body(b):
            rows = rows_of(b, 256)
            upper = nn(a_two[rows, :], w_up[m])
            active[m, rows, :] = (upper * half_erf(upper)).astype(bf16)

        loop(tiles // 2, body)

    def slope_of(upper):
        return half_erf(upper) + upper * jnp.exp(-0.5 * upper * upper) * (1.0 / (2.0 * jnp.pi) ** 0.5)

    def group_up():
        def body(i):
            upper = nn(ends_two[i], w_up[mp])
            rows = rows_of(i, end_count)
            g_all[rows, :] = (upper * half_erf(upper)).astype(bf16)
            s_all[rows, :] = slope_of(upper)

        loop(4, body)

    def full_down(b):
        rows = slice(256 * b, 256 * (b + 1))

        def body(m, total):
            return total + nt(active[m, rows, :], w_down[m])

        stage_out[rows, :] = lax.fori_loop(0, 4, body, hidden[rows, :]).astype(bf16)

    token_copies = []
    for g in range(2):
        wanted = tokens.at[rows_of(ym if g else mp, token_rows)]
        token_copies.append(pltpu.make_async_copy(wanted, x_ref.at[pl.ds(g * token_rows, token_rows)], s_local.at[g]))
        token_copies[g].start()
    pack_small()
    run("S0")
    pack_own()
    run("A0")
    image_tower()
    run("I0", "U0")
    masks(0)
    masks(1)
    run("S1", "A1", "D0", "I1", "S2", "A2", "I2", "U1", "S3", "S4")
    small_vectors()
    for g in range(2):
        token_copies[g].wait()
        first_norm(g)
    run("D1", "A3", "A4")
    blend(("U2", "I3", "D2", "U3"), [functools.partial(attention, m) for m in range(4)])
    second_norm()
    swaps = [remote(ends_two.at[mp], ends_two.at[mp], s_exs.at[j - 1], s_a2.at[j - 1], G[j]) for j in range(1, 4)]
    run("U4")
    blend(
        ("D3",),
        [functools.partial(full_up, m) for m in range(4)] + [functools.partial(project, m, 1) for m in range(4)],
    )
    loop(4, ends_up)
    run("I4")
    for swap in swaps:
        swap.wait()
    group_up()
    run("D4")

    pooled = h_ends[...]
    for m in range(4):
        upper = u_ends[m]
        pooled = pooled + nt((upper * half_erf(upper)).astype(bf16), w_down[m])
    scale_back = inverse_norm(pooled)
    text = (pooled * scale_back).astype(bf16)
    own_valid = small_own[12:13, :].astype(f32)
    own_valid = jnp.max(
        jnp.where(
            lax.rem(lax.broadcasted_iota(jnp.int32, (slots, 128), 1), slots)
            == lax.broadcasted_iota(jnp.int32, (slots, 128), 0),
            own_valid,
            0.0,
        ),
        axis=1,
        keepdims=True,
    )
    live = own_valid > 0.0
    place_col = lax.broadcasted_iota(jnp.int32, (slots, 512), 1)
    place_row = lax.broadcasted_iota(jnp.int32, (slots, 512), 0)

    def target_of(m):
        return (place_col == place_row + dp * slots) & (mp == m)

    row_sum = jnp.zeros((slots, 1), f32)
    matched = jnp.zeros((slots, 1), f32)
    for m in range(4):
        logits = logit_scale * nt(text, images[m])
        weight = jnp.exp(logits)
        matched = matched + jnp.sum(jnp.where(target_of(m), logits, 0.0), axis=1, keepdims=True)
        seen = jnp.where(valid_ref[m : m + 1, :] > 0.0, weight, 0.0)
        weight_ref[m] = seen
        row_sum = row_sum + jnp.sum(seen, axis=1, keepdims=True)
        columns = jnp.sum(jnp.where(live, weight, 0.0), axis=0, keepdims=True)
        for part in range(4):
            sum_own[4 * m + part : 4 * m + part + 1, :] = columns[:, 128 * part : 128 * (part + 1)]
    row_part = jnp.sum(jnp.where(live, jnp.log(row_sum) - 2.0 * matched, 0.0), axis=0, keepdims=True)
    sum_own[16:24, :] = jnp.broadcast_to(row_part, (8, 128))

    swaps = [remote(sum_own, sum_got.at[here], s_sums.at[j - 1], s_sum.at[j - 1], PLANE[j - 1]) for j in range(1, 8)]
    sum_got[here] = sum_own[...]
    full_down(0)
    for swap in swaps:
        swap.wait()
    sum_buf[...] = ((sum_got[0] + sum_got[1]) + (sum_got[2] + sum_got[3])) + (
        (sum_got[4] + sum_got[5]) + (sum_got[6] + sum_got[7])
    )
    swaps = [remote(sum_buf, sum_got.at[8 + z], s_sums.at[6 + j], s_sum.at[6 + j], Z[j]) for j in range(1, 4)]
    sum_got[8 + z] = sum_buf[...]
    full_down(1)
    for swap in swaps:
        swap.wait()
    sums = (sum_got[8] + sum_got[9]) + (sum_got[10] + sum_got[11])

    total = sums[16:17, 0:1]
    unit_grad = jnp.zeros((slots, text.shape[1]), f32)
    for m in range(4):
        columns = jnp.concatenate([sums[4 * m + part : 4 * m + part + 1, :] for part in range(4)], axis=1)
        seen = valid_ref[m : m + 1, :] > 0.0
        total = total + jnp.sum(jnp.where(seen, jnp.log(columns), 0.0), axis=1, keepdims=True)
        spread = 0.5 * weight_ref[m] * (1.0 / row_sum + 1.0 / columns)
        grad = jnp.where(seen & live, spread, 0.0) - jnp.where(target_of(m) & live, 1.0, 0.0)
        unit_grad = unit_grad + nn((logit_scale * grad).astype(bf16), images[m])
    loss_out[...] = total * (0.5 / slot_total)
    along = jnp.sum(unit_grad * pooled, axis=-1, keepdims=True)
    pooled_grad = scale_back * unit_grad - pooled * (scale_back * scale_back * scale_back * along)
    branch_grad = pooled_grad.astype(bf16)
    ends_grad[mp] = branch_grad
    swaps = [remote(ends_grad.at[mp], ends_grad.at[mp], s_exs.at[2 + j], s_dm.at[j - 1], G[j]) for j in range(1, 4)]

    def two_part(m):
        upper_grad = (nn(branch_grad, w_down[m]) * slope_of(u_ends[m])).astype(bf16)
        return nt(upper_grad, w_up[m])

    two_grad = two_part(0) + two_part(1)

    def block(z_, x_):
        return pl.ds(pl.multiple_of((2 * z_ + x_) * depth, 16), depth)

    grads, outs = [grad_down, grad_up, grad_attn], [down_out, up_out, attn_out]

    order = [(k, j) for k in range(3) for j in (2, 1, 3, 0)]
    sent, added = iter(order), iter(order)

    def sum_start(count):
        for _ in range(count):
            k, j = next(sent, (None, None))
            if k is not None:
                remote(grads[k].at[block(zt[j], 1 - x)], step_x.at[k, j], s_send.at[k], s_x.at[k, j], X)

    def sum_add(k, j):
        arrived(step_x.at[k, j], s_x.at[k, j], s_send.at[k])
        mine = block(zt[j], x)
        summed = grads[k][mine, :].astype(f32) + step_x[k, j].astype(f32)
        if j:
            grads[k][mine, :] = summed.astype(bf16)
            remote(grads[k].at[mine], step_z.at[k, j - 1], s_send.at[k], s_z.at[k, j - 1], Z[j])
        else:
            outs[k][...] = summed

    def sum_end(k):
        for j in range(1, 4):
            arrived(step_z.at[k, j - 1], s_z.at[k, j - 1], s_send.at[k])
        outs[k][...] = outs[k][...] + step_z[k, 0].astype(f32) + step_z[k, 1].astype(f32) + step_z[k, 2].astype(f32)
        sent = grads[k].at[pl.ds(0, 7 * depth)]
        pltpu.make_async_copy(sent, sent, s_send.at[k]).wait()

    def sum_some(count):
        for _ in range(count):
            sum_start(1)
            sum_add(*next(added))

    for swap in swaps:
        swap.wait()
    group_grad = ends_grad[...].reshape(4 * end_count, -1)
    upper_grad = (nn(group_grad, w_down[mp]) * s_all[...]).astype(bf16)
    grad_down[...] = tn(group_grad, g_all[...]).astype(bf16)

    sum_start(WINDOW)
    grad_up[...] = tn(ends_two[...].reshape(4 * end_count, -1), upper_grad).astype(bf16)

    two_grad = two_grad + two_part(2) + two_part(3)
    hat_two, rstd_two = standardise(h_ends[...])
    vec_buf[...] = jnp.zeros_like(vec_buf)
    vec_buf[2:3, :] = jnp.sum(two_grad * hat_two, axis=0, keepdims=True)
    vec_buf[3:4, :] = jnp.sum(two_grad, axis=0, keepdims=True)
    hidden_grad = pooled_grad + norm_pull(two_grad, hat_two, rstd_two, vecs[2:3, :])
    ends_back[0] = hidden_grad.astype(bf16)
    back_swap = remote(ends_back.at[0], ends_back.at[1], s_exs.at[6], s_dh.at[0], Y)

    def attention_back(m, g, mix=False):
        place = place_ref[g]
        member = member_ref[g]
        ends_row = ends_back[g]
        span = slice(token_rows * g, token_rows * (g + 1))
        k01, v01, qv, ko = (qkv[m, span, 128 * i : 128 * (i + 1)] for i in range(1, 5))
        q_e = nn(place, qkv[m, span, 0:128]).astype(bf16)
        q2_e = keep_low(nn(place, qv)).astype(bf16)
        do01 = nn(ends_row, w_attn[m, :, 640:768]).astype(bf16)
        do2 = keep_high(nn(ends_row, w_attn[m, :, 512:640])).astype(bf16)

        def head(query, keys, values, outer):
            probs = soft(nt(query, keys) * scale + member)
            probs_grad = nt(outer, values)
            centre = jnp.sum(probs_grad * probs, axis=-1, keepdims=True)
            return probs.astype(bf16), (probs * (probs_grad - centre)).astype(bf16)

        p0, ds0 = head(keep_low(q_e), k01, v01, keep_low(do01))
        p1, ds1 = head(keep_high(q_e), k01, v01, keep_high(do01))
        p2, ds2 = head(q2_e, ko, qv, do2)
        dq01 = (jnp.where(low, nn(ds0, k01), nn(ds1, k01)) * scale).astype(bf16)
        dq2 = keep_low(nn(ds2, ko) * scale).astype(bf16)
        if g == 1 and mix:
            far_mix[:, 0:128] = nn(p2, qv).astype(bf16)
            far_mix[:, 128:256] = jnp.where(low, nn(p0, v01), nn(p1, v01)).astype(bf16)
        d_ref = d_far if g else active
        d_ref[m, :, 0:128] = tn(place, dq01).astype(bf16)
        d_ref[m, :, 128:256] = (jnp.where(low, tn(ds0, q_e), tn(ds1, q_e)) * scale).astype(bf16)
        d_ref[m, :, 256:384] = jnp.where(low, tn(p0, do01), tn(p1, do01)).astype(bf16)
        d_ref[m, :, 384:512] = jnp.where(low, tn(place, dq2), tn(p2, do2)).astype(bf16)
        d_ref[m, :, 512:640] = keep_low(tn(ds2, q2_e) * scale).astype(bf16)

    def token_back(g):
        d_ref = d_far if g else active

        def body(b):
            rows = rows_of(b, 256)
            total = jnp.zeros((256, d_attn.shape[1]), f32)
            for m in range(4):
                total = total + nt(d_ref[m, rows, 0:640], w_attn[m, :, 0:640])
            d_attn[rows_of(2 * g + b, 256), :] = total

        loop(2, body)

    def attn_grad(m):
        ends_mix = nn(place_ref[0], qkv[m, 0:token_rows, 512:768]).astype(bf16)
        outer = tn(ends_back[0], ends_mix) + tn(ends_back[1], far_mix[...])

        def made(start, stop):
            span = slice(start, stop)
            return tn(a_ref[0:token_rows, :], active[m, :, span]) + tn(a_ref[token_rows:, :], d_far[m, :, span])

        last = jnp.where(low, made(512, 640), outer[:, 0:128])
        return jnp.concatenate([made(0, 512), last, outer[:, 128:256]], axis=1)

    back_swap.wait()
    own_rows = rows_of(mp, token_rows)
    far_rows = rows_of(ym, token_rows)
    out_swaps = [
        remote(stage_out, block_out.at[own_rows], s_bo.at[0], s_bo.at[1], Y),
        remote(stage_out, block_out.at[own_rows], s_bo.at[2], s_bo.at[3], C),
    ]
    keep_out = pltpu.make_async_copy(stage_out, block_out.at[own_rows], s_local.at[2])
    keep_out.start()

    m = 2 * y + (1 - c)
    attention_back(m, 0, True)
    attention_back(m, 1, True)
    attn_send[...] = attn_grad(m).astype(bf16)
    core_swap = remote(attn_send, attn_core, s_exs.at[7], s_core.at[0], C)
    sum_some(1)
    m = 2 * y + c
    attention_back(m, 0, True)
    attention_back(m, 1, True)
    sum_some(1)
    made = attn_grad(m)
    core_swap.wait()
    grad_attn[...] = (made + attn_core[...].astype(f32)).astype(bf16)
    sum_some(1)
    for i in range(2):
        for g in range(2):
            attention_back(2 * (1 - y) + i, g)
    sum_some(1)

    def token_end(g):
        def body(b):
            rows = rows_of(tiles * g + b, 128)
            hat, rstd = standardise(x_ref[rows, :].astype(f32))
            grad = d_attn[rows, :]
            if g == 0:
                vec_buf[0:1, :] += jnp.sum(grad * hat, axis=0, keepdims=True)
                vec_buf[1:2, :] += jnp.sum(grad, axis=0, keepdims=True)
            d_attn[rows, :] = norm_pull(grad, hat, rstd, vecs[0:1, :])

        loop(tiles, body)
        span = slice(token_rows * g, token_rows * (g + 1))
        stage_grad[span, :] = (d_attn[span, :] + tn(place_ref[g], ends_back[g])).astype(bf16)

    grad_swaps, keep_grads = [], []
    out_swaps[0].wait()
    on = remote(block_out.at[far_rows], block_out.at[far_rows], s_on.at[0], s_on.at[1], C)
    for g in range(2):
        token_back(g)
        sum_some(g)
        token_end(g)
        if g == 0:
            for v in range(4):
                for t in range(6):
                    vec_pack[0, 6 * v + t : 6 * v + t + 1, :] = vec_buf[v : v + 1, 128 * t : 128 * (t + 1)]
            core_vec = remote(vec_pack.at[0], vec_got.at[0], s_vs.at[0], s_v.at[0], C)
        ref = stage_grad.at[pl.ds(token_rows * g, token_rows)]
        spot = token_out.at[far_rows if g else own_rows]
        grad_swaps.append(remote(ref, spot, s_tg.at[2 * g], s_tg.at[2 * g + 1], C))
        keep_grads.append(pltpu.make_async_copy(ref, spot, s_local.at[3 + g]))
        keep_grads[g].start()
        if g == 0:
            sum_some(1)
    core_vec.wait()
    vec_pack[1] = vec_pack[0] + vec_got[0]
    across = [X, Y, (2 * z + (1 - x), ym)]
    vec_swaps = [
        remote(vec_pack.at[1], vec_got.at[1 + 2 * y + x], s_vs.at[1 + j], s_v.at[1 + j], across[j]) for j in range(3)
    ]
    vec_got[1 + 2 * y + x] = vec_pack[1]
    sum_some(1)
    for swap in vec_swaps:
        swap.wait()
    vec_pack[2] = (vec_got[1] + vec_got[2]) + (vec_got[3] + vec_got[4])
    vec_swaps = [
        remote(vec_pack.at[2], vec_got.at[5 + z], s_vs.at[3 + j], s_v.at[3 + j], Z[j]) for j in range(1, 4)
    ]
    vec_got[5 + z] = vec_pack[2]
    sum_some(1)
    for swap in vec_swaps:
        swap.wait()
    total = (vec_got[5] + vec_got[6]) + (vec_got[7] + vec_got[8])
    for v in range(4):
        for t in range(6):
            vec_out[v : v + 1, 128 * t : 128 * (t + 1)] = total[6 * v + t : 6 * v + t + 1, :]
    sum_end(0)
    sum_some(4)
    sum_end(1)
    sum_end(2)
    out_swaps[1].wait()
    on.wait()
    keep_out.wait()
    for swap in grad_swaps + keep_grads:
        swap.wait()


def layer(slot_total, w_qkv, w_out, up_own, down_own, norms, valid, classes, *rest):
    depth, width = up_own.shape
    slots = classes.shape[0]
    rows = rest[3].shape[0] // 4

    def gather_sems():
        return [DMA((4,)), DMA((4,)), DMA((4,)), DMA((8,)), DMA((8,)), DMA((1,)), DMA((1,))]

    here, there = pl.BlockSpec(memory_space=VMEM), pl.BlockSpec(memory_space=pltpu.HBM)
    square = VMEM((4, width, width), bf16)
    scratch = [
        square,
        square,
        square,
        VMEM((4, 8 * slots, width), bf16),
        VMEM((4, 128, 128), bf16),
        VMEM((2 * rows, width), bf16),
        VMEM((2 * rows, width), bf16),
        VMEM((4, 2 * rows, width), bf16),
        VMEM((rows, width), f32),
        VMEM((rows, width), bf16),
        VMEM((4, rows, width), bf16),
        VMEM((rows, width), bf16),
        VMEM((slots, width), bf16),
        VMEM((8, width), f32),
        VMEM((2 * rows // 128, 128, 128), f32),
        VMEM((2, slots, rows), bf16),
        VMEM((2, slots, rows), f32),
        VMEM((slots, width), f32),
        VMEM((4, slots, width), bf16),
        VMEM((4, slots, width), bf16),
        VMEM((4, slots, width), f32),
        VMEM((4 * slots, width), bf16),
        VMEM((4 * slots, width), f32),
        VMEM((4, slots, 8 * slots), f32),
        VMEM((8, 8 * slots), f32),
        VMEM((24, 128), f32),
        VMEM((24, 128), f32),
        VMEM((12, 24, 128), f32),
        VMEM((2 * rows, width), f32),
        VMEM((4, rows, 640), bf16),
        VMEM((width, width), bf16),
        VMEM((width, width), bf16),
        VMEM((width, width), bf16),
        VMEM((3, 4, depth, width), bf16),
        VMEM((3, 3, depth, width), bf16),
        VMEM((width, width), bf16),
        VMEM((width, width), bf16),
        VMEM((2, slots, width), bf16),
        VMEM((8, width), f32),
        VMEM((3, 24, 128), f32),
        VMEM((9, 24, 128), f32),
        VMEM((2 * rows, width), bf16),
        VMEM((depth, width), bf16),
        VMEM((16, 128), bf16),
        VMEM((slots, 256), bf16),
    ]
    for _ in range(4):
        scratch += gather_sems()
    scratch += [DMA((2,)), DMA((2,)), DMA((1,)), DMA((1,)), DMA((1,)), DMA((3, 2)), DMA((3, 2)), DMA((3, 2)), DMA((3, 2))]
    scratch += [DMA((6,)), DMA((4,)), DMA((2,)), DMA((3,)), DMA((3,)), DMA((3,)), DMA((1,)), DMA((10,)), DMA((10,))]
    scratch += [DMA((3, 4)), DMA((3, 3)), DMA((1,)), DMA((10,)), DMA((10,)), DMA((4,)), DMA((8,))]
    return pl.pallas_call(
        functools.partial(layer_kernel, slot_total),
        out_shape=[
            jax.ShapeDtypeStruct((1, 1), f32),
            jax.ShapeDtypeStruct((4 * rows, width), bf16),
            jax.ShapeDtypeStruct((4 * rows, width), bf16),
            jax.ShapeDtypeStruct((depth, width), f32),
            jax.ShapeDtypeStruct((depth, width), f32),
            jax.ShapeDtypeStruct((depth, width), f32),
            jax.ShapeDtypeStruct((4, width), f32),
        ],
        in_specs=[here] * 10 + [there, here],
        out_specs=[here, there, there, here, here, here, here],
        scratch_shapes=scratch,
        compiler_params=pltpu.CompilerParams(
            collective_id=1, has_side_effects=True, vmem_limit_bytes=63 * 2**20
        ),
        cost_estimate=pl.CostEstimate(flops=30 * 10**9, bytes_accessed=40 * 10**6, transcendentals=10**7),
        name="layer",
    )(w_qkv, w_out, up_own, down_own, norms, valid, classes, *rest)


def finish_kernel(*refs):
    (block_in, token_in, attn_in, up_in, down_in) = refs[:5]
    (block_out, token_out, qkv_out, out_out, up_out, down_out) = refs[5:11]
    (narrow, wide, held, mats, qkv, out, sems) = refs[11:]
    parts, rows = narrow.shape[0], narrow.shape[1]
    count = iter(range(sems.shape[0]))

    def copy(src, dst):
        return pltpu.make_async_copy(src, dst, sems.at[next(count)])

    mat_loads = [copy(ref, mats.at[i]) for i, ref in enumerate((attn_in, up_in, down_in))]
    loads, saves, keep_loads, keep_saves = [], [], [], []
    for i in range(parts):
        span = pl.ds(i * rows, rows)
        loads.append(copy(token_in.at[span], narrow.at[i]))
        saves.append(copy(wide.at[i], token_out.at[span]))
        keep_loads.append(copy(block_in.at[span], held.at[i]))
        keep_saves.append(copy(held.at[i], block_out.at[span]))
    for load in mat_loads + loads + keep_loads:
        load.start()
    for load in mat_loads:
        load.wait()
    mat_saves = [copy(mats.at[1], up_out), copy(mats.at[2], down_out)]
    for save in mat_saves:
        save.start()
    for i, (pair, single) in enumerate(((0, 384), (128, 512), (256, 448))):
        qkv[i] = jnp.concatenate([mats[0, :, pair : pair + 128], mats[0, :, single : single + 64]], axis=1)
    depth = mats.shape[1]
    row = lax.broadcasted_iota(jnp.int32, (depth, depth), 0)
    eye = (row == lax.broadcasted_iota(jnp.int32, (depth, depth), 1)).astype(f32).astype(bf16)
    mixed = jnp.concatenate([mats[0, :, 640:768], mats[0, :, 576:640]], axis=1)
    out[...] = sum(tn(part, eye) for part in split_three(mixed))
    mat_saves += [copy(qkv, qkv_out), copy(out, out_out)]
    for save in mat_saves[2:]:
        save.start()
    for i in range(parts):
        loads[i].wait()
        wide[i] = narrow[i].astype(f32)
        saves[i].start()
    for load, save in zip(keep_loads, keep_saves):
        load.wait()
        save.start()
    for save in mat_saves + saves + keep_saves:
        save.wait()


def finish(block_out, token_grad, own_attn, own_up, own_down):
    rows, width = token_grad.shape
    depth = own_up.shape[0]
    parts = 4
    there = pl.BlockSpec(memory_space=pltpu.HBM)
    return pl.pallas_call(
        finish_kernel,
        out_shape=[
            jax.ShapeDtypeStruct(block_out.shape, bf16),
            jax.ShapeDtypeStruct((rows, width), f32),
            jax.ShapeDtypeStruct((3, depth, 192), f32),
            jax.ShapeDtypeStruct((192, depth), f32),
            jax.ShapeDtypeStruct((depth, width), f32),
            jax.ShapeDtypeStruct((depth, width), f32),
        ],
        in_specs=[there] * 5,
        out_specs=[there] * 6,
        scratch_shapes=[
            VMEM((parts, rows // parts, width), bf16),
            VMEM((parts, rows // parts, width), f32),
            VMEM((parts, rows // parts, width), bf16),
            VMEM((3, depth, width), f32),
            VMEM((3, depth, 192), f32),
            VMEM((192, depth), f32),
            DMA((7 + 4 * parts,)),
        ],
        compiler_params=pltpu.CompilerParams(vmem_limit_bytes=63 * 2**20),
        name="finish",
    )(block_out, token_grad, own_attn, own_up, own_down)


def on_kernel(
    tokens,
    segment_ids,
    slot_valid,
    ln1_gain,
    ln1_bias,
    w_qkv,
    w_out,
    ln2_gain,
    ln2_bias,
    w_up,
    w_down,
    class_tokens,
    image_gain,
    image_bias,
    image_proj,
):
    dp_rank = lax.axis_index("dp")
    depth, slots = w_up.shape[0], slot_valid.shape[0]
    loss, block_out, token_grad, own_attn, own_up, own_down, vectors = layer(
        slots * 32,
        w_qkv,
        w_out,
        w_up,
        w_down.T,
        jnp.stack([ln1_gain, ln1_bias, ln2_gain, ln2_bias]),
        slot_valid.reshape(1, slots),
        class_tokens,
        image_gain,
        image_bias,
        image_proj,
        tokens,
        segment_ids.reshape(4, 4, 128),
    )
    block_out, token_grad, qkv_grad, out_grad, own_up, own_down = finish(
        block_out, token_grad, own_attn, own_up, own_down
    )
    vectors = lax.dynamic_slice_in_dim(vectors, dp_rank * depth, depth, 1)
    return (
        loss.reshape(()),
        block_out,
        token_grad,
        vectors[0],
        vectors[1],
        qkv_grad,
        out_grad,
        vectors[2],
        vectors[3],
        own_up,
        own_down.T,
    )


def make(dp_size, mp_size):
    def on_device(
        tokens,
        segment_ids,
        slot_valid,
        ln1_gain,
        ln1_bias,
        w_qkv,
        w_out,
        ln2_gain,
        ln2_bias,
        w_up,
        w_down,
        class_tokens,
        image_gain,
        image_bias,
        image_proj,
    ):
        both = ("dp", "mp")
        dp_rank, mp_rank = lax.axis_index("dp"), lax.axis_index("mp")
        depth = w_up.shape[0]
        width = depth * dp_size
        head_cols = w_out.shape[0]
        heads = head_cols // HEAD_DIM
        rows = tokens.shape[0] // mp_size
        seqs = rows // SEQ_LEN
        slots = slot_valid.shape[0]
        slot_total = slots * dp_size * mp_size

        packed = jnp.stack(
            [jnp.concatenate([w_qkv[0], w_qkv[1], w_qkv[2], w_out.T], axis=1), w_up, w_down.T]
        )
        norms = jnp.stack([ln1_gain, ln1_bias, ln2_gain, ln2_bias])
        image_hat, _ = standardise(class_tokens.astype(f32))
        image_normed = (image_hat * image_gain + image_bias).astype(bf16)
        image_raw = nn(image_normed, image_proj)
        image_unit = (image_raw * inverse_norm(image_raw)).astype(bf16)

        weights = lax.all_gather(packed, both, axis=0).reshape(dp_size, mp_size, 3, depth, -1)
        weights = weights.transpose(2, 1, 0, 3, 4).reshape(3, mp_size, width, -1)
        vectors = lax.all_gather(norms, "dp", axis=1, tiled=True).astype(f32)
        all_image = lax.all_gather(image_unit, both, axis=0, tiled=True)
        all_valid = lax.all_gather(slot_valid.astype(bf16), both, axis=0, tiled=True) > 0

        own = lax.dynamic_slice_in_dim(tokens, mp_rank * rows, rows, 0).astype(f32)
        ids = lax.dynamic_slice_in_dim(segment_ids, mp_rank * rows, rows, 0)
        grid_ids = ids.reshape(seqs, SEQ_LEN)
        first_len = jnp.sum((grid_ids == 0).astype(jnp.int32), axis=1)
        starts = jnp.arange(seqs, dtype=jnp.int32) * SEQ_LEN
        ends = jnp.stack([starts + first_len - 1, starts + SEQ_LEN - 1], axis=1).reshape(2 * seqs)
        place = (ends[:, None] == jnp.arange(rows)[None, :]).astype(bf16)

        hat_one, rstd_one = standardise(own)
        normed = (hat_one * vectors[0] + vectors[1]).astype(bf16)
        attn = weights[0]
        qkv = jnp.einsum("rd,mde->mre", normed, attn[:, :, : 3 * head_cols], preferred_element_type=f32)
        qkv = qkv.astype(bf16).reshape(mp_size, rows, 3, heads, HEAD_DIM)
        blocks = rows // tile_rows
        split = qkv.reshape(mp_size, blocks, tile_rows, 3, heads, HEAD_DIM)
        query, key, value = split[:, :, :, 0], split[:, :, :, 1], split[:, :, :, 2]
        tile_ids = ids.reshape(blocks, tile_rows)
        spots = jnp.arange(tile_rows)
        allowed = (
            (tile_ids[:, :, None] == tile_ids[:, None, :])
            & (spots[:, None] // SEQ_LEN == spots[None, :] // SEQ_LEN)[None]
            & (spots[:, None] >= spots[None, :])[None]
        )[None, :, None]
        scale = HEAD_DIM**-0.5
        scores = jnp.einsum("mbqhc,mbkhc->mbhqk", query, key, preferred_element_type=f32) * scale
        scores = jnp.where(allowed, scores, -1e30)
        probs = jax.nn.softmax(scores, axis=-1)
        mixed = jnp.einsum("mbhqk,mbkhc->mbqhc", probs.astype(bf16), value, preferred_element_type=f32)
        mixed = mixed.astype(bf16).reshape(mp_size, rows, head_cols)
        out_t = attn[:, :, 3 * head_cols :]
        attended = jnp.einsum("mre,mde->rd", mixed, out_t, preferred_element_type=f32)
        hidden = own + attended

        def feed(rows_in):
            hat, rstd = standardise(rows_in)
            normed_two = (hat * vectors[2] + vectors[3]).astype(bf16)
            upper = jnp.einsum("rd,mdf->mrf", normed_two, weights[1], preferred_element_type=f32)
            active = (upper * phi(upper)).astype(bf16)
            branch = jnp.einsum("mrf,mdf->rd", active, weights[2], preferred_element_type=f32)
            return hat, rstd, normed_two, upper, active, rows_in + branch

        block_out = feed(hidden)[-1].astype(bf16)
        hidden_ends = hidden[ends]
        hat_two, rstd_two, normed_two, upper, active, pooled = feed(hidden_ends)

        scale_back = inverse_norm(pooled)
        text = (pooled * scale_back).astype(bf16)
        logits = logit_scale * nt(text, all_image)
        live = slot_valid > 0
        weight = jnp.exp(logits)
        row_sum = jnp.sum(jnp.where(all_valid[None, :], weight, 0.0), axis=1)
        col_part = jnp.sum(jnp.where(live[:, None], weight, 0.0), axis=0)
        row_index = (dp_rank * mp_size + mp_rank) * slots + jnp.arange(slots)
        target = jnp.arange(slot_total)[None, :] == row_index[:, None]
        matched = jnp.sum(jnp.where(target, logits, 0.0), axis=1)
        row_part = jnp.sum(jnp.where(live, jnp.log(row_sum) - 2.0 * matched, 0.0))
        sums = lax.psum(jnp.concatenate([col_part, row_part[None]]), both)
        col_sum = sums[:slot_total]
        loss = 0.5 * (sums[slot_total] + jnp.sum(jnp.where(all_valid, jnp.log(col_sum), 0.0))) / slot_total
        pair = live[:, None] & all_valid[None, :]
        spread = 0.5 * weight * (1.0 / row_sum[:, None] + 1.0 / col_sum[None, :])
        grad_logits = jnp.where(pair, spread, 0.0) - (target & live[:, None]).astype(f32)
        cosine_grad = (logit_scale * grad_logits).astype(bf16)
        unit_grad = nn(cosine_grad, all_image)
        along = jnp.sum(unit_grad * pooled, axis=-1, keepdims=True)
        pooled_grad = scale_back * unit_grad - pooled * (scale_back * scale_back * scale_back * along)

        branch_grad = pooled_grad.astype(bf16)
        down_local = jnp.einsum("rd,mrf->mdf", branch_grad, active, preferred_element_type=f32)
        active_grad = jnp.einsum("rd,mdf->mrf", branch_grad, weights[2], preferred_element_type=f32)
        slope = phi(upper) + upper * jnp.exp(-0.5 * upper * upper) * (1.0 / (2.0 * jnp.pi) ** 0.5)
        upper_grad = (active_grad * slope).astype(bf16)
        up_local = jnp.einsum("rd,mrf->mdf", normed_two, upper_grad, preferred_element_type=f32)
        normed_two_grad = jnp.einsum("mrf,mdf->rd", upper_grad, weights[1], preferred_element_type=f32)
        gain_two = jnp.sum(normed_two_grad * hat_two, axis=0)
        bias_two = jnp.sum(normed_two_grad, axis=0)
        hidden_grad = pooled_grad + norm_pull(normed_two_grad, hat_two, rstd_two, vectors[2])

        attended_grad = hidden_grad.astype(bf16)
        mixed_ends = mixed[:, ends]
        out_local = jnp.einsum("rd,mre->mde", attended_grad, mixed_ends, preferred_element_type=f32)
        mixed_grad = jnp.einsum("rd,mde->mre", attended_grad, out_t, preferred_element_type=f32).astype(bf16)
        mixed_grad = mixed_grad.reshape(mp_size, 2 * seqs, heads, HEAD_DIM)
        query_ends, keys, values = qkv[:, ends, 0], qkv[:, :, 1], qkv[:, :, 2]
        spot = jnp.arange(rows)
        allowed_ends = (
            (ids[ends][:, None] == ids[None, :])
            & (ends[:, None] // SEQ_LEN == spot[None, :] // SEQ_LEN)
            & (ends[:, None] >= spot[None, :])
        )[None, None]
        again = jnp.einsum("mqhc,mkhc->mhqk", query_ends, keys, preferred_element_type=f32) * scale
        probs_ends = jax.nn.softmax(jnp.where(allowed_ends, again, -1e30), axis=-1)
        probs_grad = jnp.einsum("mqhc,mkhc->mhqk", mixed_grad, values, preferred_element_type=f32)
        value_grad = jnp.einsum("mhqk,mqhc->mkhc", probs_ends.astype(bf16), mixed_grad, preferred_element_type=f32)
        centre = jnp.sum(probs_grad * probs_ends, axis=-1, keepdims=True)
        score_grad = (probs_ends * (probs_grad - centre)).astype(bf16)
        query_grad = jnp.einsum("mhqk,mkhc->mqhc", score_grad, keys, preferred_element_type=f32) * scale
        key_grad = jnp.einsum("mhqk,mqhc->mkhc", score_grad, query_ends, preferred_element_type=f32) * scale
        query_grad = query_grad.astype(bf16).reshape(mp_size, 2 * seqs, head_cols)
        query_grad = jnp.einsum("er,mec->mrc", place, query_grad, preferred_element_type=f32).astype(bf16)
        proj_grad = jnp.concatenate(
            [
                query_grad,
                key_grad.astype(bf16).reshape(mp_size, rows, head_cols),
                value_grad.astype(bf16).reshape(mp_size, rows, head_cols),
            ],
            axis=-1,
        )
        qkv_local = jnp.einsum("rd,mre->mde", normed, proj_grad, preferred_element_type=f32)
        normed_grad = jnp.einsum("mre,mde->rd", proj_grad, attn[:, :, : 3 * head_cols], preferred_element_type=f32)
        gain_one = jnp.sum(normed_grad * hat_one, axis=0)
        bias_one = jnp.sum(normed_grad, axis=0)
        token_grad = norm_pull(normed_grad, hat_one, rstd_one, vectors[0])
        token_grad = token_grad.at[ends].add(hidden_grad)

        local = jnp.stack([jnp.concatenate([qkv_local, out_local], axis=-1), up_local, down_local])
        local = local.reshape(3, mp_size, dp_size, depth, -1).transpose(2, 1, 0, 3, 4)
        local = local.reshape(dp_size * mp_size, 3, depth, -1)
        summed = lax.psum_scatter(local, both, scatter_dimension=0, tiled=False)
        vector_local = lax.psum(jnp.stack([gain_one, bias_one, gain_two, bias_two]), both)
        vector_own = lax.dynamic_slice_in_dim(vector_local, dp_rank * depth, depth, 1)

        block_out = lax.all_gather(block_out, "mp", axis=0, tiled=True)
        token_grad = lax.all_gather(token_grad, "mp", axis=0, tiled=True)
        qkv_grad = summed[0, :, : 3 * head_cols].reshape(depth, 3, head_cols).transpose(1, 0, 2)
        return (
            loss,
            block_out,
            token_grad,
            vector_own[0],
            vector_own[1],
            qkv_grad,
            summed[0, :, 3 * head_cols :].T,
            vector_own[2],
            vector_own[3],
            summed[1],
            summed[2].T,
        )

    return on_device


def solution(mesh):
    placed = (
        P("dp", None),
        P("dp"),
        P(("dp", "mp")),
        P("dp"),
        P("dp"),
        P(None, "dp", "mp"),
        P("mp", "dp"),
        P("dp"),
        P("dp"),
        P("dp", "mp"),
        P("mp", "dp"),
        P(("dp", "mp"), None),
        P(),
        P(),
        P(),
    )
    sizes = (mesh.shape["dp"], mesh.shape["mp"])
    return jax.shard_map(
        on_kernel if sizes == (8, 4) else make(*sizes),
        mesh=mesh,
        in_specs=placed,
        out_specs=(
            P(),
            P("dp", None),
            P("dp", None),
            P("dp"),
            P("dp"),
            P(None, "dp", "mp"),
            P("mp", "dp"),
            P("dp"),
            P("dp"),
            P("dp", "mp"),
            P("mp", "dp"),
        ),
        check_vma=False,
    )
```

```python
import jax
import jax.numpy as jnp
from jax import lax
from jax.sharding import PartitionSpec as P
import functools
from jax.experimental import pallas as pl
from jax.experimental.pallas import tpu as pltpu

HEAD_DIM = 64
SEQ_LEN = 16
norm_epsilon = 1e-05
unit_epsilon = 1e-06
logit_scale = 50.0
tile_rows = 128
f32, bf16 = jnp.float32, jnp.bfloat16


def standardise(values):
    centred = values - jnp.mean(values, axis=-1, keepdims=True)
    rstd = lax.rsqrt(jnp.mean(centred * centred, axis=-1, keepdims=True) + norm_epsilon)
    return centred * rstd, rstd


def norm_pull(grad, hat, rstd, gain):
    scaled = grad * gain
    first = jnp.mean(scaled, axis=-1, keepdims=True)
    second = jnp.mean(scaled * hat, axis=-1, keepdims=True)
    return rstd * (scaled - first - hat * second)


def inverse_norm(values):
    return lax.rsqrt(jnp.sum(values * values, axis=-1, keepdims=True) + unit_epsilon)


def nn(left, right):
    return lax.dot_general(left, right, (((1,), (0,)), ((), ())), preferred_element_type=f32)


def nt(left, right):
    return lax.dot_general(left, right, (((1,), (1,)), ((), ())), preferred_element_type=f32)


def tn(left, right):
    return lax.dot_general(left, right, (((0,), (0,)), ((), ())), preferred_element_type=f32)


def phi(values):
    return 0.5 * lax.erfc(-values * (0.5**0.5))


MESH = pl.DeviceIdType.MESH
VMEM, DMA = pltpu.VMEM, pltpu.SemaphoreType.DMA
CUT = 48
WINDOW = 3


def loop(count, body):
    lax.fori_loop(0, count, lambda i, carry: (body(i), carry)[1], 0)


def rows_of(index, size):
    return pl.ds(pl.multiple_of(index * size, size), size)


def split_three(values):
    first = values.astype(bf16)
    rest = values - first.astype(f32)
    second = rest.astype(bf16)
    return first, second, (rest - second.astype(f32)).astype(bf16)


def pick(place, values):
    return sum(nn(place, part) for part in split_three(values))


def spread_rows(place, values):
    return sum(tn(place, part) for part in split_three(values))


def half_erf(values):
    return 0.5 + 0.5 * lax.erf(values * (0.5**0.5))


def layer_kernel(slot_total, *refs):
    (w_qkv, w_out, up_own, down_own, norms, valid_own, classes, image_gain, image_bias, image_proj, tokens, ids) = refs[:12]
    (loss_out, block_out, token_out, attn_out, up_out, down_out, vec_out) = refs[12:19]
    (w_attn, w_up, w_down, images, smalls, x_ref, a_ref, qkv, hidden, a_two, active, stage_out, image_own, vecs) = refs[19:33]
    (mask_ref, place_ref, member_ref, h_ends, ends_two, ends_grad, u_ends, g_all, s_all, weight_ref, valid_ref) = refs[33:44]
    (sum_own, sum_buf, sum_got, d_attn, d_far) = refs[44:49]
    (grad_down, grad_up, grad_attn, step_x, step_z, attn_send, attn_core, ends_back) = refs[49:57]
    (vec_buf, vec_pack, vec_got, stage_grad, attn_own, small_own, far_mix) = refs[57:64]
    gsems = refs[64:92]
    isems = refs[92:101]
    (s_local, s_bo, s_on, s_send, s_a2, s_dm, s_dh, s_sum, s_sums, s_x, s_z, s_core, s_v, s_vs, s_tg, s_exs) = refs[101:117]

    dp = lax.axis_index("dp")
    mp = lax.axis_index("mp")
    z = lax.div(dp, 2)
    x = lax.rem(dp, 2)
    y = lax.div(mp, 2)
    c = lax.rem(mp, 2)
    xd, ym, cm = 2 * z + (1 - x), 2 * (1 - y) + c, 2 * y + (1 - c)
    zt = [lax.rem(z + j, 4) for j in range(4)]
    zs = [lax.rem(z + 4 - j, 4) for j in range(4)]
    X, Y, C, YC = (xd, mp), (dp, ym), (dp, cm), (dp, 3 - mp)
    Z = [(2 * zt[j] + x, mp) for j in range(4)]
    here = 4 * x + mp
    PLANE = []
    for j in range(1, 8):
        other = lax.rem(here + j, 8)
        PLANE.append((2 * z + lax.div(other, 4), lax.rem(other, 4)))
    G = [(dp, lax.rem(mp + j, 4)) for j in range(4)]

    peers = PLANE + Z[1:]
    barrier = pltpu.get_barrier_semaphore()
    for peer in peers:
        pl.semaphore_signal(barrier, inc=1, device_id=peer, device_id_type=MESH)
    pl.semaphore_wait(barrier, len(peers))

    def remote(src, dst, send_sem, recv_sem, device):
        copy = pltpu.make_async_remote_copy(
            src_ref=src, dst_ref=dst, send_sem=send_sem, recv_sem=recv_sem, device_id=device, device_id_type=MESH
        )
        copy.start()
        return copy

    def arrived(ref, recv_sem, send_sem):
        pltpu.make_async_remote_copy(
            src_ref=ref, dst_ref=ref, send_sem=send_sem, recv_sem=recv_sem, device_id=X, device_id_type=MESH
        ).wait_recv()

    def gather_steps(src, out, rows, cut, sems):
        zr, x0, y1, y0, x1, cr, sd = sems
        first = (0, cut) if cut else (0, rows)
        second = (cut, rows - cut) if cut else None
        full = (0, rows)

        def piece(d, m, span):
            return out.at[m, pl.ds(pl.multiple_of(d * rows + span[0], 16), span[1])]

        def send(src_ref, dst_ref, sem, device):
            remote(src_ref, dst_ref, sd.at[0], sem, device)

        def got(ref, sem):
            arrived(ref, sem, sd.at[0])

        def step0():
            for j in range(1, 4):
                send(src, piece(dp, mp, full), zr.at[j], Z[j])
            send(src.at[pl.ds(*first)], piece(dp, mp, first), x0.at[0], X)
            if second:
                send(src.at[pl.ds(*second)], piece(dp, mp, second), y1.at[0], Y)
            send(src.at[pl.ds(*first)], piece(dp, mp, first), y0.at[0], Y)
            if second:
                send(src.at[pl.ds(*second)], piece(dp, mp, second), x1.at[0], X)
            send(src, piece(dp, mp, full), cr.at[0], C)
            pltpu.make_async_copy(src, piece(dp, mp, full), sd.at[0]).start()
            yield

        def step1():
            for j in range(1, 4):
                d = 2 * zs[j] + x
                block = piece(d, mp, full)
                got(block, zr.at[j])
                one = piece(d, mp, first)
                send(one, one, x0.at[j], X)
                if second:
                    two = piece(d, mp, second)
                    send(two, two, y1.at[j], Y)
                send(one, one, y0.at[j], Y)
                if second:
                    send(two, two, x1.at[j], X)
                send(block, block, cr.at[0], C)
                yield

        def step2():
            for j in range(4):
                one = piece(2 * zs[j] + (1 - x), mp, first)
                got(one, x0.at[j])
                send(one, one, y0.at[4 + j], Y)
                send(one, one, cr.at[0], C)
                if second:
                    two = piece(2 * zs[j] + x, ym, second)
                    got(two, y1.at[j])
                    send(two, two, x1.at[4 + j], X)
                    send(two, two, cr.at[0], C)
                yield

        def step3():
            for i in range(2):
                for j in range(4):
                    one = piece(2 * zs[j] + (x if i == 0 else 1 - x), ym, first)
                    got(one, y0.at[4 * i + j])
                    send(one, one, cr.at[0], C)
                    if second:
                        two = piece(2 * zs[j] + (1 - x), (mp if i == 0 else ym), second)
                        got(two, x1.at[4 * i + j])
                        send(two, two, cr.at[0], C)
                    yield

        def step4():
            half = out.at[pl.ds(0, 2)]
            pltpu.make_async_copy(half, half, cr.at[0]).wait()
            pltpu.make_async_copy(out, out, sd.at[0]).wait()
            yield

        return [step0, step1, step2, step3, step4]

    depth = up_own.shape[0]
    slots = classes.shape[0]

    def image_steps():
        near, cross, core, near_sent, core_sent, up_got, down_got, up_sent, down_sent = isems

        def at(d, m, start=0, size=slots):
            return images.at[m, pl.ds(pl.multiple_of(d * slots + start, 16), size)]

        def plane(z_, i):
            return images.at[2 * i + c, pl.ds(pl.multiple_of(2 * z_ * slots, 16), 2 * slots)]

        def to_core(ref):
            remote(ref, ref, core_sent.at[0], core.at[0], C)

        half = slots // 2

        def step0():
            remote(image_own, at(dp, mp), near_sent.at[0], near.at[0], X)
            remote(image_own, at(dp, mp), near_sent.at[0], near.at[1], Y)
            remote(image_own, at(dp, mp), core_sent.at[0], core.at[0], C)
            pltpu.make_async_copy(image_own, at(dp, mp), s_local.at[5]).start()
            yield

        def step1():
            arrived(at(xd, mp), near.at[0], near_sent.at[0])
            remote(at(xd, mp, 0, half), at(xd, mp, 0, half), near_sent.at[0], cross.at[0], Y)
            to_core(at(xd, mp))
            arrived(at(dp, ym), near.at[1], near_sent.at[0])
            remote(at(dp, ym, half, half), at(dp, ym, half, half), near_sent.at[0], cross.at[1], X)
            to_core(at(dp, ym))
            yield

        def up(i, t):
            ref = plane(z - t, i)
            return pltpu.make_async_remote_copy(
                src_ref=ref, dst_ref=ref, send_sem=up_sent.at[t, i], recv_sem=up_got.at[t, i],
                device_id=(2 * (z + 1) + x, mp), device_id_type=MESH,
            )

        def down(i, t):
            ref = plane(z + t, i)
            return pltpu.make_async_remote_copy(
                src_ref=ref, dst_ref=ref, send_sem=down_sent.at[t, i], recv_sem=down_got.at[t, i],
                device_id=(2 * (z - 1) + x, mp), device_id_type=MESH,
            )

        def step2():
            arrived(at(xd, ym, 0, half), cross.at[0], near_sent.at[0])
            arrived(at(xd, ym, half, half), cross.at[1], near_sent.at[0])
            to_core(at(xd, ym))
            pltpu.make_async_copy(image_own, at(dp, mp), s_local.at[5]).wait()
            for i in range(2):
                pl.when(z < 3)(lambda i=i: up(i, 0).start())
                pl.when(z > 0)(lambda i=i: down(i, 0).start())
            yield

        def step3():
            for t in range(1, 4):
                for i in range(2):

                    def from_below(i=i, t=t):
                        ref = plane(z - t, i)
                        arrived(ref, up_got.at[t - 1, i], near_sent.at[0])
                        if t < 3:
                            pl.when(z < 3)(lambda: up(i, t).start())
                        to_core(ref)

                    def from_above(i=i, t=t):
                        ref = plane(z + t, i)
                        arrived(ref, down_got.at[t - 1, i], near_sent.at[0])
                        if t < 3:
                            pl.when(z > 0)(lambda: down(i, t).start())
                        to_core(ref)

                    pl.when(z >= t)(from_below)
                    pl.when(z + t <= 3)(from_above)
                    yield

        def step4():
            halves = images.at[pl.ds(0, 2)]
            pltpu.make_async_copy(halves, halves, core.at[0]).wait()
            pltpu.make_async_copy(halves, halves, core_sent.at[0]).wait()
            three = images.at[0, pl.ds(0, 3 * slots)]
            pltpu.make_async_copy(three, three, near_sent.at[0]).wait()
            for t in range(3):
                for i in range(2):
                    pl.when((z >= t) & (z < 3))(lambda i=i, t=t: up(i, t).wait_send())
                    pl.when((z + t <= 3) & (z > 0))(lambda i=i, t=t: down(i, t).wait_send())
            yield

        return [step0, step1, step2, step3, step4]

    kinds = {
        "S": gather_steps(small_own, smalls, 16, 0, gsems[0:7]),
        "A": gather_steps(attn_own, w_attn, depth, CUT, gsems[7:14]),
        "U": gather_steps(up_own, w_up, depth, CUT, gsems[14:21]),
        "D": gather_steps(down_own, w_down, depth, CUT, gsems[21:28]),
        "I": image_steps(),
    }

    def run(*steps):
        for name in steps:
            for _ in kinds[name[0]][int(name[1])]():
                pass

    def blend(steps, chunks):
        chunks = list(chunks)
        micro = [kinds[name[0]][int(name[1])] for name in steps]
        count = sum((1, 3, 4, 8, 1)[int(name[1])] if name[0] != "I" else (1, 1, 1, 6, 1)[int(name[1])] for name in steps)
        done, at = 0, 0
        for step in micro:
            for _ in step():
                at += 1
                while done < len(chunks) and done * count < at * len(chunks):
                    chunks[done]()
                    done += 1
        for chunk in chunks[done:]:
            chunk()

    lane = lax.broadcasted_iota(jnp.int32, (128, 128), 1)
    sub = lax.broadcasted_iota(jnp.int32, (128, 128), 0)
    low = lax.broadcasted_iota(jnp.int32, (1, 128), 1) < 64
    token_rows = hidden.shape[0]
    tiles = token_rows // 128
    end_count = h_ends.shape[0]

    def keep_low(values):
        return jnp.where(low, values, jnp.zeros_like(values))

    def keep_high(values):
        return jnp.where(low, jnp.zeros_like(values), values)

    def pack_own():
        rows = lax.broadcasted_iota(jnp.int32, (depth, depth), 0)
        eye = (rows == lax.broadcasted_iota(jnp.int32, (depth, depth), 1)).astype(f32).astype(bf16)
        out_t = nt(eye, w_out[...]).astype(bf16)
        query, key, value = w_qkv[0], w_qkv[1], w_qkv[2]
        attn_own[:, 0:128] = query[:, 0:128]
        attn_own[:, 128:256] = key[:, 0:128]
        attn_own[:, 256:384] = value[:, 0:128]
        attn_own[:, 384:512] = jnp.concatenate([query[:, 128:192], value[:, 128:192]], axis=1)
        attn_own[:, 512:640] = jnp.concatenate([key[:, 128:192], out_t[:, 128:192]], axis=1)
        attn_own[:, 640:768] = out_t[:, 0:128]

    def pack_small():
        shift = lax.broadcasted_iota(jnp.int32, (depth, 384), 1) - lax.broadcasted_iota(jnp.int32, (depth, 384), 0)
        made = nn(norms[...], (shift == depth * lax.rem(dp, 4)).astype(f32).astype(bf16))
        shift = lax.broadcasted_iota(jnp.int32, (slots, 128), 1) - lax.broadcasted_iota(jnp.int32, (slots, 128), 0)
        flags = jnp.broadcast_to(valid_own[...].astype(f32), (8, slots)).astype(bf16)
        flags = nn(flags, (shift == slots * lax.rem(dp, 2)).astype(f32).astype(bf16))
        parts = [made[v : v + 1, 128 * t : 128 * (t + 1)] for v in range(4) for t in range(3)]
        small_own[...] = jnp.concatenate(parts + [flags[0:4, :]], axis=0).astype(bf16)

    def masks(g):
        slot_row = lax.broadcasted_iota(jnp.int32, (end_count, 128), 0)
        spots = []
        best = jnp.full((end_count, 1), -1, jnp.int32)
        for b in range(tiles):
            sequence = 8 * b + lax.shift_right_logical(lax.broadcasted_iota(jnp.int32, (1, 128), 1), 4)
            caption = 2 * sequence + ids[ym if g else mp, pl.ds(b, 1), :]
            column = jnp.sum(jnp.where(lane == sub, caption, 0), axis=1, keepdims=True)
            mask_ref[tiles * g + b] = jnp.where((column == caption) & (sub >= lane), 0.0, -1e30)
            member = slot_row == caption
            spot = lax.broadcasted_iota(jnp.int32, (end_count, 128), 1) + 128 * b
            best = jnp.maximum(best, jnp.max(jnp.where(member, spot, -1), axis=1, keepdims=True))
            member_ref[g, :, 128 * b : 128 * (b + 1)] = jnp.where(member, 0.0, -1e30)
            spots.append(spot)
        for b in range(tiles):
            place_ref[g, :, 128 * b : 128 * (b + 1)] = (spots[b] == best).astype(f32).astype(bf16)

    def image_tower():
        hat, _ = standardise(classes[...].astype(f32))
        raw = nn((hat * image_gain[...].reshape(1, -1) + image_bias[...].reshape(1, -1)).astype(bf16), image_proj[...])
        image_own[...] = (raw * inverse_norm(raw)).astype(bf16)

    def small_vectors():
        halves = []
        for w in range(2):
            halves.append(sum(smalls[0, 64 * w + 16 * d : 64 * w + 16 * (d + 1), :].astype(f32) for d in range(4)))
        for v in range(4):
            for w in range(2):
                for t in range(3):
                    at = 384 * w + 128 * t
                    vecs[v : v + 1, at : at + 128] = halves[w][3 * v + t : 3 * v + t + 1, :]
        for m in range(4):
            for pair in range(4):
                both = sum(smalls[m, 32 * pair + 16 * d : 32 * pair + 16 * (d + 1), :].astype(f32) for d in range(2))
                valid_ref[m : m + 1, 128 * pair : 128 * (pair + 1)] = both[12:13, :]

    def first_norm(g):
        def body(b):
            rows = rows_of(tiles * g + b, 128)
            values = x_ref[rows, :].astype(f32)
            hat, _ = standardise(values)
            a_ref[rows, :] = (hat * vecs[0:1, :] + vecs[1:2, :]).astype(bf16)
            if g == 0:
                hidden[rows, :] = values

        loop(tiles, body)

    def soft(scores):
        top = jnp.max(scores, axis=-1, keepdims=True)
        raised = jnp.exp(scores - top)
        return raised * (1.0 / jnp.sum(raised, axis=-1, keepdims=True))

    scale = HEAD_DIM**-0.5

    def project(m, g):
        def body(b):
            rows = rows_of(2 * g + b, 256)
            qkv[m, rows, :] = nn(a_ref[rows, :], w_attn[m]).astype(bf16)

        loop(2, body)

    def attention(m):
        project(m, 0)

        def body(pair):
            for b in (2 * pair, 2 * pair + 1):
                rows = rows_of(b, 128)
                q01, k01, v01, qv, ko = (qkv[m, rows, 128 * i : 128 * (i + 1)] for i in range(5))
                mask = mask_ref[b]
                p0 = soft(nt(keep_low(q01), k01) * scale + mask).astype(bf16)
                p1 = soft(nt(keep_high(q01), k01) * scale + mask).astype(bf16)
                p2 = soft(nt(keep_low(qv), ko) * scale + mask).astype(bf16)
                o01 = jnp.where(low, nn(p0, v01), nn(p1, v01)).astype(bf16)
                o2 = keep_high(nn(p2, qv)).astype(bf16)
                qkv[m, rows, 512:640] = keep_low(ko) + o2
                qkv[m, rows, 640:768] = o01

        loop(tiles // 2, body)

        def attended(b):
            rows = rows_of(b, 256)
            mixed = jnp.concatenate([keep_high(qkv[m, rows, 512:640]), qkv[m, rows, 640:768]], axis=1)
            hidden[rows, :] += nt(mixed, w_attn[m, :, 512:768])

        loop(2, attended)

    def second_norm():
        def body(b):
            rows = rows_of(b, 128)
            hat, _ = standardise(hidden[rows, :])
            a_two[rows, :] = (hat * vecs[2:3, :] + vecs[3:4, :]).astype(bf16)

        loop(tiles, body)
        place = place_ref[0]
        ends = pick(place, hidden[...])
        h_ends[...] = ends
        hat, _ = standardise(ends)
        ends_two[mp] = (hat * vecs[2:3, :] + vecs[3:4, :]).astype(bf16)

    def ends_up(m):
        u_ends[m] = nn(ends_two[mp], w_up[m])

    def full_up(m):
        def body(b):
            rows = rows_of(b, 256)
            upper = nn(a_two[rows, :], w_up[m])
            active[m, rows, :] = (upper * half_erf(upper)).astype(bf16)

        loop(tiles // 2, body)

    def slope_of(upper):
        return half_erf(upper) + upper * jnp.exp(-0.5 * upper * upper) * (1.0 / (2.0 * jnp.pi) ** 0.5)

    def group_up(start):
        def body(i):
            upper = nn(ends_two[start + i], w_up[mp])
            rows = rows_of(start + i, end_count)
            g_all[rows, :] = (upper * half_erf(upper)).astype(bf16)
            s_all[rows, :] = slope_of(upper)

        loop(2, body)

    def full_down(b):
        rows = slice(256 * b, 256 * (b + 1))

        def body(m, total):
            return total + nt(active[m, rows, :], w_down[m])

        stage_out[rows, :] = lax.fori_loop(0, 4, body, hidden[rows, :]).astype(bf16)

    token_copies = []
    for g in range(2):
        wanted = tokens.at[rows_of(ym if g else mp, token_rows)]
        token_copies.append(pltpu.make_async_copy(wanted, x_ref.at[pl.ds(g * token_rows, token_rows)], s_local.at[g]))
        token_copies[g].start()
    pack_small()
    run("S0")
    pack_own()
    run("A0")
    image_tower()
    run("I0", "U0")
    masks(0)
    masks(1)
    run("S1", "A1", "D0", "I1", "S2", "A2", "I2", "U1", "S3", "S4")
    small_vectors()
    for g in range(2):
        token_copies[g].wait()
        first_norm(g)
    run("D1", "A3", "A4")
    blend(("U2", "I3", "D2", "U3"), [functools.partial(attention, m) for m in range(4)])
    second_norm()
    swaps = [remote(ends_two.at[mp], ends_two.at[mp], s_exs.at[j - 1], s_a2.at[j - 1], G[j]) for j in range(1, 4)]
    run("U4")
    blend(("D3",), [functools.partial(full_up, m) for m in range(4)])
    loop(4, ends_up)
    run("I4")
    for swap in swaps:
        swap.wait()
    run("D4")

    pooled = h_ends[...]
    for m in range(4):
        upper = u_ends[m]
        pooled = pooled + nt((upper * half_erf(upper)).astype(bf16), w_down[m])
    scale_back = inverse_norm(pooled)
    text = (pooled * scale_back).astype(bf16)
    own_valid = small_own[12:13, :].astype(f32)
    own_valid = jnp.max(
        jnp.where(
            lax.rem(lax.broadcasted_iota(jnp.int32, (slots, 128), 1), slots)
            == lax.broadcasted_iota(jnp.int32, (slots, 128), 0),
            own_valid,
            0.0,
        ),
        axis=1,
        keepdims=True,
    )
    live = own_valid > 0.0
    place_col = lax.broadcasted_iota(jnp.int32, (slots, 512), 1)
    place_row = lax.broadcasted_iota(jnp.int32, (slots, 512), 0)

    def target_of(m):
        return (place_col == place_row + dp * slots) & (mp == m)

    row_sum = jnp.zeros((slots, 1), f32)
    matched = jnp.zeros((slots, 1), f32)
    for m in range(4):
        logits = logit_scale * nt(text, images[m])
        weight = jnp.exp(logits)
        matched = matched + jnp.sum(jnp.where(target_of(m), logits, 0.0), axis=1, keepdims=True)
        seen = jnp.where(valid_ref[m : m + 1, :] > 0.0, weight, 0.0)
        weight_ref[m] = seen
        row_sum = row_sum + jnp.sum(seen, axis=1, keepdims=True)
        columns = jnp.sum(jnp.where(live, weight, 0.0), axis=0, keepdims=True)
        for part in range(4):
            sum_own[4 * m + part : 4 * m + part + 1, :] = columns[:, 128 * part : 128 * (part + 1)]
    row_part = jnp.sum(jnp.where(live, jnp.log(row_sum) - 2.0 * matched, 0.0), axis=0, keepdims=True)
    sum_own[16:24, :] = jnp.broadcast_to(row_part, (8, 128))

    swaps = [remote(sum_own, sum_got.at[here], s_sums.at[j - 1], s_sum.at[j - 1], PLANE[j - 1]) for j in range(1, 8)]
    sum_got[here] = sum_own[...]
    group_up(0)
    for swap in swaps:
        swap.wait()
    sum_buf[...] = ((sum_got[0] + sum_got[1]) + (sum_got[2] + sum_got[3])) + (
        (sum_got[4] + sum_got[5]) + (sum_got[6] + sum_got[7])
    )
    swaps = [remote(sum_buf, sum_got.at[8 + z], s_sums.at[6 + j], s_sum.at[6 + j], Z[j]) for j in range(1, 4)]
    sum_got[8 + z] = sum_buf[...]
    group_up(2)
    for swap in swaps:
        swap.wait()
    sums = (sum_got[8] + sum_got[9]) + (sum_got[10] + sum_got[11])

    total = sums[16:17, 0:1]
    unit_grad = jnp.zeros((slots, text.shape[1]), f32)
    for m in range(4):
        columns = jnp.concatenate([sums[4 * m + part : 4 * m + part + 1, :] for part in range(4)], axis=1)
        seen = valid_ref[m : m + 1, :] > 0.0
        total = total + jnp.sum(jnp.where(seen, jnp.log(columns), 0.0), axis=1, keepdims=True)
        spread = 0.5 * weight_ref[m] * (1.0 / row_sum + 1.0 / columns)
        grad = jnp.where(seen & live, spread, 0.0) - jnp.where(target_of(m) & live, 1.0, 0.0)
        unit_grad = unit_grad + nn((logit_scale * grad).astype(bf16), images[m])
    loss_out[...] = total * (0.5 / slot_total)
    along = jnp.sum(unit_grad * pooled, axis=-1, keepdims=True)
    pooled_grad = scale_back * unit_grad - pooled * (scale_back * scale_back * scale_back * along)
    branch_grad = pooled_grad.astype(bf16)
    ends_grad[mp] = branch_grad
    swaps = [remote(ends_grad.at[mp], ends_grad.at[mp], s_exs.at[2 + j], s_dm.at[j - 1], G[j]) for j in range(1, 4)]

    def two_part(m):
        upper_grad = (nn(branch_grad, w_down[m]) * slope_of(u_ends[m])).astype(bf16)
        return nt(upper_grad, w_up[m])

    two_grad = two_part(0) + two_part(1)

    def block(z_, x_):
        return pl.ds(pl.multiple_of((2 * z_ + x_) * depth, 16), depth)

    grads, outs = [grad_down, grad_up, grad_attn], [down_out, up_out, attn_out]

    order = [(k, j) for k in range(3) for j in (2, 1, 3, 0)]
    sent, added = iter(order), iter(order)

    def sum_start(count):
        for _ in range(count):
            k, j = next(sent, (None, None))
            if k is not None:
                remote(grads[k].at[block(zt[j], 1 - x)], step_x.at[k, j], s_send.at[k], s_x.at[k, j], X)

    def sum_add(k, j):
        arrived(step_x.at[k, j], s_x.at[k, j], s_send.at[k])
        mine = block(zt[j], x)
        summed = grads[k][mine, :].astype(f32) + step_x[k, j].astype(f32)
        if j:
            grads[k][mine, :] = summed.astype(bf16)
            remote(grads[k].at[mine], step_z.at[k, j - 1], s_send.at[k], s_z.at[k, j - 1], Z[j])
        else:
            outs[k][...] = summed

    def sum_end(k):
        for j in range(1, 4):
            arrived(step_z.at[k, j - 1], s_z.at[k, j - 1], s_send.at[k])
        outs[k][...] = outs[k][...] + step_z[k, 0].astype(f32) + step_z[k, 1].astype(f32) + step_z[k, 2].astype(f32)
        sent = grads[k].at[pl.ds(0, 7 * depth)]
        pltpu.make_async_copy(sent, sent, s_send.at[k]).wait()

    def sum_some(count):
        for _ in range(count):
            sum_start(1)
            sum_add(*next(added))

    for swap in swaps:
        swap.wait()
    group_grad = ends_grad[...].reshape(4 * end_count, -1)
    upper_grad = (nn(group_grad, w_down[mp]) * s_all[...]).astype(bf16)
    grad_down[...] = tn(group_grad, g_all[...]).astype(bf16)

    sum_start(WINDOW)
    grad_up[...] = tn(ends_two[...].reshape(4 * end_count, -1), upper_grad).astype(bf16)

    two_grad = two_grad + two_part(2) + two_part(3)
    hat_two, rstd_two = standardise(h_ends[...])
    vec_buf[...] = jnp.zeros_like(vec_buf)
    vec_buf[2:3, :] = jnp.sum(two_grad * hat_two, axis=0, keepdims=True)
    vec_buf[3:4, :] = jnp.sum(two_grad, axis=0, keepdims=True)
    hidden_grad = pooled_grad + norm_pull(two_grad, hat_two, rstd_two, vecs[2:3, :])
    ends_back[0] = hidden_grad.astype(bf16)
    back_swap = remote(ends_back.at[0], ends_back.at[1], s_exs.at[6], s_dh.at[0], Y)

    def attention_back(m, g, mix=False):
        place = place_ref[g]
        member = member_ref[g]
        ends_row = ends_back[g]
        span = slice(token_rows * g, token_rows * (g + 1))
        k01, v01, qv, ko = (qkv[m, span, 128 * i : 128 * (i + 1)] for i in range(1, 5))
        q_e = nn(place, qkv[m, span, 0:128]).astype(bf16)
        q2_e = keep_low(nn(place, qv)).astype(bf16)
        do01 = nn(ends_row, w_attn[m, :, 640:768]).astype(bf16)
        do2 = keep_high(nn(ends_row, w_attn[m, :, 512:640])).astype(bf16)

        def head(query, keys, values, outer):
            probs = soft(nt(query, keys) * scale + member)
            probs_grad = nt(outer, values)
            centre = jnp.sum(probs_grad * probs, axis=-1, keepdims=True)
            return probs.astype(bf16), (probs * (probs_grad - centre)).astype(bf16)

        p0, ds0 = head(keep_low(q_e), k01, v01, keep_low(do01))
        p1, ds1 = head(keep_high(q_e), k01, v01, keep_high(do01))
        p2, ds2 = head(q2_e, ko, qv, do2)
        dq01 = (jnp.where(low, nn(ds0, k01), nn(ds1, k01)) * scale).astype(bf16)
        dq2 = keep_low(nn(ds2, ko) * scale).astype(bf16)
        if g == 1 and mix:
            far_mix[:, 0:128] = nn(p2, qv).astype(bf16)
            far_mix[:, 128:256] = jnp.where(low, nn(p0, v01), nn(p1, v01)).astype(bf16)
        d_ref = d_far if g else active
        d_ref[m, :, 0:128] = tn(place, dq01).astype(bf16)
        d_ref[m, :, 128:256] = (jnp.where(low, tn(ds0, q_e), tn(ds1, q_e)) * scale).astype(bf16)
        d_ref[m, :, 256:384] = jnp.where(low, tn(p0, do01), tn(p1, do01)).astype(bf16)
        d_ref[m, :, 384:512] = jnp.where(low, tn(place, dq2), tn(p2, do2)).astype(bf16)
        d_ref[m, :, 512:640] = keep_low(tn(ds2, q2_e) * scale).astype(bf16)

    def token_back(g):
        d_ref = d_far if g else active

        def body(b):
            rows = rows_of(b, 256)
            total = jnp.zeros((256, d_attn.shape[1]), f32)
            for m in range(4):
                total = total + nt(d_ref[m, rows, 0:640], w_attn[m, :, 0:640])
            d_attn[rows_of(2 * g + b, 256), :] = total

        loop(2, body)

    def attn_grad(m):
        ends_mix = nn(place_ref[0], qkv[m, 0:token_rows, 512:768]).astype(bf16)
        outer = tn(ends_back[0], ends_mix) + tn(ends_back[1], far_mix[...])

        def made(start, stop):
            span = slice(start, stop)
            return tn(a_ref[0:token_rows, :], active[m, :, span]) + tn(a_ref[token_rows:, :], d_far[m, :, span])

        last = jnp.where(low, made(512, 640), outer[:, 0:128])
        return jnp.concatenate([made(0, 512), last, outer[:, 128:256]], axis=1)

    full_down(0)
    sum_some(1)
    back_swap.wait()
    full_down(1)
    own_rows = rows_of(mp, token_rows)
    far_rows = rows_of(ym, token_rows)
    out_swaps = [
        remote(stage_out, block_out.at[own_rows], s_bo.at[0], s_bo.at[1], Y),
        remote(stage_out, block_out.at[own_rows], s_bo.at[2], s_bo.at[3], C),
    ]
    keep_out = pltpu.make_async_copy(stage_out, block_out.at[own_rows], s_local.at[2])
    keep_out.start()

    def both_back(m, mix=False):
        project(m, 1)
        attention_back(m, 0, mix)
        attention_back(m, 1, mix)
        sum_some(1)

    sum_some(1)
    m = 2 * y + (1 - c)
    both_back(m, True)
    attn_send[...] = attn_grad(m).astype(bf16)
    core_swap = remote(attn_send, attn_core, s_exs.at[7], s_core.at[0], C)
    sum_some(1)
    m = 2 * y + c
    both_back(m, True)
    made = attn_grad(m)
    core_swap.wait()
    grad_attn[...] = (made + attn_core[...].astype(f32)).astype(bf16)
    sum_some(1)
    for i in range(2):
        both_back(2 * (1 - y) + i)

    def token_end(g):
        def body(b):
            rows = rows_of(tiles * g + b, 128)
            hat, rstd = standardise(x_ref[rows, :].astype(f32))
            grad = d_attn[rows, :]
            if g == 0:
                vec_buf[0:1, :] += jnp.sum(grad * hat, axis=0, keepdims=True)
                vec_buf[1:2, :] += jnp.sum(grad, axis=0, keepdims=True)
            d_attn[rows, :] = norm_pull(grad, hat, rstd, vecs[0:1, :])

        loop(tiles, body)
        span = slice(token_rows * g, token_rows * (g + 1))
        stage_grad[span, :] = (d_attn[span, :] + tn(place_ref[g], ends_back[g])).astype(bf16)

    grad_swaps, keep_grads = [], []
    out_swaps[0].wait()
    on = remote(block_out.at[far_rows], block_out.at[far_rows], s_on.at[0], s_on.at[1], C)
    for g in range(2):
        token_back(g)
        token_end(g)
        if g == 0:
            for v in range(4):
                for t in range(6):
                    vec_pack[0, 6 * v + t : 6 * v + t + 1, :] = vec_buf[v : v + 1, 128 * t : 128 * (t + 1)]
            core_vec = remote(vec_pack.at[0], vec_got.at[0], s_vs.at[0], s_v.at[0], C)
        ref = stage_grad.at[pl.ds(token_rows * g, token_rows)]
        spot = token_out.at[far_rows if g else own_rows]
        grad_swaps.append(remote(ref, spot, s_tg.at[2 * g], s_tg.at[2 * g + 1], C))
        keep_grads.append(pltpu.make_async_copy(ref, spot, s_local.at[3 + g]))
        keep_grads[g].start()
        sum_some(1)
    core_vec.wait()
    vec_pack[1] = vec_pack[0] + vec_got[0]
    across = [X, Y, (2 * z + (1 - x), ym)]
    vec_swaps = [
        remote(vec_pack.at[1], vec_got.at[1 + 2 * y + x], s_vs.at[1 + j], s_v.at[1 + j], across[j]) for j in range(3)
    ]
    vec_got[1 + 2 * y + x] = vec_pack[1]
    sum_some(1)
    for swap in vec_swaps:
        swap.wait()
    vec_pack[2] = (vec_got[1] + vec_got[2]) + (vec_got[3] + vec_got[4])
    vec_swaps = [
        remote(vec_pack.at[2], vec_got.at[5 + z], s_vs.at[3 + j], s_v.at[3 + j], Z[j]) for j in range(1, 4)
    ]
    vec_got[5 + z] = vec_pack[2]
    sum_some(1)
    for swap in vec_swaps:
        swap.wait()
    total = (vec_got[5] + vec_got[6]) + (vec_got[7] + vec_got[8])
    for v in range(4):
        for t in range(6):
            vec_out[v : v + 1, 128 * t : 128 * (t + 1)] = total[6 * v + t : 6 * v + t + 1, :]
    sum_end(0)
    sum_end(1)
    sum_end(2)
    out_swaps[1].wait()
    on.wait()
    keep_out.wait()
    for swap in grad_swaps + keep_grads:
        swap.wait()


def layer(slot_total, w_qkv, w_out, up_own, down_own, norms, valid, classes, *rest):
    depth, width = up_own.shape
    slots = classes.shape[0]
    rows = rest[3].shape[0] // 4

    def gather_sems():
        return [DMA((4,)), DMA((4,)), DMA((4,)), DMA((8,)), DMA((8,)), DMA((1,)), DMA((1,))]

    here, there = pl.BlockSpec(memory_space=VMEM), pl.BlockSpec(memory_space=pltpu.HBM)
    square = VMEM((4, width, width), bf16)
    scratch = [
        square,
        square,
        square,
        VMEM((4, 8 * slots, width), bf16),
        VMEM((4, 128, 128), bf16),
        VMEM((2 * rows, width), bf16),
        VMEM((2 * rows, width), bf16),
        VMEM((4, 2 * rows, width), bf16),
        VMEM((rows, width), f32),
        VMEM((rows, width), bf16),
        VMEM((4, rows, width), bf16),
        VMEM((rows, width), bf16),
        VMEM((slots, width), bf16),
        VMEM((8, width), f32),
        VMEM((2 * rows // 128, 128, 128), f32),
        VMEM((2, slots, rows), bf16),
        VMEM((2, slots, rows), f32),
        VMEM((slots, width), f32),
        VMEM((4, slots, width), bf16),
        VMEM((4, slots, width), bf16),
        VMEM((4, slots, width), f32),
        VMEM((4 * slots, width), bf16),
        VMEM((4 * slots, width), f32),
        VMEM((4, slots, 8 * slots), f32),
        VMEM((8, 8 * slots), f32),
        VMEM((24, 128), f32),
        VMEM((24, 128), f32),
        VMEM((12, 24, 128), f32),
        VMEM((2 * rows, width), f32),
        VMEM((4, rows, 640), bf16),
        VMEM((width, width), bf16),
        VMEM((width, width), bf16),
        VMEM((width, width), bf16),
        VMEM((3, 4, depth, width), bf16),
        VMEM((3, 3, depth, width), bf16),
        VMEM((width, width), bf16),
        VMEM((width, width), bf16),
        VMEM((2, slots, width), bf16),
        VMEM((8, width), f32),
        VMEM((3, 24, 128), f32),
        VMEM((9, 24, 128), f32),
        VMEM((2 * rows, width), bf16),
        VMEM((depth, width), bf16),
        VMEM((16, 128), bf16),
        VMEM((slots, 256), bf16),
    ]
    for _ in range(4):
        scratch += gather_sems()
    scratch += [DMA((2,)), DMA((2,)), DMA((1,)), DMA((1,)), DMA((1,)), DMA((3, 2)), DMA((3, 2)), DMA((3, 2)), DMA((3, 2))]
    scratch += [DMA((6,)), DMA((4,)), DMA((2,)), DMA((3,)), DMA((3,)), DMA((3,)), DMA((1,)), DMA((10,)), DMA((10,))]
    scratch += [DMA((3, 4)), DMA((3, 3)), DMA((1,)), DMA((10,)), DMA((10,)), DMA((4,)), DMA((8,))]
    return pl.pallas_call(
        functools.partial(layer_kernel, slot_total),
        out_shape=[
            jax.ShapeDtypeStruct((1, 1), f32),
            jax.ShapeDtypeStruct((4 * rows, width), bf16),
            jax.ShapeDtypeStruct((4 * rows, width), bf16),
            jax.ShapeDtypeStruct((depth, width), f32),
            jax.ShapeDtypeStruct((depth, width), f32),
            jax.ShapeDtypeStruct((depth, width), f32),
            jax.ShapeDtypeStruct((4, width), f32),
        ],
        in_specs=[here] * 10 + [there, here],
        out_specs=[here, there, there, here, here, here, here],
        scratch_shapes=scratch,
        compiler_params=pltpu.CompilerParams(
            collective_id=1, has_side_effects=True, vmem_limit_bytes=63 * 2**20
        ),
        cost_estimate=pl.CostEstimate(flops=30 * 10**9, bytes_accessed=40 * 10**6, transcendentals=10**7),
        name="layer",
    )(w_qkv, w_out, up_own, down_own, norms, valid, classes, *rest)


def finish_kernel(*refs):
    (block_in, token_in, attn_in, up_in, down_in) = refs[:5]
    (block_out, token_out, qkv_out, out_out, up_out, down_out) = refs[5:11]
    (narrow, wide, held, mats, qkv, out, sems) = refs[11:]
    parts, rows = narrow.shape[0], narrow.shape[1]
    count = iter(range(sems.shape[0]))

    def copy(src, dst):
        return pltpu.make_async_copy(src, dst, sems.at[next(count)])

    mat_loads = [copy(ref, mats.at[i]) for i, ref in enumerate((attn_in, up_in, down_in))]
    loads, saves, keep_loads, keep_saves = [], [], [], []
    for i in range(parts):
        span = pl.ds(i * rows, rows)
        loads.append(copy(token_in.at[span], narrow.at[i]))
        saves.append(copy(wide.at[i], token_out.at[span]))
        keep_loads.append(copy(block_in.at[span], held.at[i]))
        keep_saves.append(copy(held.at[i], block_out.at[span]))
    for load in mat_loads + loads + keep_loads:
        load.start()
    for load in mat_loads:
        load.wait()
    mat_saves = [copy(mats.at[1], up_out), copy(mats.at[2], down_out)]
    for save in mat_saves:
        save.start()
    for i, (pair, single) in enumerate(((0, 384), (128, 512), (256, 448))):
        qkv[i] = jnp.concatenate([mats[0, :, pair : pair + 128], mats[0, :, single : single + 64]], axis=1)
    depth = mats.shape[1]
    row = lax.broadcasted_iota(jnp.int32, (depth, depth), 0)
    eye = (row == lax.broadcasted_iota(jnp.int32, (depth, depth), 1)).astype(f32).astype(bf16)
    mixed = jnp.concatenate([mats[0, :, 640:768], mats[0, :, 576:640]], axis=1)
    out[...] = sum(tn(part, eye) for part in split_three(mixed))
    mat_saves += [copy(qkv, qkv_out), copy(out, out_out)]
    for save in mat_saves[2:]:
        save.start()
    for i in range(parts):
        loads[i].wait()
        wide[i] = narrow[i].astype(f32)
        saves[i].start()
    for load, save in zip(keep_loads, keep_saves):
        load.wait()
        save.start()
    for save in mat_saves + saves + keep_saves:
        save.wait()


def finish(block_out, token_grad, own_attn, own_up, own_down):
    rows, width = token_grad.shape
    depth = own_up.shape[0]
    parts = 4
    there = pl.BlockSpec(memory_space=pltpu.HBM)
    return pl.pallas_call(
        finish_kernel,
        out_shape=[
            jax.ShapeDtypeStruct(block_out.shape, bf16),
            jax.ShapeDtypeStruct((rows, width), f32),
            jax.ShapeDtypeStruct((3, depth, 192), f32),
            jax.ShapeDtypeStruct((192, depth), f32),
            jax.ShapeDtypeStruct((depth, width), f32),
            jax.ShapeDtypeStruct((depth, width), f32),
        ],
        in_specs=[there] * 5,
        out_specs=[there] * 6,
        scratch_shapes=[
            VMEM((parts, rows // parts, width), bf16),
            VMEM((parts, rows // parts, width), f32),
            VMEM((parts, rows // parts, width), bf16),
            VMEM((3, depth, width), f32),
            VMEM((3, depth, 192), f32),
            VMEM((192, depth), f32),
            DMA((7 + 4 * parts,)),
        ],
        compiler_params=pltpu.CompilerParams(vmem_limit_bytes=63 * 2**20),
        name="finish",
    )(block_out, token_grad, own_attn, own_up, own_down)


def on_kernel(
    tokens,
    segment_ids,
    slot_valid,
    ln1_gain,
    ln1_bias,
    w_qkv,
    w_out,
    ln2_gain,
    ln2_bias,
    w_up,
    w_down,
    class_tokens,
    image_gain,
    image_bias,
    image_proj,
):
    dp_rank = lax.axis_index("dp")
    depth, slots = w_up.shape[0], slot_valid.shape[0]
    loss, block_out, token_grad, own_attn, own_up, own_down, vectors = layer(
        slots * 32,
        w_qkv,
        w_out,
        w_up,
        w_down.T,
        jnp.stack([ln1_gain, ln1_bias, ln2_gain, ln2_bias]),
        slot_valid.reshape(1, slots),
        class_tokens,
        image_gain,
        image_bias,
        image_proj,
        tokens,
        segment_ids.reshape(4, 4, 128),
    )
    block_out, token_grad, qkv_grad, out_grad, own_up, own_down = finish(
        block_out, token_grad, own_attn, own_up, own_down
    )
    vectors = lax.dynamic_slice_in_dim(vectors, dp_rank * depth, depth, 1)
    return (
        loss.reshape(()),
        block_out,
        token_grad,
        vectors[0],
        vectors[1],
        qkv_grad,
        out_grad,
        vectors[2],
        vectors[3],
        own_up,
        own_down.T,
    )


def make(dp_size, mp_size):
    def on_device(
        tokens,
        segment_ids,
        slot_valid,
        ln1_gain,
        ln1_bias,
        w_qkv,
        w_out,
        ln2_gain,
        ln2_bias,
        w_up,
        w_down,
        class_tokens,
        image_gain,
        image_bias,
        image_proj,
    ):
        both = ("dp", "mp")
        dp_rank, mp_rank = lax.axis_index("dp"), lax.axis_index("mp")
        depth = w_up.shape[0]
        width = depth * dp_size
        head_cols = w_out.shape[0]
        heads = head_cols // HEAD_DIM
        rows = tokens.shape[0] // mp_size
        seqs = rows // SEQ_LEN
        slots = slot_valid.shape[0]
        slot_total = slots * dp_size * mp_size

        packed = jnp.stack(
            [jnp.concatenate([w_qkv[0], w_qkv[1], w_qkv[2], w_out.T], axis=1), w_up, w_down.T]
        )
        norms = jnp.stack([ln1_gain, ln1_bias, ln2_gain, ln2_bias])
        image_hat, _ = standardise(class_tokens.astype(f32))
        image_normed = (image_hat * image_gain + image_bias).astype(bf16)
        image_raw = nn(image_normed, image_proj)
        image_unit = (image_raw * inverse_norm(image_raw)).astype(bf16)

        weights = lax.all_gather(packed, both, axis=0).reshape(dp_size, mp_size, 3, depth, -1)
        weights = weights.transpose(2, 1, 0, 3, 4).reshape(3, mp_size, width, -1)
        vectors = lax.all_gather(norms, "dp", axis=1, tiled=True).astype(f32)
        all_image = lax.all_gather(image_unit, both, axis=0, tiled=True)
        all_valid = lax.all_gather(slot_valid.astype(bf16), both, axis=0, tiled=True) > 0

        own = lax.dynamic_slice_in_dim(tokens, mp_rank * rows, rows, 0).astype(f32)
        ids = lax.dynamic_slice_in_dim(segment_ids, mp_rank * rows, rows, 0)
        grid_ids = ids.reshape(seqs, SEQ_LEN)
        first_len = jnp.sum((grid_ids == 0).astype(jnp.int32), axis=1)
        starts = jnp.arange(seqs, dtype=jnp.int32) * SEQ_LEN
        ends = jnp.stack([starts + first_len - 1, starts + SEQ_LEN - 1], axis=1).reshape(2 * seqs)
        place = (ends[:, None] == jnp.arange(rows)[None, :]).astype(bf16)

        hat_one, rstd_one = standardise(own)
        normed = (hat_one * vectors[0] + vectors[1]).astype(bf16)
        attn = weights[0]
        qkv = jnp.einsum("rd,mde->mre", normed, attn[:, :, : 3 * head_cols], preferred_element_type=f32)
        qkv = qkv.astype(bf16).reshape(mp_size, rows, 3, heads, HEAD_DIM)
        blocks = rows // tile_rows
        split = qkv.reshape(mp_size, blocks, tile_rows, 3, heads, HEAD_DIM)
        query, key, value = split[:, :, :, 0], split[:, :, :, 1], split[:, :, :, 2]
        tile_ids = ids.reshape(blocks, tile_rows)
        spots = jnp.arange(tile_rows)
        allowed = (
            (tile_ids[:, :, None] == tile_ids[:, None, :])
            & (spots[:, None] // SEQ_LEN == spots[None, :] // SEQ_LEN)[None]
            & (spots[:, None] >= spots[None, :])[None]
        )[None, :, None]
        scale = HEAD_DIM**-0.5
        scores = jnp.einsum("mbqhc,mbkhc->mbhqk", query, key, preferred_element_type=f32) * scale
        scores = jnp.where(allowed, scores, -1e30)
        probs = jax.nn.softmax(scores, axis=-1)
        mixed = jnp.einsum("mbhqk,mbkhc->mbqhc", probs.astype(bf16), value, preferred_element_type=f32)
        mixed = mixed.astype(bf16).reshape(mp_size, rows, head_cols)
        out_t = attn[:, :, 3 * head_cols :]
        attended = jnp.einsum("mre,mde->rd", mixed, out_t, preferred_element_type=f32)
        hidden = own + attended

        def feed(rows_in):
            hat, rstd = standardise(rows_in)
            normed_two = (hat * vectors[2] + vectors[3]).astype(bf16)
            upper = jnp.einsum("rd,mdf->mrf", normed_two, weights[1], preferred_element_type=f32)
            active = (upper * phi(upper)).astype(bf16)
            branch = jnp.einsum("mrf,mdf->rd", active, weights[2], preferred_element_type=f32)
            return hat, rstd, normed_two, upper, active, rows_in + branch

        block_out = feed(hidden)[-1].astype(bf16)
        hidden_ends = hidden[ends]
        hat_two, rstd_two, normed_two, upper, active, pooled = feed(hidden_ends)

        scale_back = inverse_norm(pooled)
        text = (pooled * scale_back).astype(bf16)
        logits = logit_scale * nt(text, all_image)
        live = slot_valid > 0
        weight = jnp.exp(logits)
        row_sum = jnp.sum(jnp.where(all_valid[None, :], weight, 0.0), axis=1)
        col_part = jnp.sum(jnp.where(live[:, None], weight, 0.0), axis=0)
        row_index = (dp_rank * mp_size + mp_rank) * slots + jnp.arange(slots)
        target = jnp.arange(slot_total)[None, :] == row_index[:, None]
        matched = jnp.sum(jnp.where(target, logits, 0.0), axis=1)
        row_part = jnp.sum(jnp.where(live, jnp.log(row_sum) - 2.0 * matched, 0.0))
        sums = lax.psum(jnp.concatenate([col_part, row_part[None]]), both)
        col_sum = sums[:slot_total]
        loss = 0.5 * (sums[slot_total] + jnp.sum(jnp.where(all_valid, jnp.log(col_sum), 0.0))) / slot_total
        pair = live[:, None] & all_valid[None, :]
        spread = 0.5 * weight * (1.0 / row_sum[:, None] + 1.0 / col_sum[None, :])
        grad_logits = jnp.where(pair, spread, 0.0) - (target & live[:, None]).astype(f32)
        cosine_grad = (logit_scale * grad_logits).astype(bf16)
        unit_grad = nn(cosine_grad, all_image)
        along = jnp.sum(unit_grad * pooled, axis=-1, keepdims=True)
        pooled_grad = scale_back * unit_grad - pooled * (scale_back * scale_back * scale_back * along)

        branch_grad = pooled_grad.astype(bf16)
        down_local = jnp.einsum("rd,mrf->mdf", branch_grad, active, preferred_element_type=f32)
        active_grad = jnp.einsum("rd,mdf->mrf", branch_grad, weights[2], preferred_element_type=f32)
        slope = phi(upper) + upper * jnp.exp(-0.5 * upper * upper) * (1.0 / (2.0 * jnp.pi) ** 0.5)
        upper_grad = (active_grad * slope).astype(bf16)
        up_local = jnp.einsum("rd,mrf->mdf", normed_two, upper_grad, preferred_element_type=f32)
        normed_two_grad = jnp.einsum("mrf,mdf->rd", upper_grad, weights[1], preferred_element_type=f32)
        gain_two = jnp.sum(normed_two_grad * hat_two, axis=0)
        bias_two = jnp.sum(normed_two_grad, axis=0)
        hidden_grad = pooled_grad + norm_pull(normed_two_grad, hat_two, rstd_two, vectors[2])

        attended_grad = hidden_grad.astype(bf16)
        mixed_ends = mixed[:, ends]
        out_local = jnp.einsum("rd,mre->mde", attended_grad, mixed_ends, preferred_element_type=f32)
        mixed_grad = jnp.einsum("rd,mde->mre", attended_grad, out_t, preferred_element_type=f32).astype(bf16)
        mixed_grad = mixed_grad.reshape(mp_size, 2 * seqs, heads, HEAD_DIM)
        query_ends, keys, values = qkv[:, ends, 0], qkv[:, :, 1], qkv[:, :, 2]
        spot = jnp.arange(rows)
        allowed_ends = (
            (ids[ends][:, None] == ids[None, :])
            & (ends[:, None] // SEQ_LEN == spot[None, :] // SEQ_LEN)
            & (ends[:, None] >= spot[None, :])
        )[None, None]
        again = jnp.einsum("mqhc,mkhc->mhqk", query_ends, keys, preferred_element_type=f32) * scale
        probs_ends = jax.nn.softmax(jnp.where(allowed_ends, again, -1e30), axis=-1)
        probs_grad = jnp.einsum("mqhc,mkhc->mhqk", mixed_grad, values, preferred_element_type=f32)
        value_grad = jnp.einsum("mhqk,mqhc->mkhc", probs_ends.astype(bf16), mixed_grad, preferred_element_type=f32)
        centre = jnp.sum(probs_grad * probs_ends, axis=-1, keepdims=True)
        score_grad = (probs_ends * (probs_grad - centre)).astype(bf16)
        query_grad = jnp.einsum("mhqk,mkhc->mqhc", score_grad, keys, preferred_element_type=f32) * scale
        key_grad = jnp.einsum("mhqk,mqhc->mkhc", score_grad, query_ends, preferred_element_type=f32) * scale
        query_grad = query_grad.astype(bf16).reshape(mp_size, 2 * seqs, head_cols)
        query_grad = jnp.einsum("er,mec->mrc", place, query_grad, preferred_element_type=f32).astype(bf16)
        proj_grad = jnp.concatenate(
            [
                query_grad,
                key_grad.astype(bf16).reshape(mp_size, rows, head_cols),
                value_grad.astype(bf16).reshape(mp_size, rows, head_cols),
            ],
            axis=-1,
        )
        qkv_local = jnp.einsum("rd,mre->mde", normed, proj_grad, preferred_element_type=f32)
        normed_grad = jnp.einsum("mre,mde->rd", proj_grad, attn[:, :, : 3 * head_cols], preferred_element_type=f32)
        gain_one = jnp.sum(normed_grad * hat_one, axis=0)
        bias_one = jnp.sum(normed_grad, axis=0)
        token_grad = norm_pull(normed_grad, hat_one, rstd_one, vectors[0])
        token_grad = token_grad.at[ends].add(hidden_grad)

        local = jnp.stack([jnp.concatenate([qkv_local, out_local], axis=-1), up_local, down_local])
        local = local.reshape(3, mp_size, dp_size, depth, -1).transpose(2, 1, 0, 3, 4)
        local = local.reshape(dp_size * mp_size, 3, depth, -1)
        summed = lax.psum_scatter(local, both, scatter_dimension=0, tiled=False)
        vector_local = lax.psum(jnp.stack([gain_one, bias_one, gain_two, bias_two]), both)
        vector_own = lax.dynamic_slice_in_dim(vector_local, dp_rank * depth, depth, 1)

        block_out = lax.all_gather(block_out, "mp", axis=0, tiled=True)
        token_grad = lax.all_gather(token_grad, "mp", axis=0, tiled=True)
        qkv_grad = summed[0, :, : 3 * head_cols].reshape(depth, 3, head_cols).transpose(1, 0, 2)
        return (
            loss,
            block_out,
            token_grad,
            vector_own[0],
            vector_own[1],
            qkv_grad,
            summed[0, :, 3 * head_cols :].T,
            vector_own[2],
            vector_own[3],
            summed[1],
            summed[2].T,
        )

    return on_device


def solution(mesh):
    placed = (
        P("dp", None),
        P("dp"),
        P(("dp", "mp")),
        P("dp"),
        P("dp"),
        P(None, "dp", "mp"),
        P("mp", "dp"),
        P("dp"),
        P("dp"),
        P("dp", "mp"),
        P("mp", "dp"),
        P(("dp", "mp"), None),
        P(),
        P(),
        P(),
    )
    sizes = (mesh.shape["dp"], mesh.shape["mp"])
    return jax.shard_map(
        on_kernel if sizes == (8, 4) else make(*sizes),
        mesh=mesh,
        in_specs=placed,
        out_specs=(
            P(),
            P("dp", None),
            P("dp", None),
            P("dp"),
            P("dp"),
            P(None, "dp", "mp"),
            P("mp", "dp"),
            P("dp"),
            P("dp"),
            P("dp", "mp"),
            P("mp", "dp"),
        ),
        check_vma=False,
    )
```

```python
import jax
import jax.numpy as jnp
from jax import lax
from jax.sharding import PartitionSpec as P
import functools
from jax.experimental import pallas as pl
from jax.experimental.pallas import tpu as pltpu

HEAD_DIM = 64
SEQ_LEN = 16
norm_epsilon = 1e-05
unit_epsilon = 1e-06
logit_scale = 50.0
tile_rows = 128
f32, bf16 = jnp.float32, jnp.bfloat16


def standardise(values):
    centred = values - jnp.mean(values, axis=-1, keepdims=True)
    rstd = lax.rsqrt(jnp.mean(centred * centred, axis=-1, keepdims=True) + norm_epsilon)
    return centred * rstd, rstd


def norm_pull(grad, hat, rstd, gain):
    scaled = grad * gain
    first = jnp.mean(scaled, axis=-1, keepdims=True)
    second = jnp.mean(scaled * hat, axis=-1, keepdims=True)
    return rstd * (scaled - first - hat * second)


def inverse_norm(values):
    return lax.rsqrt(jnp.sum(values * values, axis=-1, keepdims=True) + unit_epsilon)


def nn(left, right):
    return lax.dot_general(left, right, (((1,), (0,)), ((), ())), preferred_element_type=f32)


def nt(left, right):
    return lax.dot_general(left, right, (((1,), (1,)), ((), ())), preferred_element_type=f32)


def tn(left, right):
    return lax.dot_general(left, right, (((0,), (0,)), ((), ())), preferred_element_type=f32)


def phi(values):
    return 0.5 * lax.erfc(-values * (0.5**0.5))


MESH = pl.DeviceIdType.MESH
VMEM, DMA = pltpu.VMEM, pltpu.SemaphoreType.DMA
CUT = 48
WINDOW = 3


def loop(count, body):
    lax.fori_loop(0, count, lambda i, carry: (body(i), carry)[1], 0)


def rows_of(index, size):
    return pl.ds(pl.multiple_of(index * size, size), size)


def split_three(values):
    first = values.astype(bf16)
    rest = values - first.astype(f32)
    second = rest.astype(bf16)
    return first, second, (rest - second.astype(f32)).astype(bf16)


def pick(place, values):
    return sum(nn(place, part) for part in split_three(values))


def spread_rows(place, values):
    return sum(tn(place, part) for part in split_three(values))


def half_erf(values):
    return 0.5 + 0.5 * lax.erf(values * (0.5**0.5))


def layer_kernel(slot_total, *refs):
    (w_qkv, w_out, up_own, down_own) = refs[:4]
    norms = refs[4:8]
    (valid_own, classes, image_gain, image_bias, image_proj, tokens, ids) = refs[8:15]
    (loss_out, block_out, token_out, attn_out, up_out, down_out, vec_out) = refs[15:22]
    (w_attn, w_up, w_down, images, smalls, x_ref, a_ref, qkv, hidden, a_two, active, stage_out, image_own, vecs) = refs[22:36]
    (mask_ref, place_ref, member_ref, h_ends, ends_two, ends_grad, u_ends, g_all, s_all, weight_ref, valid_ref) = refs[36:47]
    (sum_own, sum_buf, sum_got, d_attn, d_far) = refs[47:52]
    (grad_down, grad_up, grad_attn, step_x, step_z, attn_send, attn_core, ends_back) = refs[52:60]
    (vec_buf, vec_pack, vec_got, stage_grad, attn_own, small_own, far_mix) = refs[60:67]
    gsems = refs[67:95]
    isems = refs[95:104]
    (s_local, s_bo, s_on, s_send, s_a2, s_dm, s_dh, s_sum, s_sums, s_x, s_z, s_core, s_v, s_vs, s_tg, s_exs) = refs[104:120]

    dp = lax.axis_index("dp")
    mp = lax.axis_index("mp")
    z = lax.div(dp, 2)
    x = lax.rem(dp, 2)
    y = lax.div(mp, 2)
    c = lax.rem(mp, 2)
    xd, ym, cm = 2 * z + (1 - x), 2 * (1 - y) + c, 2 * y + (1 - c)
    zt = [lax.rem(z + j, 4) for j in range(4)]
    zs = [lax.rem(z + 4 - j, 4) for j in range(4)]
    X, Y, C, YC = (xd, mp), (dp, ym), (dp, cm), (dp, 3 - mp)
    Z = [(2 * zt[j] + x, mp) for j in range(4)]
    here = 4 * x + mp
    PLANE = []
    for j in range(1, 8):
        other = lax.rem(here + j, 8)
        PLANE.append((2 * z + lax.div(other, 4), lax.rem(other, 4)))
    G = [(dp, lax.rem(mp + j, 4)) for j in range(4)]

    peers = PLANE + Z[1:]
    barrier = pltpu.get_barrier_semaphore()
    for peer in peers:
        pl.semaphore_signal(barrier, inc=1, device_id=peer, device_id_type=MESH)
    pl.semaphore_wait(barrier, len(peers))

    def remote(src, dst, send_sem, recv_sem, device):
        copy = pltpu.make_async_remote_copy(
            src_ref=src, dst_ref=dst, send_sem=send_sem, recv_sem=recv_sem, device_id=device, device_id_type=MESH
        )
        copy.start()
        return copy

    def arrived(ref, recv_sem, send_sem):
        pltpu.make_async_remote_copy(
            src_ref=ref, dst_ref=ref, send_sem=send_sem, recv_sem=recv_sem, device_id=X, device_id_type=MESH
        ).wait_recv()

    def gather_steps(src, out, rows, cut, sems):
        zr, x0, y1, y0, x1, cr, sd = sems
        first = (0, cut) if cut else (0, rows)
        second = (cut, rows - cut) if cut else None
        full = (0, rows)

        def piece(d, m, span):
            return out.at[m, pl.ds(pl.multiple_of(d * rows + span[0], 16), span[1])]

        def send(src_ref, dst_ref, sem, device):
            remote(src_ref, dst_ref, sd.at[0], sem, device)

        def got(ref, sem):
            arrived(ref, sem, sd.at[0])

        def step0():
            for j in range(1, 4):
                send(src, piece(dp, mp, full), zr.at[j], Z[j])
            send(src.at[pl.ds(*first)], piece(dp, mp, first), x0.at[0], X)
            if second:
                send(src.at[pl.ds(*second)], piece(dp, mp, second), y1.at[0], Y)
            send(src.at[pl.ds(*first)], piece(dp, mp, first), y0.at[0], Y)
            if second:
                send(src.at[pl.ds(*second)], piece(dp, mp, second), x1.at[0], X)
            send(src, piece(dp, mp, full), cr.at[0], C)
            pltpu.make_async_copy(src, piece(dp, mp, full), sd.at[0]).start()
            yield

        def step1():
            for j in range(1, 4):
                d = 2 * zs[j] + x
                block = piece(d, mp, full)
                got(block, zr.at[j])
                one = piece(d, mp, first)
                send(one, one, x0.at[j], X)
                if second:
                    two = piece(d, mp, second)
                    send(two, two, y1.at[j], Y)
                send(one, one, y0.at[j], Y)
                if second:
                    send(two, two, x1.at[j], X)
                send(block, block, cr.at[0], C)
                yield

        def step2():
            for j in range(4):
                one = piece(2 * zs[j] + (1 - x), mp, first)
                got(one, x0.at[j])
                send(one, one, y0.at[4 + j], Y)
                send(one, one, cr.at[0], C)
                if second:
                    two = piece(2 * zs[j] + x, ym, second)
                    got(two, y1.at[j])
                    send(two, two, x1.at[4 + j], X)
                    send(two, two, cr.at[0], C)
                yield

        def step3():
            for i in range(2):
                for j in range(4):
                    one = piece(2 * zs[j] + (x if i == 0 else 1 - x), ym, first)
                    got(one, y0.at[4 * i + j])
                    send(one, one, cr.at[0], C)
                    if second:
                        two = piece(2 * zs[j] + (1 - x), (mp if i == 0 else ym), second)
                        got(two, x1.at[4 * i + j])
                        send(two, two, cr.at[0], C)
                    yield

        def step4():
            half = out.at[pl.ds(0, 2)]
            pltpu.make_async_copy(half, half, cr.at[0]).wait()
            pltpu.make_async_copy(out, out, sd.at[0]).wait()
            yield

        return [step0, step1, step2, step3, step4]

    depth = up_own.shape[0]
    slots = classes.shape[0]

    def image_steps():
        near, cross, core, near_sent, core_sent, up_got, down_got, up_sent, down_sent = isems

        def at(d, m, start=0, size=slots):
            return images.at[m, pl.ds(pl.multiple_of(d * slots + start, 16), size)]

        def plane(z_, i):
            return images.at[2 * i + c, pl.ds(pl.multiple_of(2 * z_ * slots, 16), 2 * slots)]

        def to_core(ref):
            remote(ref, ref, core_sent.at[0], core.at[0], C)

        half = slots // 2

        def step0():
            remote(image_own, at(dp, mp), near_sent.at[0], near.at[0], X)
            remote(image_own, at(dp, mp), near_sent.at[0], near.at[1], Y)
            remote(image_own, at(dp, mp), core_sent.at[0], core.at[0], C)
            pltpu.make_async_copy(image_own, at(dp, mp), s_local.at[5]).start()
            yield

        def step1():
            arrived(at(xd, mp), near.at[0], near_sent.at[0])
            remote(at(xd, mp, 0, half), at(xd, mp, 0, half), near_sent.at[0], cross.at[0], Y)
            to_core(at(xd, mp))
            arrived(at(dp, ym), near.at[1], near_sent.at[0])
            remote(at(dp, ym, half, half), at(dp, ym, half, half), near_sent.at[0], cross.at[1], X)
            to_core(at(dp, ym))
            yield

        def up(i, t):
            ref = plane(z - t, i)
            return pltpu.make_async_remote_copy(
                src_ref=ref, dst_ref=ref, send_sem=up_sent.at[t, i], recv_sem=up_got.at[t, i],
                device_id=(2 * (z + 1) + x, mp), device_id_type=MESH,
            )

        def down(i, t):
            ref = plane(z + t, i)
            return pltpu.make_async_remote_copy(
                src_ref=ref, dst_ref=ref, send_sem=down_sent.at[t, i], recv_sem=down_got.at[t, i],
                device_id=(2 * (z - 1) + x, mp), device_id_type=MESH,
            )

        def step2():
            arrived(at(xd, ym, 0, half), cross.at[0], near_sent.at[0])
            arrived(at(xd, ym, half, half), cross.at[1], near_sent.at[0])
            to_core(at(xd, ym))
            pltpu.make_async_copy(image_own, at(dp, mp), s_local.at[5]).wait()
            for i in range(2):
                pl.when(z < 3)(lambda i=i: up(i, 0).start())
                pl.when(z > 0)(lambda i=i: down(i, 0).start())
            yield

        def step3():
            for t in range(1, 4):
                for i in range(2):

                    def from_below(i=i, t=t):
                        ref = plane(z - t, i)
                        arrived(ref, up_got.at[t - 1, i], near_sent.at[0])
                        if t < 3:
                            pl.when(z < 3)(lambda: up(i, t).start())
                        to_core(ref)

                    def from_above(i=i, t=t):
                        ref = plane(z + t, i)
                        arrived(ref, down_got.at[t - 1, i], near_sent.at[0])
                        if t < 3:
                            pl.when(z > 0)(lambda: down(i, t).start())
                        to_core(ref)

                    pl.when(z >= t)(from_below)
                    pl.when(z + t <= 3)(from_above)
                    yield

        def step4():
            halves = images.at[pl.ds(0, 2)]
            pltpu.make_async_copy(halves, halves, core.at[0]).wait()
            pltpu.make_async_copy(halves, halves, core_sent.at[0]).wait()
            three = images.at[0, pl.ds(0, 3 * slots)]
            pltpu.make_async_copy(three, three, near_sent.at[0]).wait()
            for t in range(3):
                for i in range(2):
                    pl.when((z >= t) & (z < 3))(lambda i=i, t=t: up(i, t).wait_send())
                    pl.when((z + t <= 3) & (z > 0))(lambda i=i, t=t: down(i, t).wait_send())
            yield

        return [step0, step1, step2, step3, step4]

    kinds = {
        "S": gather_steps(small_own, smalls, 16, 0, gsems[0:7]),
        "A": gather_steps(attn_own, w_attn, depth, CUT, gsems[7:14]),
        "U": gather_steps(up_own, w_up, depth, CUT, gsems[14:21]),
        "D": gather_steps(down_own, w_down, depth, CUT, gsems[21:28]),
        "I": image_steps(),
    }

    def run(*steps):
        for name in steps:
            for _ in kinds[name[0]][int(name[1])]():
                pass

    def blend(steps, chunks):
        chunks = list(chunks)
        micro = [kinds[name[0]][int(name[1])] for name in steps]
        count = sum((1, 3, 4, 8, 1)[int(name[1])] if name[0] != "I" else (1, 1, 1, 6, 1)[int(name[1])] for name in steps)
        done, at = 0, 0
        for step in micro:
            for _ in step():
                at += 1
                while done < len(chunks) and done * count < at * len(chunks):
                    chunks[done]()
                    done += 1
        for chunk in chunks[done:]:
            chunk()

    lane = lax.broadcasted_iota(jnp.int32, (128, 128), 1)
    sub = lax.broadcasted_iota(jnp.int32, (128, 128), 0)
    low = lax.broadcasted_iota(jnp.int32, (1, 128), 1) < 64
    token_rows = hidden.shape[0]
    tiles = token_rows // 128
    end_count = h_ends.shape[0]

    def keep_low(values):
        return jnp.where(low, values, jnp.zeros_like(values))

    def keep_high(values):
        return jnp.where(low, jnp.zeros_like(values), values)

    def pack_own():
        rows = lax.broadcasted_iota(jnp.int32, (depth, depth), 0)
        eye = (rows == lax.broadcasted_iota(jnp.int32, (depth, depth), 1)).astype(f32).astype(bf16)
        out_t = nt(eye, w_out[...]).astype(bf16)
        query, key, value = w_qkv[0], w_qkv[1], w_qkv[2]
        attn_own[:, 0:128] = query[:, 0:128]
        attn_own[:, 128:256] = key[:, 0:128]
        attn_own[:, 256:384] = value[:, 0:128]
        attn_own[:, 384:512] = jnp.concatenate([query[:, 128:192], value[:, 128:192]], axis=1)
        attn_own[:, 512:640] = jnp.concatenate([key[:, 128:192], out_t[:, 128:192]], axis=1)
        attn_own[:, 640:768] = out_t[:, 0:128]

    def pack_small():
        shift = lax.broadcasted_iota(jnp.int32, (depth, 384), 1) - lax.broadcasted_iota(jnp.int32, (depth, 384), 0)
        made = nn(jnp.concatenate([row[...].astype(f32) for row in norms], axis=0).astype(bf16), (shift == depth * lax.rem(dp, 4)).astype(f32).astype(bf16))
        shift = lax.broadcasted_iota(jnp.int32, (slots, 128), 1) - lax.broadcasted_iota(jnp.int32, (slots, 128), 0)
        flags = jnp.broadcast_to(valid_own[...].astype(f32), (8, slots)).astype(bf16)
        flags = nn(flags, (shift == slots * lax.rem(dp, 2)).astype(f32).astype(bf16))
        parts = [made[v : v + 1, 128 * t : 128 * (t + 1)] for v in range(4) for t in range(3)]
        small_own[...] = jnp.concatenate(parts + [flags[0:4, :]], axis=0).astype(bf16)

    def masks(g):
        slot_row = lax.broadcasted_iota(jnp.int32, (end_count, 128), 0)
        spots = []
        best = jnp.full((end_count, 1), -1, jnp.int32)
        for b in range(tiles):
            sequence = 8 * b + lax.shift_right_logical(lax.broadcasted_iota(jnp.int32, (1, 128), 1), 4)
            caption = 2 * sequence + ids[ym if g else mp, pl.ds(b, 1), :]
            column = jnp.sum(jnp.where(lane == sub, caption, 0), axis=1, keepdims=True)
            mask_ref[tiles * g + b] = jnp.where((column == caption) & (sub >= lane), 0.0, -1e30)
            member = slot_row == caption
            spot = lax.broadcasted_iota(jnp.int32, (end_count, 128), 1) + 128 * b
            best = jnp.maximum(best, jnp.max(jnp.where(member, spot, -1), axis=1, keepdims=True))
            member_ref[g, :, 128 * b : 128 * (b + 1)] = jnp.where(member, 0.0, -1e30)
            spots.append(spot)
        for b in range(tiles):
            place_ref[g, :, 128 * b : 128 * (b + 1)] = (spots[b] == best).astype(f32).astype(bf16)

    def image_tower():
        hat, _ = standardise(classes[...].astype(f32))
        raw = nn((hat * image_gain[...].reshape(1, -1) + image_bias[...].reshape(1, -1)).astype(bf16), image_proj[...])
        image_own[...] = (raw * inverse_norm(raw)).astype(bf16)

    def small_vectors():
        halves = []
        for w in range(2):
            halves.append(sum(smalls[0, 64 * w + 16 * d : 64 * w + 16 * (d + 1), :].astype(f32) for d in range(4)))
        for v in range(4):
            for w in range(2):
                for t in range(3):
                    at = 384 * w + 128 * t
                    vecs[v : v + 1, at : at + 128] = halves[w][3 * v + t : 3 * v + t + 1, :]
        for m in range(4):
            for pair in range(4):
                both = sum(smalls[m, 32 * pair + 16 * d : 32 * pair + 16 * (d + 1), :].astype(f32) for d in range(2))
                valid_ref[m : m + 1, 128 * pair : 128 * (pair + 1)] = both[12:13, :]

    def first_norm(g):
        def body(b):
            rows = rows_of(tiles * g + b, 128)
            values = x_ref[rows, :].astype(f32)
            hat, _ = standardise(values)
            a_ref[rows, :] = (hat * vecs[0:1, :] + vecs[1:2, :]).astype(bf16)
            if g == 0:
                hidden[rows, :] = values

        loop(tiles, body)

    def soft(scores):
        top = jnp.max(scores, axis=-1, keepdims=True)
        raised = jnp.exp(scores - top)
        return raised * (1.0 / jnp.sum(raised, axis=-1, keepdims=True))

    scale = HEAD_DIM**-0.5

    def project(m, g):
        def body(b):
            rows = rows_of(2 * g + b, 256)
            qkv[m, rows, :] = nn(a_ref[rows, :], w_attn[m]).astype(bf16)

        loop(2, body)

    def attention(m):
        project(m, 0)

        def body(pair):
            for b in (2 * pair, 2 * pair + 1):
                rows = rows_of(b, 128)
                q01, k01, v01, qv, ko = (qkv[m, rows, 128 * i : 128 * (i + 1)] for i in range(5))
                mask = mask_ref[b]
                p0 = soft(nt(keep_low(q01), k01) * scale + mask).astype(bf16)
                p1 = soft(nt(keep_high(q01), k01) * scale + mask).astype(bf16)
                p2 = soft(nt(keep_low(qv), ko) * scale + mask).astype(bf16)
                o01 = jnp.where(low, nn(p0, v01), nn(p1, v01)).astype(bf16)
                o2 = keep_high(nn(p2, qv)).astype(bf16)
                qkv[m, rows, 512:640] = keep_low(ko) + o2
                qkv[m, rows, 640:768] = o01

        loop(tiles // 2, body)

        def attended(b):
            rows = rows_of(b, 256)
            mixed = jnp.concatenate([keep_high(qkv[m, rows, 512:640]), qkv[m, rows, 640:768]], axis=1)
            hidden[rows, :] += nt(mixed, w_attn[m, :, 512:768])

        loop(2, attended)

    def second_norm():
        def body(b):
            rows = rows_of(b, 128)
            hat, _ = standardise(hidden[rows, :])
            a_two[rows, :] = (hat * vecs[2:3, :] + vecs[3:4, :]).astype(bf16)

        loop(tiles, body)
        place = place_ref[0]
        ends = pick(place, hidden[...])
        h_ends[...] = ends
        hat, _ = standardise(ends)
        ends_two[mp] = (hat * vecs[2:3, :] + vecs[3:4, :]).astype(bf16)

    def ends_up(m):
        u_ends[m] = nn(ends_two[mp], w_up[m])

    def full_up(m):
        def body(b):
            rows = rows_of(b, 256)
            upper = nn(a_two[rows, :], w_up[m])
            active[m, rows, :] = (upper * half_erf(upper)).astype(bf16)

        loop(tiles // 2, body)

    def slope_of(upper):
        return half_erf(upper) + upper * jnp.exp(-0.5 * upper * upper) * (1.0 / (2.0 * jnp.pi) ** 0.5)

    def group_up(start):
        def body(i):
            upper = nn(ends_two[start + i], w_up[mp])
            rows = rows_of(start + i, end_count)
            g_all[rows, :] = (upper * half_erf(upper)).astype(bf16)
            s_all[rows, :] = slope_of(upper)

        loop(2, body)

    def full_down(b):
        rows = slice(256 * b, 256 * (b + 1))

        def body(m, total):
            return total + nt(active[m, rows, :], w_down[m])

        stage_out[rows, :] = lax.fori_loop(0, 4, body, hidden[rows, :]).astype(bf16)

    token_copies = []
    for g in range(2):
        wanted = tokens.at[rows_of(ym if g else mp, token_rows)]
        token_copies.append(pltpu.make_async_copy(wanted, x_ref.at[pl.ds(g * token_rows, token_rows)], s_local.at[g]))
        token_copies[g].start()
    pack_small()
    run("S0")
    pack_own()
    run("A0")
    image_tower()
    run("I0", "U0")
    masks(0)
    masks(1)
    run("S1", "A1", "D0", "I1", "S2", "A2", "I2", "U1", "S3", "S4")
    small_vectors()
    for g in range(2):
        token_copies[g].wait()
        first_norm(g)
    run("D1", "A3", "A4")
    blend(("U2", "I3", "D2", "U3"), [functools.partial(attention, m) for m in range(4)])
    second_norm()
    swaps = [remote(ends_two.at[mp], ends_two.at[mp], s_exs.at[j - 1], s_a2.at[j - 1], G[j]) for j in range(1, 4)]
    run("U4")
    blend(("D3",), [functools.partial(full_up, m) for m in range(4)])
    loop(4, ends_up)
    run("I4")
    for swap in swaps:
        swap.wait()
    run("D4")

    pooled = h_ends[...]
    for m in range(4):
        upper = u_ends[m]
        pooled = pooled + nt((upper * half_erf(upper)).astype(bf16), w_down[m])
    scale_back = inverse_norm(pooled)
    text = (pooled * scale_back).astype(bf16)
    own_valid = small_own[12:13, :].astype(f32)
    own_valid = jnp.max(
        jnp.where(
            lax.rem(lax.broadcasted_iota(jnp.int32, (slots, 128), 1), slots)
            == lax.broadcasted_iota(jnp.int32, (slots, 128), 0),
            own_valid,
            0.0,
        ),
        axis=1,
        keepdims=True,
    )
    live = own_valid > 0.0
    place_col = lax.broadcasted_iota(jnp.int32, (slots, 512), 1)
    place_row = lax.broadcasted_iota(jnp.int32, (slots, 512), 0)

    def target_of(m):
        return (place_col == place_row + dp * slots) & (mp == m)

    row_sum = jnp.zeros((slots, 1), f32)
    matched = jnp.zeros((slots, 1), f32)
    for m in range(4):
        logits = logit_scale * nt(text, images[m])
        weight = jnp.exp(logits)
        matched = matched + jnp.sum(jnp.where(target_of(m), logits, 0.0), axis=1, keepdims=True)
        seen = jnp.where(valid_ref[m : m + 1, :] > 0.0, weight, 0.0)
        weight_ref[m] = seen
        row_sum = row_sum + jnp.sum(seen, axis=1, keepdims=True)
        columns = jnp.sum(jnp.where(live, weight, 0.0), axis=0, keepdims=True)
        for part in range(4):
            sum_own[4 * m + part : 4 * m + part + 1, :] = columns[:, 128 * part : 128 * (part + 1)]
    row_part = jnp.sum(jnp.where(live, jnp.log(row_sum) - 2.0 * matched, 0.0), axis=0, keepdims=True)
    sum_own[16:24, :] = jnp.broadcast_to(row_part, (8, 128))

    swaps = [remote(sum_own, sum_got.at[here], s_sums.at[j - 1], s_sum.at[j - 1], PLANE[j - 1]) for j in range(1, 8)]
    sum_got[here] = sum_own[...]
    group_up(0)
    for swap in swaps:
        swap.wait()
    sum_buf[...] = ((sum_got[0] + sum_got[1]) + (sum_got[2] + sum_got[3])) + (
        (sum_got[4] + sum_got[5]) + (sum_got[6] + sum_got[7])
    )
    swaps = [remote(sum_buf, sum_got.at[8 + z], s_sums.at[6 + j], s_sum.at[6 + j], Z[j]) for j in range(1, 4)]
    sum_got[8 + z] = sum_buf[...]
    group_up(2)
    for swap in swaps:
        swap.wait()
    sums = (sum_got[8] + sum_got[9]) + (sum_got[10] + sum_got[11])

    total = sums[16:17, 0:1]
    unit_grad = jnp.zeros((slots, text.shape[1]), f32)
    for m in range(4):
        columns = jnp.concatenate([sums[4 * m + part : 4 * m + part + 1, :] for part in range(4)], axis=1)
        seen = valid_ref[m : m + 1, :] > 0.0
        total = total + jnp.sum(jnp.where(seen, jnp.log(columns), 0.0), axis=1, keepdims=True)
        spread = 0.5 * weight_ref[m] * (1.0 / row_sum + 1.0 / columns)
        grad = jnp.where(seen & live, spread, 0.0) - jnp.where(target_of(m) & live, 1.0, 0.0)
        unit_grad = unit_grad + nn((logit_scale * grad).astype(bf16), images[m])
    loss_out[...] = total * (0.5 / slot_total)
    along = jnp.sum(unit_grad * pooled, axis=-1, keepdims=True)
    pooled_grad = scale_back * unit_grad - pooled * (scale_back * scale_back * scale_back * along)
    branch_grad = pooled_grad.astype(bf16)
    ends_grad[mp] = branch_grad
    swaps = [remote(ends_grad.at[mp], ends_grad.at[mp], s_exs.at[2 + j], s_dm.at[j - 1], G[j]) for j in range(1, 4)]

    def two_part(m):
        upper_grad = (nn(branch_grad, w_down[m]) * slope_of(u_ends[m])).astype(bf16)
        return nt(upper_grad, w_up[m])

    two_grad = two_part(0) + two_part(1)

    def block(z_, x_):
        return pl.ds(pl.multiple_of((2 * z_ + x_) * depth, 16), depth)

    grads, outs = [grad_down, grad_up, grad_attn], [down_out, up_out, attn_out]

    order = [(k, j) for k in range(3) for j in (2, 1, 3, 0)]
    sent, added = iter(order), iter(order)

    def sum_start(count):
        for _ in range(count):
            k, j = next(sent, (None, None))
            if k is not None:
                remote(grads[k].at[block(zt[j], 1 - x)], step_x.at[k, j], s_send.at[k], s_x.at[k, j], X)

    def sum_add(k, j):
        arrived(step_x.at[k, j], s_x.at[k, j], s_send.at[k])
        mine = block(zt[j], x)
        summed = grads[k][mine, :].astype(f32) + step_x[k, j].astype(f32)
        if j:
            grads[k][mine, :] = summed.astype(bf16)
            remote(grads[k].at[mine], step_z.at[k, j - 1], s_send.at[k], s_z.at[k, j - 1], Z[j])
        else:
            outs[k][...] = summed

    def sum_end(k):
        for j in range(1, 4):
            arrived(step_z.at[k, j - 1], s_z.at[k, j - 1], s_send.at[k])
        outs[k][...] = outs[k][...] + step_z[k, 0].astype(f32) + step_z[k, 1].astype(f32) + step_z[k, 2].astype(f32)
        sent = grads[k].at[pl.ds(0, 7 * depth)]
        pltpu.make_async_copy(sent, sent, s_send.at[k]).wait()

    def sum_some(count):
        for _ in range(count):
            sum_start(1)
            sum_add(*next(added))

    for swap in swaps:
        swap.wait()
    group_grad = ends_grad[...].reshape(4 * end_count, -1)
    upper_grad = (nn(group_grad, w_down[mp]) * s_all[...]).astype(bf16)
    grad_down[...] = tn(group_grad, g_all[...]).astype(bf16)

    sum_start(WINDOW)
    grad_up[...] = tn(ends_two[...].reshape(4 * end_count, -1), upper_grad).astype(bf16)

    two_grad = two_grad + two_part(2) + two_part(3)
    hat_two, rstd_two = standardise(h_ends[...])
    vec_buf[...] = jnp.zeros_like(vec_buf)
    vec_buf[2:3, :] = jnp.sum(two_grad * hat_two, axis=0, keepdims=True)
    vec_buf[3:4, :] = jnp.sum(two_grad, axis=0, keepdims=True)
    hidden_grad = pooled_grad + norm_pull(two_grad, hat_two, rstd_two, vecs[2:3, :])
    ends_back[0] = hidden_grad.astype(bf16)
    back_swap = remote(ends_back.at[0], ends_back.at[1], s_exs.at[6], s_dh.at[0], Y)

    def attention_back(m, g, mix=False):
        place = place_ref[g]
        member = member_ref[g]
        ends_row = ends_back[g]
        span = slice(token_rows * g, token_rows * (g + 1))
        k01, v01, qv, ko = (qkv[m, span, 128 * i : 128 * (i + 1)] for i in range(1, 5))
        q_e = nn(place, qkv[m, span, 0:128]).astype(bf16)
        q2_e = keep_low(nn(place, qv)).astype(bf16)
        do01 = nn(ends_row, w_attn[m, :, 640:768]).astype(bf16)
        do2 = keep_high(nn(ends_row, w_attn[m, :, 512:640])).astype(bf16)

        def head(query, keys, values, outer):
            probs = soft(nt(query, keys) * scale + member)
            probs_grad = nt(outer, values)
            centre = jnp.sum(probs_grad * probs, axis=-1, keepdims=True)
            return probs.astype(bf16), (probs * (probs_grad - centre)).astype(bf16)

        p0, ds0 = head(keep_low(q_e), k01, v01, keep_low(do01))
        p1, ds1 = head(keep_high(q_e), k01, v01, keep_high(do01))
        p2, ds2 = head(q2_e, ko, qv, do2)
        dq01 = (jnp.where(low, nn(ds0, k01), nn(ds1, k01)) * scale).astype(bf16)
        dq2 = keep_low(nn(ds2, ko) * scale).astype(bf16)
        if g == 1 and mix:
            far_mix[:, 0:128] = nn(p2, qv).astype(bf16)
            far_mix[:, 128:256] = jnp.where(low, nn(p0, v01), nn(p1, v01)).astype(bf16)
        d_ref = d_far if g else active
        d_ref[m, :, 0:128] = tn(place, dq01).astype(bf16)
        d_ref[m, :, 128:256] = (jnp.where(low, tn(ds0, q_e), tn(ds1, q_e)) * scale).astype(bf16)
        d_ref[m, :, 256:384] = jnp.where(low, tn(p0, do01), tn(p1, do01)).astype(bf16)
        d_ref[m, :, 384:512] = jnp.where(low, tn(place, dq2), tn(p2, do2)).astype(bf16)
        d_ref[m, :, 512:640] = keep_low(tn(ds2, q2_e) * scale).astype(bf16)

    def token_back(g):
        d_ref = d_far if g else active

        def body(b):
            rows = rows_of(b, 256)
            total = jnp.zeros((256, d_attn.shape[1]), f32)
            for m in range(4):
                total = total + nt(d_ref[m, rows, 0:640], w_attn[m, :, 0:640])
            d_attn[rows_of(2 * g + b, 256), :] = total

        loop(2, body)

    def attn_grad(m):
        ends_mix = nn(place_ref[0], qkv[m, 0:token_rows, 512:768]).astype(bf16)
        outer = tn(ends_back[0], ends_mix) + tn(ends_back[1], far_mix[...])

        def made(start, stop):
            span = slice(start, stop)
            return tn(a_ref[0:token_rows, :], active[m, :, span]) + tn(a_ref[token_rows:, :], d_far[m, :, span])

        last = jnp.where(low, made(512, 640), outer[:, 0:128])
        return jnp.concatenate([made(0, 512), last, outer[:, 128:256]], axis=1)

    full_down(0)
    sum_some(1)
    back_swap.wait()
    full_down(1)
    own_rows = rows_of(mp, token_rows)
    far_rows = rows_of(ym, token_rows)
    out_swaps = [
        remote(stage_out, block_out.at[own_rows], s_bo.at[0], s_bo.at[1], Y),
        remote(stage_out, block_out.at[own_rows], s_bo.at[2], s_bo.at[3], C),
    ]
    keep_out = pltpu.make_async_copy(stage_out, block_out.at[own_rows], s_local.at[2])
    keep_out.start()

    def both_back(m, mix=False):
        project(m, 1)
        attention_back(m, 0, mix)
        attention_back(m, 1, mix)
        sum_some(1)

    sum_some(1)
    m = 2 * y + (1 - c)
    both_back(m, True)
    attn_send[...] = attn_grad(m).astype(bf16)
    core_swap = remote(attn_send, attn_core, s_exs.at[7], s_core.at[0], C)
    sum_some(1)
    m = 2 * y + c
    both_back(m, True)
    made = attn_grad(m)
    core_swap.wait()
    grad_attn[...] = (made + attn_core[...].astype(f32)).astype(bf16)
    sum_some(1)
    for i in range(2):
        both_back(2 * (1 - y) + i)

    def token_end(g):
        def body(b):
            rows = rows_of(tiles * g + b, 128)
            hat, rstd = standardise(x_ref[rows, :].astype(f32))
            grad = d_attn[rows, :]
            if g == 0:
                vec_buf[0:1, :] += jnp.sum(grad * hat, axis=0, keepdims=True)
                vec_buf[1:2, :] += jnp.sum(grad, axis=0, keepdims=True)
            d_attn[rows, :] = norm_pull(grad, hat, rstd, vecs[0:1, :])

        loop(tiles, body)
        span = slice(token_rows * g, token_rows * (g + 1))
        stage_grad[span, :] = (d_attn[span, :] + tn(place_ref[g], ends_back[g])).astype(bf16)

    grad_swaps, keep_grads = [], []
    out_swaps[0].wait()
    on = remote(block_out.at[far_rows], block_out.at[far_rows], s_on.at[0], s_on.at[1], C)
    for g in range(2):
        token_back(g)
        token_end(g)
        if g == 0:
            for v in range(4):
                for t in range(6):
                    vec_pack[0, 6 * v + t : 6 * v + t + 1, :] = vec_buf[v : v + 1, 128 * t : 128 * (t + 1)]
            core_vec = remote(vec_pack.at[0], vec_got.at[0], s_vs.at[0], s_v.at[0], C)
        ref = stage_grad.at[pl.ds(token_rows * g, token_rows)]
        spot = token_out.at[far_rows if g else own_rows]
        grad_swaps.append(remote(ref, spot, s_tg.at[2 * g], s_tg.at[2 * g + 1], C))
        keep_grads.append(pltpu.make_async_copy(ref, spot, s_local.at[3 + g]))
        keep_grads[g].start()
        sum_some(1)
    core_vec.wait()
    vec_pack[1] = vec_pack[0] + vec_got[0]
    across = [X, Y, (2 * z + (1 - x), ym)]
    vec_swaps = [
        remote(vec_pack.at[1], vec_got.at[1 + 2 * y + x], s_vs.at[1 + j], s_v.at[1 + j], across[j]) for j in range(3)
    ]
    vec_got[1 + 2 * y + x] = vec_pack[1]
    sum_some(1)
    for swap in vec_swaps:
        swap.wait()
    vec_pack[2] = (vec_got[1] + vec_got[2]) + (vec_got[3] + vec_got[4])
    vec_swaps = [
        remote(vec_pack.at[2], vec_got.at[5 + z], s_vs.at[3 + j], s_v.at[3 + j], Z[j]) for j in range(1, 4)
    ]
    vec_got[5 + z] = vec_pack[2]
    sum_some(1)
    for swap in vec_swaps:
        swap.wait()
    total = (vec_got[5] + vec_got[6]) + (vec_got[7] + vec_got[8])
    for v in range(4):
        for t in range(6):
            vec_out[v : v + 1, 128 * t : 128 * (t + 1)] = total[6 * v + t : 6 * v + t + 1, :]
    sum_end(0)
    sum_end(1)
    sum_end(2)
    out_swaps[1].wait()
    on.wait()
    keep_out.wait()
    for swap in grad_swaps + keep_grads:
        swap.wait()


def layer(slot_total, w_qkv, w_out, up_own, down_own, norms, valid, classes, *rest):
    depth, width = up_own.shape
    slots = classes.shape[0]
    rows = rest[3].shape[0] // 4

    def gather_sems():
        return [DMA((4,)), DMA((4,)), DMA((4,)), DMA((8,)), DMA((8,)), DMA((1,)), DMA((1,))]

    here, there = pl.BlockSpec(memory_space=VMEM), pl.BlockSpec(memory_space=pltpu.HBM)
    square = VMEM((4, width, width), bf16)
    scratch = [
        square,
        square,
        square,
        VMEM((4, 8 * slots, width), bf16),
        VMEM((4, 128, 128), bf16),
        VMEM((2 * rows, width), bf16),
        VMEM((2 * rows, width), bf16),
        VMEM((4, 2 * rows, width), bf16),
        VMEM((rows, width), f32),
        VMEM((rows, width), bf16),
        VMEM((4, rows, width), bf16),
        VMEM((rows, width), bf16),
        VMEM((slots, width), bf16),
        VMEM((8, width), f32),
        VMEM((2 * rows // 128, 128, 128), f32),
        VMEM((2, slots, rows), bf16),
        VMEM((2, slots, rows), f32),
        VMEM((slots, width), f32),
        VMEM((4, slots, width), bf16),
        VMEM((4, slots, width), bf16),
        VMEM((4, slots, width), f32),
        VMEM((4 * slots, width), bf16),
        VMEM((4 * slots, width), f32),
        VMEM((4, slots, 8 * slots), f32),
        VMEM((8, 8 * slots), f32),
        VMEM((24, 128), f32),
        VMEM((24, 128), f32),
        VMEM((12, 24, 128), f32),
        VMEM((2 * rows, width), f32),
        VMEM((4, rows, 640), bf16),
        VMEM((width, width), bf16),
        VMEM((width, width), bf16),
        VMEM((width, width), bf16),
        VMEM((3, 4, depth, width), bf16),
        VMEM((3, 3, depth, width), bf16),
        VMEM((width, width), bf16),
        VMEM((width, width), bf16),
        VMEM((2, slots, width), bf16),
        VMEM((8, width), f32),
        VMEM((3, 24, 128), f32),
        VMEM((9, 24, 128), f32),
        VMEM((2 * rows, width), bf16),
        VMEM((depth, width), bf16),
        VMEM((16, 128), bf16),
        VMEM((slots, 256), bf16),
    ]
    for _ in range(4):
        scratch += gather_sems()
    scratch += [DMA((2,)), DMA((2,)), DMA((1,)), DMA((1,)), DMA((1,)), DMA((3, 2)), DMA((3, 2)), DMA((3, 2)), DMA((3, 2))]
    scratch += [DMA((6,)), DMA((4,)), DMA((2,)), DMA((3,)), DMA((3,)), DMA((3,)), DMA((1,)), DMA((10,)), DMA((10,))]
    scratch += [DMA((3, 4)), DMA((3, 3)), DMA((1,)), DMA((10,)), DMA((10,)), DMA((4,)), DMA((8,))]
    return pl.pallas_call(
        functools.partial(layer_kernel, slot_total),
        out_shape=[
            jax.ShapeDtypeStruct((1, 1), f32),
            jax.ShapeDtypeStruct((4 * rows, width), bf16),
            jax.ShapeDtypeStruct((4 * rows, width), bf16),
            jax.ShapeDtypeStruct((depth, width), f32),
            jax.ShapeDtypeStruct((depth, width), f32),
            jax.ShapeDtypeStruct((depth, width), f32),
            jax.ShapeDtypeStruct((4, width), f32),
        ],
        in_specs=[here] * 13 + [there, here],
        out_specs=[here, there, there, here, here, here, here],
        scratch_shapes=scratch,
        compiler_params=pltpu.CompilerParams(
            collective_id=1, has_side_effects=True, vmem_limit_bytes=63 * 2**20
        ),
        cost_estimate=pl.CostEstimate(flops=30 * 10**9, bytes_accessed=40 * 10**6, transcendentals=10**7),
        name="layer",
    )(w_qkv, w_out, up_own, down_own, *norms, valid, classes, *rest)


def finish_kernel(*refs):
    (block_in, token_in, attn_in, up_in, down_in) = refs[:5]
    (block_out, token_out, qkv_out, out_out, up_out, down_out) = refs[5:11]
    (narrow, wide, held, mats, qkv, out, sems) = refs[11:]
    parts, rows = narrow.shape[0], narrow.shape[1]
    count = iter(range(sems.shape[0]))

    def copy(src, dst):
        return pltpu.make_async_copy(src, dst, sems.at[next(count)])

    mat_loads = [copy(ref, mats.at[i]) for i, ref in enumerate((attn_in, up_in, down_in))]
    loads, saves, keep_loads, keep_saves = [], [], [], []
    for i in range(parts):
        span = pl.ds(i * rows, rows)
        loads.append(copy(token_in.at[span], narrow.at[i]))
        saves.append(copy(wide.at[i], token_out.at[span]))
        keep_loads.append(copy(block_in.at[span], held.at[i]))
        keep_saves.append(copy(held.at[i], block_out.at[span]))
    for load in mat_loads + loads + keep_loads:
        load.start()
    for load in mat_loads:
        load.wait()
    mat_saves = [copy(mats.at[1], up_out), copy(mats.at[2], down_out)]
    for save in mat_saves:
        save.start()
    for i, (pair, single) in enumerate(((0, 384), (128, 512), (256, 448))):
        qkv[i] = jnp.concatenate([mats[0, :, pair : pair + 128], mats[0, :, single : single + 64]], axis=1)
    depth = mats.shape[1]
    row = lax.broadcasted_iota(jnp.int32, (depth, depth), 0)
    eye = (row == lax.broadcasted_iota(jnp.int32, (depth, depth), 1)).astype(f32).astype(bf16)
    mixed = jnp.concatenate([mats[0, :, 640:768], mats[0, :, 576:640]], axis=1)
    out[...] = sum(tn(part, eye) for part in split_three(mixed))
    mat_saves += [copy(qkv, qkv_out), copy(out, out_out)]
    for save in mat_saves[2:]:
        save.start()
    for i in range(parts):
        loads[i].wait()
        wide[i] = narrow[i].astype(f32)
        saves[i].start()
    for load, save in zip(keep_loads, keep_saves):
        load.wait()
        save.start()
    for save in mat_saves + saves + keep_saves:
        save.wait()


def finish(block_out, token_grad, own_attn, own_up, own_down):
    rows, width = token_grad.shape
    depth = own_up.shape[0]
    parts = 4
    there = pl.BlockSpec(memory_space=pltpu.HBM)
    return pl.pallas_call(
        finish_kernel,
        out_shape=[
            jax.ShapeDtypeStruct(block_out.shape, bf16),
            jax.ShapeDtypeStruct((rows, width), f32),
            jax.ShapeDtypeStruct((3, depth, 192), f32),
            jax.ShapeDtypeStruct((192, depth), f32),
            jax.ShapeDtypeStruct((depth, width), f32),
            jax.ShapeDtypeStruct((depth, width), f32),
        ],
        in_specs=[there] * 5,
        out_specs=[there] * 6,
        scratch_shapes=[
            VMEM((parts, rows // parts, width), bf16),
            VMEM((parts, rows // parts, width), f32),
            VMEM((parts, rows // parts, width), bf16),
            VMEM((3, depth, width), f32),
            VMEM((3, depth, 192), f32),
            VMEM((192, depth), f32),
            DMA((7 + 4 * parts,)),
        ],
        compiler_params=pltpu.CompilerParams(vmem_limit_bytes=63 * 2**20),
        name="finish",
    )(block_out, token_grad, own_attn, own_up, own_down)


def on_kernel(
    tokens,
    segment_ids,
    slot_valid,
    ln1_gain,
    ln1_bias,
    w_qkv,
    w_out,
    ln2_gain,
    ln2_bias,
    w_up,
    w_down,
    class_tokens,
    image_gain,
    image_bias,
    image_proj,
):
    dp_rank = lax.axis_index("dp")
    depth, slots = w_up.shape[0], slot_valid.shape[0]
    loss, block_out, token_grad, own_attn, own_up, own_down, vectors = layer(
        slots * 32,
        w_qkv,
        w_out,
        w_up,
        w_down.T,
        [row.reshape(1, -1) for row in (ln1_gain, ln1_bias, ln2_gain, ln2_bias)],
        slot_valid.reshape(1, slots),
        class_tokens,
        image_gain,
        image_bias,
        image_proj,
        tokens,
        segment_ids.reshape(4, 4, 128),
    )
    block_out, token_grad, qkv_grad, out_grad, own_up, own_down = finish(
        block_out, token_grad, own_attn, own_up, own_down
    )
    vectors = lax.dynamic_slice_in_dim(vectors, dp_rank * depth, depth, 1)
    return (
        loss.reshape(()),
        block_out,
        token_grad,
        vectors[0],
        vectors[1],
        qkv_grad,
        out_grad,
        vectors[2],
        vectors[3],
        own_up,
        own_down.T,
    )


def make(dp_size, mp_size):
    def on_device(
        tokens,
        segment_ids,
        slot_valid,
        ln1_gain,
        ln1_bias,
        w_qkv,
        w_out,
        ln2_gain,
        ln2_bias,
        w_up,
        w_down,
        class_tokens,
        image_gain,
        image_bias,
        image_proj,
    ):
        both = ("dp", "mp")
        dp_rank, mp_rank = lax.axis_index("dp"), lax.axis_index("mp")
        depth = w_up.shape[0]
        width = depth * dp_size
        head_cols = w_out.shape[0]
        heads = head_cols // HEAD_DIM
        rows = tokens.shape[0] // mp_size
        seqs = rows // SEQ_LEN
        slots = slot_valid.shape[0]
        slot_total = slots * dp_size * mp_size

        packed = jnp.stack(
            [jnp.concatenate([w_qkv[0], w_qkv[1], w_qkv[2], w_out.T], axis=1), w_up, w_down.T]
        )
        norms = jnp.stack([ln1_gain, ln1_bias, ln2_gain, ln2_bias])
        image_hat, _ = standardise(class_tokens.astype(f32))
        image_normed = (image_hat * image_gain + image_bias).astype(bf16)
        image_raw = nn(image_normed, image_proj)
        image_unit = (image_raw * inverse_norm(image_raw)).astype(bf16)

        weights = lax.all_gather(packed, both, axis=0).reshape(dp_size, mp_size, 3, depth, -1)
        weights = weights.transpose(2, 1, 0, 3, 4).reshape(3, mp_size, width, -1)
        vectors = lax.all_gather(norms, "dp", axis=1, tiled=True).astype(f32)
        all_image = lax.all_gather(image_unit, both, axis=0, tiled=True)
        all_valid = lax.all_gather(slot_valid.astype(bf16), both, axis=0, tiled=True) > 0

        own = lax.dynamic_slice_in_dim(tokens, mp_rank * rows, rows, 0).astype(f32)
        ids = lax.dynamic_slice_in_dim(segment_ids, mp_rank * rows, rows, 0)
        grid_ids = ids.reshape(seqs, SEQ_LEN)
        first_len = jnp.sum((grid_ids == 0).astype(jnp.int32), axis=1)
        starts = jnp.arange(seqs, dtype=jnp.int32) * SEQ_LEN
        ends = jnp.stack([starts + first_len - 1, starts + SEQ_LEN - 1], axis=1).reshape(2 * seqs)
        place = (ends[:, None] == jnp.arange(rows)[None, :]).astype(bf16)

        hat_one, rstd_one = standardise(own)
        normed = (hat_one * vectors[0] + vectors[1]).astype(bf16)
        attn = weights[0]
        qkv = jnp.einsum("rd,mde->mre", normed, attn[:, :, : 3 * head_cols], preferred_element_type=f32)
        qkv = qkv.astype(bf16).reshape(mp_size, rows, 3, heads, HEAD_DIM)
        blocks = rows // tile_rows
        split = qkv.reshape(mp_size, blocks, tile_rows, 3, heads, HEAD_DIM)
        query, key, value = split[:, :, :, 0], split[:, :, :, 1], split[:, :, :, 2]
        tile_ids = ids.reshape(blocks, tile_rows)
        spots = jnp.arange(tile_rows)
        allowed = (
            (tile_ids[:, :, None] == tile_ids[:, None, :])
            & (spots[:, None] // SEQ_LEN == spots[None, :] // SEQ_LEN)[None]
            & (spots[:, None] >= spots[None, :])[None]
        )[None, :, None]
        scale = HEAD_DIM**-0.5
        scores = jnp.einsum("mbqhc,mbkhc->mbhqk", query, key, preferred_element_type=f32) * scale
        scores = jnp.where(allowed, scores, -1e30)
        probs = jax.nn.softmax(scores, axis=-1)
        mixed = jnp.einsum("mbhqk,mbkhc->mbqhc", probs.astype(bf16), value, preferred_element_type=f32)
        mixed = mixed.astype(bf16).reshape(mp_size, rows, head_cols)
        out_t = attn[:, :, 3 * head_cols :]
        attended = jnp.einsum("mre,mde->rd", mixed, out_t, preferred_element_type=f32)
        hidden = own + attended

        def feed(rows_in):
            hat, rstd = standardise(rows_in)
            normed_two = (hat * vectors[2] + vectors[3]).astype(bf16)
            upper = jnp.einsum("rd,mdf->mrf", normed_two, weights[1], preferred_element_type=f32)
            active = (upper * phi(upper)).astype(bf16)
            branch = jnp.einsum("mrf,mdf->rd", active, weights[2], preferred_element_type=f32)
            return hat, rstd, normed_two, upper, active, rows_in + branch

        block_out = feed(hidden)[-1].astype(bf16)
        hidden_ends = hidden[ends]
        hat_two, rstd_two, normed_two, upper, active, pooled = feed(hidden_ends)

        scale_back = inverse_norm(pooled)
        text = (pooled * scale_back).astype(bf16)
        logits = logit_scale * nt(text, all_image)
        live = slot_valid > 0
        weight = jnp.exp(logits)
        row_sum = jnp.sum(jnp.where(all_valid[None, :], weight, 0.0), axis=1)
        col_part = jnp.sum(jnp.where(live[:, None], weight, 0.0), axis=0)
        row_index = (dp_rank * mp_size + mp_rank) * slots + jnp.arange(slots)
        target = jnp.arange(slot_total)[None, :] == row_index[:, None]
        matched = jnp.sum(jnp.where(target, logits, 0.0), axis=1)
        row_part = jnp.sum(jnp.where(live, jnp.log(row_sum) - 2.0 * matched, 0.0))
        sums = lax.psum(jnp.concatenate([col_part, row_part[None]]), both)
        col_sum = sums[:slot_total]
        loss = 0.5 * (sums[slot_total] + jnp.sum(jnp.where(all_valid, jnp.log(col_sum), 0.0))) / slot_total
        pair = live[:, None] & all_valid[None, :]
        spread = 0.5 * weight * (1.0 / row_sum[:, None] + 1.0 / col_sum[None, :])
        grad_logits = jnp.where(pair, spread, 0.0) - (target & live[:, None]).astype(f32)
        cosine_grad = (logit_scale * grad_logits).astype(bf16)
        unit_grad = nn(cosine_grad, all_image)
        along = jnp.sum(unit_grad * pooled, axis=-1, keepdims=True)
        pooled_grad = scale_back * unit_grad - pooled * (scale_back * scale_back * scale_back * along)

        branch_grad = pooled_grad.astype(bf16)
        down_local = jnp.einsum("rd,mrf->mdf", branch_grad, active, preferred_element_type=f32)
        active_grad = jnp.einsum("rd,mdf->mrf", branch_grad, weights[2], preferred_element_type=f32)
        slope = phi(upper) + upper * jnp.exp(-0.5 * upper * upper) * (1.0 / (2.0 * jnp.pi) ** 0.5)
        upper_grad = (active_grad * slope).astype(bf16)
        up_local = jnp.einsum("rd,mrf->mdf", normed_two, upper_grad, preferred_element_type=f32)
        normed_two_grad = jnp.einsum("mrf,mdf->rd", upper_grad, weights[1], preferred_element_type=f32)
        gain_two = jnp.sum(normed_two_grad * hat_two, axis=0)
        bias_two = jnp.sum(normed_two_grad, axis=0)
        hidden_grad = pooled_grad + norm_pull(normed_two_grad, hat_two, rstd_two, vectors[2])

        attended_grad = hidden_grad.astype(bf16)
        mixed_ends = mixed[:, ends]
        out_local = jnp.einsum("rd,mre->mde", attended_grad, mixed_ends, preferred_element_type=f32)
        mixed_grad = jnp.einsum("rd,mde->mre", attended_grad, out_t, preferred_element_type=f32).astype(bf16)
        mixed_grad = mixed_grad.reshape(mp_size, 2 * seqs, heads, HEAD_DIM)
        query_ends, keys, values = qkv[:, ends, 0], qkv[:, :, 1], qkv[:, :, 2]
        spot = jnp.arange(rows)
        allowed_ends = (
            (ids[ends][:, None] == ids[None, :])
            & (ends[:, None] // SEQ_LEN == spot[None, :] // SEQ_LEN)
            & (ends[:, None] >= spot[None, :])
        )[None, None]
        again = jnp.einsum("mqhc,mkhc->mhqk", query_ends, keys, preferred_element_type=f32) * scale
        probs_ends = jax.nn.softmax(jnp.where(allowed_ends, again, -1e30), axis=-1)
        probs_grad = jnp.einsum("mqhc,mkhc->mhqk", mixed_grad, values, preferred_element_type=f32)
        value_grad = jnp.einsum("mhqk,mqhc->mkhc", probs_ends.astype(bf16), mixed_grad, preferred_element_type=f32)
        centre = jnp.sum(probs_grad * probs_ends, axis=-1, keepdims=True)
        score_grad = (probs_ends * (probs_grad - centre)).astype(bf16)
        query_grad = jnp.einsum("mhqk,mkhc->mqhc", score_grad, keys, preferred_element_type=f32) * scale
        key_grad = jnp.einsum("mhqk,mqhc->mkhc", score_grad, query_ends, preferred_element_type=f32) * scale
        query_grad = query_grad.astype(bf16).reshape(mp_size, 2 * seqs, head_cols)
        query_grad = jnp.einsum("er,mec->mrc", place, query_grad, preferred_element_type=f32).astype(bf16)
        proj_grad = jnp.concatenate(
            [
                query_grad,
                key_grad.astype(bf16).reshape(mp_size, rows, head_cols),
                value_grad.astype(bf16).reshape(mp_size, rows, head_cols),
            ],
            axis=-1,
        )
        qkv_local = jnp.einsum("rd,mre->mde", normed, proj_grad, preferred_element_type=f32)
        normed_grad = jnp.einsum("mre,mde->rd", proj_grad, attn[:, :, : 3 * head_cols], preferred_element_type=f32)
        gain_one = jnp.sum(normed_grad * hat_one, axis=0)
        bias_one = jnp.sum(normed_grad, axis=0)
        token_grad = norm_pull(normed_grad, hat_one, rstd_one, vectors[0])
        token_grad = token_grad.at[ends].add(hidden_grad)

        local = jnp.stack([jnp.concatenate([qkv_local, out_local], axis=-1), up_local, down_local])
        local = local.reshape(3, mp_size, dp_size, depth, -1).transpose(2, 1, 0, 3, 4)
        local = local.reshape(dp_size * mp_size, 3, depth, -1)
        summed = lax.psum_scatter(local, both, scatter_dimension=0, tiled=False)
        vector_local = lax.psum(jnp.stack([gain_one, bias_one, gain_two, bias_two]), both)
        vector_own = lax.dynamic_slice_in_dim(vector_local, dp_rank * depth, depth, 1)

        block_out = lax.all_gather(block_out, "mp", axis=0, tiled=True)
        token_grad = lax.all_gather(token_grad, "mp", axis=0, tiled=True)
        qkv_grad = summed[0, :, : 3 * head_cols].reshape(depth, 3, head_cols).transpose(1, 0, 2)
        return (
            loss,
            block_out,
            token_grad,
            vector_own[0],
            vector_own[1],
            qkv_grad,
            summed[0, :, 3 * head_cols :].T,
            vector_own[2],
            vector_own[3],
            summed[1],
            summed[2].T,
        )

    return on_device


def solution(mesh):
    placed = (
        P("dp", None),
        P("dp"),
        P(("dp", "mp")),
        P("dp"),
        P("dp"),
        P(None, "dp", "mp"),
        P("mp", "dp"),
        P("dp"),
        P("dp"),
        P("dp", "mp"),
        P("mp", "dp"),
        P(("dp", "mp"), None),
        P(),
        P(),
        P(),
    )
    sizes = (mesh.shape["dp"], mesh.shape["mp"])
    return jax.shard_map(
        on_kernel if sizes == (8, 4) else make(*sizes),
        mesh=mesh,
        in_specs=placed,
        out_specs=(
            P(),
            P("dp", None),
            P("dp", None),
            P("dp"),
            P("dp"),
            P(None, "dp", "mp"),
            P("mp", "dp"),
            P("dp"),
            P("dp"),
            P("dp", "mp"),
            P("mp", "dp"),
        ),
        check_vma=False,
    )
```
